32 devices in a mesh: dp: 16 (over z, y, x), space: 2 (over core).
Axes of the slice: x: 2, y: 2, z: 4, core: 2. Of those that a mesh axis runs over, the one named last changes fastest.
Arguments:
- tokens: bfloat16 [64, 256, 1024], P('dp', 'space'), may hold values from -6 to 6
- cotangent: bfloat16 [64, 256, 1024], P('dp', 'space'), may hold values from -6 to 6
- labels: int32 [64], P(('dp', 'space')), may hold values from 0 to 999
- sigma_index: int32 [64], P(('dp', 'space')), may hold values from 0 to 63
- fourier: float32 [128], replicated, may hold values from -4 to 4
- class_table: bfloat16 [1000, 768], replicated, may hold values from -6 to 6
- w_time: bfloat16 [256, 768], replicated, may hold values from -0.375 to 0.375
- w_map_up: bfloat16 [768, 4608], replicated, may hold values from -0.21875 to 0.21875
- w_map_down: bfloat16 [2304, 768], replicated, may hold values from -0.125 to 0.125
- map_gains: bfloat16 [3, 768], replicated, may hold values from 0.099609375 to 1.8984375
- w_ada_attn: bfloat16 [768, 1024], replicated, may hold values from -0.109375 to 0.109375
- w_ada_ffn: bfloat16 [768, 1024], replicated, may hold values from -0.109375 to 0.109375
- w_qkv: bfloat16 [1024, 3072], replicated, may hold values from -0.1875 to 0.1875
- head_scale: bfloat16 [16], replicated, may hold values from 8 to 16
- w_out: bfloat16 [1024, 1024], replicated, may hold values from -1 to 1
- w_up: bfloat16 [1024, 6144], replicated, may hold values from -0.1875 to 0.1875
- w_down: bfloat16 [3072, 1024], replicated, may hold values from -0.109375 to 0.109375
Outputs:
- out_tokens: bfloat16 [64, 256, 1024], P('dp', 'space')
- grad_tokens: float32 [64, 256, 1024], P('dp', 'space')
- grad_class_table: float32 [1000, 768], P(None, ('dp', 'space'))
- grad_w_time: float32 [256, 768], P(None, ('dp', 'space'))
- grad_map_up: float32 [768, 4608], P(None, ('dp', 'space'))
- grad_map_down: float32 [2304, 768], P(None, ('dp', 'space'))
- grad_map_gains: float32 [3, 768], P(None, ('dp', 'space'))
- grad_ada_attn: float32 [768, 1024], P(None, ('dp', 'space'))
- grad_ada_ffn: float32 [768, 1024], P(None, ('dp', 'space'))
- grad_qkv: float32 [1024, 3072], P(None, ('dp', 'space'))
- grad_head_scale: float32 [16], replicated
- grad_out: float32 [1024, 1024], P(None, ('dp', 'space'))
- grad_up: float32 [1024, 6144], P(None, ('dp', 'space'))
- grad_down: float32 [3072, 1024], P(None, ('dp', 'space'))
The draws below stay inside these ranges and needn't reach their ends.
All inputs are finite; a program needn't handle non-finite values.
Results may differ from the reference program's by a relative error of at most 0.024.
Values may be sent and summed in bfloat16 or wider, within the bound.
No kernel may reach another device: no remote copies, remote signals or barrier semaphores. Data moves between devices by JAX's collectives and lax.ppermute only.
A program may use at most 320 MiB of HBM per device.

```python
import math
import jax
import jax.numpy as jnp
from jax import lax

D = 1024
H = 16
FF = 3072
C = 768
MFF = 2304
NCLASS = 1000
NFOUR = 128
NSIG = 64
GRID = 16
SEQ = 256
IMAGES = 64


def place_ends(entries, own_key, low, largest):
    shape = entries.shape
    spot = [jax.random.randint(jax.random.fold_in(own_key, axis), (), 0, shape[axis]) for axis in range(len(shape))]
    entries = entries.at[tuple(spot)].set(low)
    longest = shape.index(max(shape))
    spot[longest] = (spot[longest] + 1) % shape[longest]
    return entries.at[tuple(spot)].set(largest)


def with_spikes(entries, own_key, source, target, parts, factor):
    owner, partner = [(jnp.arange(entries.shape[position]) // (entries.shape[position] // parts)).reshape([-1 if axis == position else 1 for axis in range(entries.ndim)]) for position in (source, target)]
    chosen = jax.random.permutation(own_key, parts)[partner]
    strong = (owner == chosen) | (owner == (partner + parts // 2) % parts)
    return jnp.where(strong, factor * entries, entries)


def steps_of(rng, shape, split, low, largest):
    level, own = 1.0, jax.random.fold_in(rng, 6)
    for dim, parts in split:
        draws = jnp.exp(jax.random.uniform(jax.random.fold_in(own, dim), (parts,), jnp.float32, low / len(split), largest / len(split)))
        level = level * jnp.repeat(draws, shape[dim] // parts).reshape([-1 if axis == dim else 1 for axis in range(len(shape))])
    return level


def centred(key, extent, spread, most, split=(), dtype=jnp.bfloat16):
    factor_of = steps_of(key, extent, split, -0.22, 0.18) if split else 1.0
    drawn = jax.random.normal(key, extent, jnp.float32) * spread * factor_of
    return jnp.minimum(jnp.maximum(drawn, -most), most).astype(dtype)


def noise_with(rng, extent, width, reach, cuts, heavy, kind=jnp.bfloat16):
    values = width * jax.random.normal(rng, extent, jnp.float32)
    if cuts:
        values = values * steps_of(rng, extent, cuts, -0.22, 0.18)
    return jnp.clip(with_spikes(values, jax.random.fold_in(rng, 3), *heavy), -reach, reach).astype(kind)


def setup_inputs(seed: int = 0) -> dict:
    seeds = jax.random.split(jax.random.key(seed), 18)
    tokens = centred(seeds[0], (IMAGES, SEQ, D), 1.0, 6.0, ((0, 16), (1, 2)))
    cotangent = noise_with(seeds[1], (IMAGES, SEQ, D), 1.0, 6.0, ((0, 16), (1, 2)), (0, 2, 16, 2.0))
    labels = place_ends(jax.random.randint(seeds[2], (IMAGES,), 0, NCLASS), jax.random.fold_in(seeds[2], 1), 0, NCLASS - 1).astype(jnp.int32)
    sigma_index = place_ends(jax.random.randint(seeds[3], (IMAGES,), 0, NSIG), jax.random.fold_in(seeds[3], 1), 0, NSIG - 1).astype(jnp.int32)
    fourier = centred(seeds[4], (NFOUR,), 1.0, 4.0, (), jnp.float32)
    class_table = centred(seeds[5], (NCLASS, C), 1.0, 6.0)
    w_time = centred(seeds[6], (2 * NFOUR, C), (2 * NFOUR) ** -0.5, 0.375)
    w_map_up = centred(seeds[7], (C, 2 * MFF), C ** -0.5, 0.21875)
    w_map_down = centred(seeds[8], (MFF, C), MFF ** -0.5, 0.125)
    map_gains = jnp.clip(1.0 + 0.18 * jax.random.normal(seeds[9], (3, C), jnp.float32), 0.099609375, 1.8984375).astype(jnp.bfloat16)
    w_ada_attn = centred(seeds[10], (C, D), (4 * C) ** -0.5, 0.109375)
    w_ada_ffn = centred(seeds[11], (C, D), (4 * C) ** -0.5, 0.109375)
    w_qkv = centred(seeds[12], (D, 3 * D), D ** -0.5, 0.1875)
    head_scale = jnp.clip(jax.random.uniform(seeds[13], (H,), jnp.float32, 8.0, 16.0), 8.0, 16.0).astype(jnp.bfloat16)
    w_out = centred(seeds[14], (D, D), (D // 32) ** -0.5, 1.0)
    w_up = centred(seeds[15], (D, 2 * FF), D ** -0.5, 0.1875)
    w_down = centred(seeds[16], (FF, D), FF ** -0.5, 0.109375)
    return {"tokens": tokens, "cotangent": cotangent, "labels": labels, "sigma_index": sigma_index, "fourier": fourier, "class_table": class_table, "w_time": w_time, "w_map_up": w_map_up, "w_map_down": w_map_down, "map_gains": map_gains, "w_ada_attn": w_ada_attn, "w_ada_ffn": w_ada_ffn, "w_qkv": w_qkv, "head_scale": head_scale, "w_out": w_out, "w_up": w_up, "w_down": w_down}


@jax.custom_vjp
def low(v):
    return lax.optimization_barrier(v.astype(jnp.bfloat16)).astype(jnp.float32)

@jax.custom_vjp
def low_back(v):
    return v

def low_keep(v):
    return (low(v), None)

def low_pass(kept, grad):
    return (grad,)

def back_keep(v):
    return (v, None)

def back_low(kept, grad):
    return (low(grad),)
low.defvjp(low_keep, low_pass)
low_back.defvjp(back_keep, back_low)
EPSILON = 1e-06
PRECISE = lax.Precision.HIGHEST
LOG_LOW = math.log(0.01)
LOG_SPAN = math.log(10000.0)

def rms_norm(vector, scaling):
    return vector * lax.rsqrt(lax.optimization_barrier(jnp.mean(vector * vector, axis=-1, keepdims=True)) + EPSILON) * scaling

def geglu(projected):
    half_width = projected.shape[-1] // 2
    return projected[..., :half_width] * jax.nn.gelu(projected[..., half_width:], approximate=False)

def rope_table(first_token, token_count, num_heads, head_dim, grid_side):
    quarter = head_dim // 8
    order_index = jnp.arange(quarter)[None, :] * num_heads + jnp.arange(num_heads)[:, None]
    frequency = jnp.exp(math.log(math.pi) + math.log(10.0) * order_index.astype(jnp.float32) / (num_heads * quarter))
    places = first_token + jnp.arange(token_count)
    row_pos = -1.0 + (2.0 * (places // grid_side).astype(jnp.float32) + 1.0) / grid_side
    col_pos = -1.0 + (2.0 * (places % grid_side).astype(jnp.float32) + 1.0) / grid_side
    angles = jnp.concatenate([row_pos[:, None, None] * frequency[None], col_pos[:, None, None] * frequency[None]], axis=-1)
    return (jnp.cos(angles), jnp.sin(angles))

def cosine_rope(head_vectors, scaling, cos_table, sin_table):
    squares = lax.optimization_barrier(jnp.sum(head_vectors * head_vectors, axis=-1, keepdims=True))
    normed = head_vectors * (jnp.sqrt(scaling)[:, None] * lax.rsqrt(squares + EPSILON))
    quarter = head_vectors.shape[-1] // 4
    first_part = normed[..., :quarter]
    second_part = normed[..., quarter:2 * quarter]
    return jnp.concatenate([first_part * cos_table - second_part * sin_table, second_part * cos_table + first_part * sin_table, normed[..., 2 * quarter:]], axis=-1)

def fourier_features(sigma_index, fourier):
    noise_level = (LOG_LOW + LOG_SPAN * sigma_index.astype(jnp.float32) / (NSIG - 1)) / 4.0
    angles = 2.0 * math.pi * noise_level[:, None] * fourier[None, :]
    return jnp.concatenate([jnp.cos(angles), jnp.sin(angles)], axis=-1)

def mapping_net(labels, sigma_index, fourier, class_table, w_time, w_map_up, w_map_down, map_gains, w_ada_attn, w_ada_ffn):
    feats = low(fourier_features(sigma_index, fourier))
    start_cond = jnp.dot(feats, w_time, precision=PRECISE) + jnp.take(class_table, labels, axis=0)
    first_cond = rms_norm(start_cond, map_gains[0])
    map_hidden = low(rms_norm(first_cond, map_gains[1]))
    map_gated = low(geglu(jnp.dot(map_hidden, w_map_up, precision=PRECISE)))
    second_cond = first_cond + jnp.dot(map_gated, w_map_down, precision=PRECISE)
    cond = low(rms_norm(second_cond, map_gains[2]))
    return (jnp.dot(cond, w_ada_attn, precision=PRECISE), jnp.dot(cond, w_ada_ffn, precision=PRECISE))

def layer_forward(tokens, mod_attn, mod_ffn, w_qkv, head_scale, w_out, w_up, w_down, cos_table, sin_table):
    num_images, seq_len, model_width = tokens.shape
    num_heads = head_scale.shape[0]
    head_dim = model_width // num_heads
    normed = low(rms_norm(tokens, 1.0 + mod_attn[:, None, :]))
    qkv = low_back(jnp.einsum('btd,de->bte', normed, w_qkv, precision=PRECISE))
    qkv_heads = qkv.reshape(num_images, seq_len, 3, num_heads, head_dim)
    queries = low(cosine_rope(qkv_heads[:, :, 0], head_scale, cos_table, sin_table))
    key_heads = low(cosine_rope(qkv_heads[:, :, 1], head_scale, cos_table, sin_table))
    value_heads = low(qkv_heads[:, :, 2])
    scores = low_back(jnp.einsum('bqhd,bkhd->bhqk', queries, key_heads, precision=PRECISE))
    attn_probs = low(jax.nn.softmax(scores, axis=-1))
    attended = low_back(jnp.einsum('bhqk,bkhd->bqhd', attn_probs, value_heads, precision=PRECISE))
    attended = low(attended.reshape(num_images, seq_len, model_width))
    mixed_tokens = tokens + low_back(jnp.einsum('btd,de->bte', attended, w_out, precision=PRECISE))
    normed_ffn = low(rms_norm(mixed_tokens, 1.0 + mod_ffn[:, None, :]))
    up_proj = low_back(jnp.einsum('btd,de->bte', normed_ffn, w_up, precision=PRECISE))
    gated = low(geglu(up_proj))
    return mixed_tokens + low_back(jnp.einsum('btf,fd->btd', gated, w_down, precision=PRECISE))

def reference(tokens, cotangent, labels, sigma_index, fourier, class_table, w_time, w_map_up, w_map_down, map_gains, w_ada_attn, w_ada_ffn, w_qkv, head_scale, w_out, w_up, w_down):
    params = tuple((item.astype(jnp.float32) for item in (class_table, w_time, w_map_up, w_map_down, map_gains, w_ada_attn, w_ada_ffn, w_qkv, head_scale, w_out, w_up, w_down)))
    fourier_f = fourier.astype(jnp.float32)
    num_heads = head_scale.shape[0]
    cos_table, sin_table = rope_table(0, SEQ, num_heads, D // num_heads, GRID)
    group_size = math.gcd(IMAGES, 16)
    num_groups = IMAGES // group_size

    def group_step(running, pieces):
        group_tokens, group_cot, group_labels, group_sigma = pieces

        def forward(tok_in, param_list):
            mod_attn, mod_ffn = mapping_net(group_labels, group_sigma, fourier_f, param_list[0], param_list[1], param_list[2], param_list[3], param_list[4], param_list[5], param_list[6])
            return layer_forward(tok_in, mod_attn, mod_ffn, param_list[7], param_list[8], param_list[9], param_list[10], param_list[11], cos_table, sin_table)
        result, pull_back = jax.vjp(forward, group_tokens.astype(jnp.float32), params)
        grad_in, grad_params = pull_back(group_cot.astype(jnp.float32))
        running = jax.tree.map(jnp.add, running, grad_params)
        return (running, (result.astype(jnp.bfloat16), grad_in))
    initial = jax.tree.map(jnp.zeros_like, params)
    stacked = (tokens.reshape(num_groups, group_size, SEQ, D), cotangent.reshape(num_groups, group_size, SEQ, D), labels.reshape(num_groups, group_size), sigma_index.reshape(num_groups, group_size))
    totals, (outputs, grads_in) = lax.scan(group_step, initial, stacked)
    return (outputs.reshape(IMAGES, SEQ, D), grads_in.reshape(IMAGES, SEQ, D), totals[0], totals[1], totals[2], totals[3], totals[4], totals[5], totals[6], totals[7], totals[8], totals[9], totals[10], totals[11])
```

```python
import functools
import math

import jax
import jax.numpy as jnp
import numpy as np
from jax import lax
from jax.experimental import pallas as pl
from jax.experimental.pallas import tpu as pltpu
from jax.sharding import PartitionSpec as P

NSIG = 64
GRID = 16


EPSILON = 1e-06
BOTH = ("dp", "space")
LOG_LOW = math.log(0.01)
LOG_SPAN = math.log(10000.0)


def rope_tables(tokens, heads, head_dim, side):
    quarter = head_dim // 8
    order = np.arange(quarter)[None, :] * heads + np.arange(heads)[:, None]
    frequency = np.exp(math.log(math.pi) + math.log(10.0) * order / (heads * quarter))
    places = np.arange(tokens)
    row = -1.0 + (2.0 * (places // side) + 1.0) / side
    col = -1.0 + (2.0 * (places % side) + 1.0) / side
    angles = np.concatenate(
        [row[:, None, None] * frequency[None], col[:, None, None] * frequency[None]], axis=-1
    )
    cos, sin, flat = np.cos(angles), np.sin(angles), np.zeros_like(angles)
    tables = [
        np.concatenate([cos, cos, flat + 1.0, flat + 1.0], axis=-1),
        np.concatenate([-sin, sin, flat, flat], axis=-1),
    ]
    return [table.reshape(tokens, heads * head_dim).astype(np.float32) for table in tables]


VMEM_LIMIT = 60 * 1024 * 1024
NN = (((1,), (0,)), ((), ()))
NT = (((1,), (1,)), ((), ()))
TN = (((0,), (0,)), ((), ()))


def mm(left, right, dims=NN):
    return lax.dot_general(left, right, dims, preferred_element_type=jnp.float32)


def held(value, after):
    return lax.optimization_barrier((value, *after))[0] if after else value


def call(body, grid, ins, outs, scratch=(), flops=0, moved=0, after=()):
    arrays = [array for array, _, _ in ins]
    least = min(range(len(arrays)), key=lambda k: arrays[k].size)
    arrays[least] = held(arrays[least], after)
    return pl.pallas_call(
        body,
        grid=grid,
        name=getattr(body, "__name__", "ffn_kernel"),
        in_specs=[
            pl.BlockSpec(memory_space=pltpu.SMEM) if block is None else pl.BlockSpec(block, where)
            for _, block, where in ins
        ],
        out_specs=[pl.BlockSpec(block, where) for _, block, where in outs],
        out_shape=[shape for shape, _, _ in outs],
        scratch_shapes=list(scratch),
        compiler_params=pltpu.CompilerParams(
            dimension_semantics=("arbitrary",) * len(grid), vmem_limit_bytes=VMEM_LIMIT
        ),
        cost_estimate=pl.CostEstimate(flops=flops, bytes_accessed=moved, transcendentals=0),
    )(*arrays)


def head_sums(values):
    lanes = values.shape[1]
    row = lax.broadcasted_iota(jnp.int32, (lanes, lanes), 0) // (lanes // 2)
    col = lax.broadcasted_iota(jnp.int32, (lanes, lanes), 1) // (lanes // 2)
    ones = jnp.where(row == col, 1.0, 0.0).astype(jnp.bfloat16)
    high = values.astype(jnp.bfloat16)
    rest = (values - high.astype(jnp.float32)).astype(jnp.bfloat16)
    return mm(high, ones) + mm(rest, ones)


def rotate(values, cos, sin):
    lanes = values.shape[1]
    lane = lax.broadcasted_iota(jnp.int32, values.shape, 1)
    first = lane % (lanes // 2) < lanes // 8
    near = jnp.where(first, pltpu.roll(values, lanes - lanes // 8, 1), pltpu.roll(values, lanes // 8, 1))
    return values * cos + near * sin


def qkv_kernel(tok_ref, scale_ref, w_ref, cos_ref, sin_ref, root_ref, normed_ref, qkv_ref, unit_ref):
    step = pl.program_id(0)
    count, seq = scale_ref.shape[0], cos_ref.shape[0]

    @pl.when(step == 0)
    def _():
        for image in range(count):
            rows = pl.ds(image * seq, seq)
            tok = tok_ref[rows, :].astype(jnp.float32)
            inverse = lax.rsqrt(jnp.mean(tok * tok, axis=-1, keepdims=True) + EPSILON)
            normed_ref[rows, :] = (tok * inverse * scale_ref[image]).astype(jnp.bfloat16)

    rotated = step < 2 * pl.num_programs(0) // 3

    @pl.when(rotated)
    def _():
        for image in range(count):
            rows = pl.ds(image * seq, seq)
            for lane in range(0, w_ref.shape[1], 256):
                wide = mm(normed_ref[rows, :], w_ref[:, lane : lane + 256])
                for part in range(0, 256, 128):
                    at = slice(lane + part, lane + part + 128)
                    heads = wide[:, part : part + 128]
                    unit = root_ref[:, at] * lax.rsqrt(head_sums(heads * heads) + EPSILON)
                    unit_ref[rows, at] = unit
                    turned = rotate(heads * unit, cos_ref[:, at], sin_ref[:, at])
                    qkv_ref[rows, at] = turned.astype(jnp.bfloat16)

    @pl.when(jnp.logical_not(rotated))
    def _():
        qkv_ref[...] = mm(normed_ref[...], w_ref[...]).astype(jnp.bfloat16)


def project_qkv(tokens, scale_attn, w_qkv, cos, sin, root, after=()):
    rows, width = tokens.shape
    total, block = w_qkv.shape[1], 512
    steps = total // block
    turned = steps * 2 // 3
    per = width // block
    return call(
        qkv_kernel,
        (steps,),
        [
            (tokens, (rows, width), lambda j: (0, 0)),
            (scale_attn, scale_attn.shape, lambda j: (0, 0, 0)),
            (w_qkv, (width, block), lambda j: (0, j)),
            (cos, (cos.shape[0], block), lambda j: (0, j % per)),
            (sin, (sin.shape[0], block), lambda j: (0, j % per)),
            (root, (1, block), lambda j: (0, j % per)),
        ],
        [
            (jax.ShapeDtypeStruct((rows, width), jnp.bfloat16), (rows, width), lambda j: (0, 0)),
            (jax.ShapeDtypeStruct((rows, total), jnp.bfloat16), (rows, block), lambda j: (0, j)),
            (
                jax.ShapeDtypeStruct((rows, 2 * width), jnp.float32),
                (rows, block),
                lambda j: (0, jnp.minimum(j, turned - 1)),
            ),
        ],
        flops=2 * rows * width * total,
        moved=2 * width * total + 14 * rows * width,
        after=after,
    )


def attention_kernel(q_ref, k_ref, v_ref, tok_ref, scale_ref, w_ref, att_ref, inv_ref, mixed_ref, nf_ref):
    seq, width = q_ref.shape
    left = lax.broadcasted_iota(jnp.int32, (seq, 128), 1) < 64
    for pair in range(width // 128):
        at = slice(pair * 128, pair * 128 + 128)
        queries, keys, values = q_ref[:, at], k_ref[:, at], v_ref[:, at]
        none, one = jnp.zeros_like(queries), jnp.ones_like(queries)
        weights0 = jnp.exp(mm(jnp.where(left, queries, none), keys, NT)).astype(jnp.bfloat16)
        weights1 = jnp.exp(mm(jnp.where(left, none, queries), keys, NT)).astype(jnp.bfloat16)
        both0 = mm(weights0, jnp.where(left, values, one))
        both1 = mm(weights1, jnp.where(left, one, values))
        totals = pltpu.roll(jnp.where(left, both1, both0), 64, 1)
        inverse = 1.0 / totals
        inv_ref[:, at] = inverse
        att_ref[:, at] = (jnp.where(left, both0, both1) * inverse).astype(jnp.bfloat16)
    mixed = tok_ref[...].astype(jnp.float32) + mm(att_ref[...], w_ref[...])
    mixed_ref[...] = mixed
    inverse = lax.rsqrt(jnp.mean(mixed * mixed, axis=-1, keepdims=True) + EPSILON)
    nf_ref[...] = (mixed * inverse * scale_ref[0]).astype(jnp.bfloat16)


def attend(qkv, tokens, scale_ffn, w_out, after=()):
    rows, width = tokens.shape
    images = scale_ffn.shape[0]
    seq = rows // images

    def part(index):
        return (qkv, (seq, width), lambda i: (i, index))

    def result(dtype):
        return (jax.ShapeDtypeStruct((rows, width), dtype), (seq, width), lambda i: (i, 0))

    return call(
        attention_kernel,
        (images,),
        [
            part(0),
            part(1),
            part(2),
            (tokens, (seq, width), lambda i: (i, 0)),
            (scale_ffn, (1, 1, width), lambda i: (i, 0, 0)),
            (w_out, w_out.shape, lambda i: (0, 0)),
        ],
        [result(jnp.bfloat16), result(jnp.float32), result(jnp.float32), result(jnp.bfloat16)],
        flops=2 * rows * width * width + 4 * rows * seq * width,
        moved=2 * width * width + 20 * rows * width,
        after=after,
    )


def ffn_kernel(first, nf_ref, cot_ref, cot_t_ref, wa_ref, wb_ref, wd_ref, y_in, g_in, gu_t, gd_t, y_ref, g_ref):
    @pl.when(pl.program_id(0) == 0)
    def _():
        y_ref[...] = y_in[...]
        if first:
            g_ref[...] = jnp.zeros_like(g_ref)
        else:
            g_ref[...] = g_in[...]

    rows = nf_ref.shape[0]
    parts = 2
    size = rows // parts
    low_a, low_b, low_g = [], [], []
    for part in range(parts):
        at = pl.ds(part * size, size)
        nf = nf_ref[at, :]
        value = mm(nf, wa_ref[...])
        gate = mm(nf, wb_ref[...])
        grad = mm(cot_ref[at, :], wd_ref[...], NT)
        normal = 0.5 + 0.5 * lax.erf(gate * math.sqrt(0.5))
        bent = gate * normal
        slope = normal + gate * (jnp.exp(-0.5 * gate * gate) * (1.0 / math.sqrt(2.0 * math.pi)))
        gated = (value * bent).astype(jnp.bfloat16)
        ga = (grad * bent).astype(jnp.bfloat16)
        gb = (grad * value * slope).astype(jnp.bfloat16)
        y_ref[at, :] += mm(gated, wd_ref[...])
        g_ref[at, :] += mm(ga, wa_ref[...], NT) + mm(gb, wb_ref[...], NT)
        low_a.append(ga)
        low_b.append(gb)
        low_g.append(gated)
    ga, gb, gated = [jnp.concatenate(v, axis=0) for v in (low_a, low_b, low_g)]
    gu_t[0] = mm(ga, nf_ref[...], TN).astype(jnp.bfloat16)
    gu_t[1] = mm(gb, nf_ref[...], TN).astype(jnp.bfloat16)
    gd_t[...] = mm(cot_t_ref[...], gated).astype(jnp.bfloat16)


def ffn(piece, pieces, nf, cot, cot_t, w_up, w_down, y_in, g_in, after=()):
    rows, width = nf.shape
    hidden = w_down.shape[0]
    block = 384
    steps = hidden // pieces // block
    base, gate = piece * steps, hidden // block

    def whole(array):
        return (array, array.shape, lambda j: (0, 0))

    first = g_in is None
    return call(
        functools.partial(ffn_kernel, first),
        (steps,),
        [
            whole(nf),
            whole(cot),
            whole(cot_t),
            (w_up, (width, block), lambda j: (0, base + j)),
            (w_up, (width, block), lambda j: (0, gate + base + j)),
            (w_down, (block, width), lambda j: (base + j, 0)),
            whole(y_in),
            (g_in if g_in is not None else jnp.zeros((8, 128), jnp.float32), (8, 128) if first else g_in.shape, lambda j: (0, 0)),
        ],
        [
            (
                jax.ShapeDtypeStruct((2, steps * block, width), jnp.bfloat16),
                (2, block, width),
                lambda j: (0, j, 0),
            ),
            (
                jax.ShapeDtypeStruct((width, steps * block), jnp.bfloat16),
                (width, block),
                lambda j: (0, j),
            ),
            (jax.ShapeDtypeStruct((rows, width), jnp.float32), (rows, width), lambda j: (0, 0)),
            (jax.ShapeDtypeStruct((rows, width), jnp.float32), (rows, width), lambda j: (0, 0)),
        ],
        flops=18 * rows * width * steps * block,
        moved=12 * width * steps * block + 20 * rows * width,
        after=after,
    )


def mixed_kernel(cot_ref, mixed_ref, gnf_ref, scale_ref, w_ref, gm_ref, low_ref, gatt_ref, gmod_ref):
    mixed, scale = mixed_ref[...], scale_ref[0]
    inverse = lax.rsqrt(jnp.mean(mixed * mixed, axis=-1, keepdims=True) + EPSILON)
    grad = gnf_ref[...]
    unit = mixed * inverse
    gmod_ref[0] = jnp.sum(grad * unit, axis=0, keepdims=True)
    scaled = grad * scale
    mean = jnp.mean(scaled * unit, axis=-1, keepdims=True)
    total = cot_ref[...].astype(jnp.float32) + inverse * (scaled - unit * mean)
    gm_ref[...] = total
    low = total.astype(jnp.bfloat16)
    low_ref[...] = low
    gatt_ref[...] = mm(low, w_ref[...], NT).astype(jnp.bfloat16)


def mixed_backward(cot, mixed, grad_nf, scale_ffn, w_out, after=()):
    rows, width = mixed.shape
    images = scale_ffn.shape[0]
    seq = rows // images

    def own(array):
        return (array, (seq, width), lambda i: (i, 0))

    def result(dtype):
        return (jax.ShapeDtypeStruct((rows, width), dtype), (seq, width), lambda i: (i, 0))

    return call(
        mixed_kernel,
        (images,),
        [
            own(cot),
            own(mixed),
            own(grad_nf),
            (scale_ffn, (1, 1, width), lambda i: (i, 0, 0)),
            (w_out, w_out.shape, lambda i: (0, 0)),
        ],
        [
            result(jnp.float32),
            result(jnp.bfloat16),
            result(jnp.bfloat16),
            (jax.ShapeDtypeStruct((images, 1, width), jnp.float32), (1, 1, width), lambda i: (i, 0, 0)),
        ],
        flops=2 * rows * width * width,
        moved=2 * width * width + 18 * rows * width,
        after=after,
    )


def attention_back_kernel(
    q_ref, k_ref, v_ref, att_ref, inv_ref, gatt_ref, uq_ref, uk_ref, cos_ref, sin_ref, root_ref, g_ref, gs_ref
):
    seq, width = q_ref.shape
    lane = lax.broadcasted_iota(jnp.int32, (seq, 128), 1)
    left = lane < 64

    @pl.when(pl.program_id(0) == 0)
    def _():
        gs_ref[...] = jnp.zeros_like(gs_ref)

    def own(mask, values):
        return jnp.where(mask, values, jnp.zeros_like(values))

    for pair in range(width // 128):
        at = slice(pair * 128, pair * 128 + 128)
        queries, keys, values = q_ref[:, at], k_ref[:, at], v_ref[:, at]
        grad = gatt_ref[:, at].astype(jnp.float32) * inv_ref[:, at]
        low = grad.astype(jnp.bfloat16)
        along = grad * att_ref[:, at].astype(jnp.float32)
        grads = [None, None, None]
        for head in range(2):
            mask = left if head == 0 else jnp.logical_not(left)
            delta = -jnp.sum(own(mask, along), axis=-1, keepdims=True)
            high = delta.astype(jnp.bfloat16).astype(jnp.float32)
            spot = 64 if head == 0 else 0
            extra = jnp.where(lane == spot, high, jnp.where(lane == spot + 1, delta - high, 0.0))
            ones = jnp.where((lane == spot) | (lane == spot + 1), 1.0, 0.0).astype(jnp.bfloat16)
            shifted = jnp.where(mask, low, extra.astype(jnp.bfloat16))
            weights = jnp.exp(mm(keys, own(mask, queries), NT))
            grad_scores = (weights * mm(jnp.where(mask, values, ones), shifted, NT)).astype(jnp.bfloat16)
            found = (
                mm(grad_scores, own(mask, keys), TN),
                mm(grad_scores, own(mask, queries)),
                mm(weights.astype(jnp.bfloat16), own(mask, low)),
            )
            grads = [new if old is None else old + new for old, new in zip(grads, found)]
        root = root_ref[:, at]
        for part, (turned, unit_ref) in enumerate(((queries, uq_ref), (keys, uk_ref))):
            grad_turned = grads[part]
            turned = turned.astype(jnp.float32)
            dots = head_sums(grad_turned * turned) / (root * root)
            gs_ref[:, at] += 0.5 * jnp.sum(dots, axis=0, keepdims=True)
            inner = rotate(grad_turned - turned * dots, cos_ref[:, at], -sin_ref[:, at])
            g_ref[:, part * width + pair * 128 : part * width + pair * 128 + 128] = (
                inner * unit_ref[:, at]
            ).astype(jnp.bfloat16)
        g_ref[:, 2 * width + pair * 128 : 2 * width + pair * 128 + 128] = grads[2].astype(jnp.bfloat16)


def attention_backward(qkv, attended, inverse, grad_att, unit, cos, sin, root, images, after=()):
    rows, width = attended.shape
    seq = rows // images

    def part(array, index):
        return (array, (seq, width), lambda i: (i, index))

    def whole(array):
        return (array, array.shape, lambda i: (0, 0))

    return call(
        attention_back_kernel,
        (images,),
        [
            part(qkv, 0),
            part(qkv, 1),
            part(qkv, 2),
            part(attended, 0),
            part(inverse, 0),
            part(grad_att, 0),
            part(unit, 0),
            part(unit, 1),
            whole(cos),
            whole(sin),
            whole(root),
        ],
        [
            (jax.ShapeDtypeStruct((rows, 3 * width), jnp.bfloat16), (seq, 3 * width), lambda i: (i, 0)),
            (jax.ShapeDtypeStruct((1, width), jnp.float32), (1, width), lambda i: (0, 0)),
        ],
        flops=10 * rows * seq * width,
        moved=30 * rows * width,
        after=after,
    )


def qkv_grad_kernel(g_ref, normed_ref, out_ref):
    out_ref[...] = mm(g_ref[...], normed_ref[...], TN).astype(jnp.bfloat16)


def weight_grad(grad, inputs, after=()):
    rows, width = inputs.shape
    total, block = grad.shape[1], 512
    return call(
        qkv_grad_kernel,
        (total // block,),
        [
            (grad, (rows, block), lambda j: (0, j)),
            (inputs, inputs.shape, lambda j: (0, 0)),
        ],
        [(jax.ShapeDtypeStruct((total, width), jnp.bfloat16), (block, width), lambda j: (j, 0))],
        flops=2 * rows * width * total,
        moved=2 * (rows * total + rows * width + width * total),
        after=after,
    )[0]


def tokens_kernel(g_ref, w_ref, tok_ref, scale_ref, gm_ref, out_ref, gmod_ref, total_ref):
    step, steps = pl.program_id(0), pl.num_programs(0)
    part = mm(g_ref[...], w_ref[...], NT)

    @pl.when(step == 0)
    def _():
        total_ref[...] = part

    @pl.when(step > 0)
    def _():
        total_ref[...] += part

    @pl.when(step == steps - 1)
    def _():
        images = scale_ref.shape[0]
        seq = tok_ref.shape[0] // images
        for image in range(images):
            at = pl.ds(image * seq, seq)
            tok = tok_ref[at, :].astype(jnp.float32)
            inverse = lax.rsqrt(jnp.mean(tok * tok, axis=-1, keepdims=True) + EPSILON)
            unit = tok * inverse
            grad = total_ref[at, :]
            gmod_ref[image] = jnp.sum(grad * unit, axis=0, keepdims=True)
            scaled = grad * scale_ref[image]
            mean = jnp.mean(scaled * unit, axis=-1, keepdims=True)
            out_ref[at, :] = gm_ref[at, :] + inverse * (scaled - unit * mean)


def tokens_backward(grad_qkv, w_qkv, tokens, scale_attn, grad_mixed, after=()):
    rows, width = tokens.shape
    total, block = w_qkv.shape[1], 512
    images = scale_attn.shape[0]

    def whole(array):
        return (array, array.shape, lambda j: (0,) * array.ndim)

    return call(
        tokens_kernel,
        (total // block,),
        [
            (grad_qkv, (rows, block), lambda j: (0, j)),
            (w_qkv, (width, block), lambda j: (0, j)),
            whole(tokens),
            whole(scale_attn),
            whole(grad_mixed),
        ],
        [
            (jax.ShapeDtypeStruct((rows, width), jnp.float32), (rows, width), lambda j: (0, 0)),
            (jax.ShapeDtypeStruct((images, 1, width), jnp.float32), (images, 1, width), lambda j: (0, 0, 0)),
        ],
        scratch=[pltpu.VMEM((rows, width), jnp.float32)],
        flops=2 * rows * width * total,
        moved=2 * (rows * total + width * total) + 10 * rows * width,
        after=after,
    )


def norm_rows(values, gain):
    return values * lax.rsqrt(jnp.mean(values * values, axis=-1, keepdims=True) + EPSILON) * gain


def norm_back(values, gain, grad):
    inverse = lax.rsqrt(jnp.mean(values * values, axis=-1, keepdims=True) + EPSILON)
    unit = values * inverse
    scaled = grad * gain
    mean = jnp.mean(scaled * unit, axis=-1, keepdims=True)
    return inverse * (scaled - unit * mean), jnp.sum(grad * unit, axis=0, keepdims=True)


def gate_parts(gate):
    normal = 0.5 + 0.5 * lax.erf(gate * math.sqrt(0.5))
    density = jnp.exp(-0.5 * gate * gate) * (1.0 / math.sqrt(2.0 * math.pi))
    return gate * normal, normal + gate * density


def halves(value):
    high = value.astype(jnp.bfloat16)
    rest = (value - high.astype(jnp.float32)).astype(jnp.bfloat16)
    return jnp.concatenate([high, rest], axis=0)


def times(rows, weight, dims=NT):
    count = rows.shape[0]
    product = mm(halves(rows), weight, dims)
    return product[:count] + product[count:]


def outer(low_rows, rows):
    return mm(jnp.concatenate([low_rows, low_rows], axis=0), halves(rows), TN)


def first_rows(label, sigma, fourier_ref, table_ref, time_ref, gains_ref):
    level = (LOG_LOW + LOG_SPAN * sigma.astype(jnp.float32) / (NSIG - 1)) / 4.0
    angles = 2.0 * math.pi * level * fourier_ref[...]
    feats = jnp.concatenate([jnp.cos(angles), jnp.sin(angles)], axis=-1).astype(jnp.bfloat16)
    classes = lax.broadcasted_iota(jnp.int32, (label.shape[0], table_ref.shape[0]), 1)
    one_hot = jnp.where(classes == label, 1.0, 0.0).astype(jnp.bfloat16)
    start = mm(feats, time_ref[...]) + mm(one_hot, table_ref[...])
    first = norm_rows(start, gains_ref[0:1].astype(jnp.float32))
    hidden = norm_rows(first, gains_ref[1:2].astype(jnp.float32)).astype(jnp.bfloat16)
    return feats, one_hot, start, first, hidden


def map_kernel(
    label_ref,
    sigma_ref,
    fourier_ref,
    table_ref,
    time_ref,
    gains_ref,
    wa_ref,
    wb_ref,
    wd_ref,
    attn_ref,
    ffn_ref,
    scale_attn_ref,
    scale_ffn_ref,
    start_ref,
    first_ref,
    second_ref,
    up_ref,
    sent_ref,
    hidden_ref,
):
    step = pl.program_id(0)
    count = scale_attn_ref.shape[0]

    @pl.when(step == 0)
    def _():
        row = lax.broadcasted_iota(jnp.int32, (8, 1), 0)
        label, sigma = jnp.zeros((8, 1), jnp.int32), jnp.zeros((8, 1), jnp.int32)
        for image in range(count):
            label = jnp.where(row == image, label_ref[image], label)
            sigma = jnp.where(row == image, sigma_ref[image], sigma)
        lane = lax.broadcasted_iota(jnp.int32, (8, 128), 1)
        numbers = jnp.where(lane == 0, label, jnp.where(lane == 1, sigma, 0))
        for device in range(sent_ref.shape[0]):
            sent_ref[device] = numbers
        _, _, start, first, hidden = first_rows(
            label, sigma, fourier_ref, table_ref, time_ref, gains_ref
        )
        start_ref[...] = start
        first_ref[...] = first
        second_ref[...] = first
        hidden_ref[...] = hidden.astype(jnp.float32)

    hidden = hidden_ref[...].astype(jnp.bfloat16)
    value, gate = mm(hidden, wa_ref[...]), mm(hidden, wb_ref[...])
    up_ref[0] = value
    up_ref[1] = gate
    gated = (value * gate_parts(gate)[0]).astype(jnp.bfloat16)
    second_ref[...] += mm(gated, wd_ref[...])

    @pl.when(step == pl.num_programs(0) - 1)
    def _():
        cond = norm_rows(second_ref[...], gains_ref[2:3].astype(jnp.float32)).astype(jnp.bfloat16)
        for weight, scale_ref in ((attn_ref, scale_attn_ref), (ffn_ref, scale_ffn_ref)):
            scale = 1.0 + mm(cond, weight[...])
            for image in range(count):
                scale_ref[image] = scale[image : image + 1]


def whole(array):
    return (array, array.shape, lambda j: (0,) * array.ndim)


def fresh(shape, dtype=jnp.float32):
    return (jax.ShapeDtypeStruct(shape, dtype), shape, lambda j: (0,) * len(shape))


def hidden_blocks(w_map_up, w_map_down, block):
    width, steps = w_map_up.shape[0], w_map_down.shape[0] // block
    return [
        (w_map_up, (width, block), lambda j: (0, j)),
        (w_map_up, (width, block), lambda j: (0, steps + j)),
        (w_map_down, (block, width), lambda j: (j, 0)),
    ]


def scalars(array):
    return (array, None, None)


def map_forward(labels, sigma, fourier, table, w_time, w_up, w_down, gains, w_attn, w_ffn, devices):
    images, width = labels.shape[0], w_time.shape[1]
    hidden, block, model = w_down.shape[0], 384, w_attn.shape[1]
    return call(
        map_kernel,
        (hidden // block,),
        [
            scalars(labels),
            scalars(sigma),
            whole(fourier[None]),
            whole(table),
            whole(w_time),
            whole(gains),
            *hidden_blocks(w_up, w_down, block),
            whole(w_attn),
            whole(w_ffn),
        ],
        [
            fresh((images, 1, model)),
            fresh((images, 1, model)),
            fresh((8, width)),
            fresh((8, width)),
            fresh((8, width)),
            (jax.ShapeDtypeStruct((2, 8, hidden), jnp.float32), (2, 8, block), lambda j: (0, 0, j)),
            fresh((devices, 8, 128), jnp.int32),
        ],
        scratch=[pltpu.VMEM((8, width), jnp.float32)],
        flops=16 * width * (3 * hidden + 2 * model),
        moved=2 * width * (3 * hidden + 2 * model + 1256),
    )


def map_back_kernel(
    gattn_ref,
    gffn_ref,
    heads_ref,
    gains_ref,
    start_ref,
    first_ref,
    second_ref,
    up_ref,
    wa_ref,
    wb_ref,
    wd_ref,
    attn_ref,
    ffn_ref,
    sent_ref,
    gsecond_ref,
    gup_ref,
    ghidden_ref,
    gain_ref,
    rows_ref,
):
    step, steps = pl.program_id(0), pl.num_programs(0)
    count = gattn_ref.shape[0]
    block = wd_ref.shape[0]
    gains = gains_ref[...].astype(jnp.float32)

    @pl.when(step == 0)
    def _():
        rows_ref[...] = jnp.zeros_like(rows_ref)
        for image in range(count):
            rows_ref[0, image : image + 1] = gattn_ref[image]
            rows_ref[1, image : image + 1] = gffn_ref[image]
        grad = times(rows_ref[0], attn_ref[...]) + times(rows_ref[1], ffn_ref[...])
        gsecond, gain = norm_back(second_ref[...], gains[2:3], grad)
        gsecond_ref[...] = gsecond
        gain_ref[2:3] = gain
        ghidden_ref[...] = jnp.zeros_like(ghidden_ref)

    grad = times(gsecond_ref[...], wd_ref[...])
    bent, slope = gate_parts(up_ref[1])
    for part, (new, weight) in enumerate(((grad * bent, wa_ref), (grad * up_ref[0] * slope, wb_ref))):
        at = pl.multiple_of(step * block, block)
        gup_ref[part, :, pl.ds(at, block)] = new
        ghidden_ref[...] += times(new, weight[...])

    @pl.when(step == steps - 1)
    def _():
        gfirst, gain = norm_back(first_ref[...], gains[1:2], ghidden_ref[...])
        gain_ref[1:2] = gain
        gsecond = gsecond_ref[...]
        gstart, gain = norm_back(start_ref[...], gains[0:1], gfirst + gsecond)
        gain_ref[0:1] = gain
        model = heads_ref.shape[1]
        lane = lax.broadcasted_iota(jnp.int32, (model, 128), 1)
        row = lax.broadcasted_iota(jnp.int32, (model, 128), 0)
        pick = jnp.where(row == lane * 64, 1.0, 0.0).astype(jnp.bfloat16)
        heads = times(jnp.concatenate([heads_ref[...], jnp.zeros((7, model))], axis=0), pick, NN)
        sent_ref[...] = jnp.zeros_like(sent_ref)
        devices = sent_ref.shape[0]
        hidden = gup_ref.shape[2]
        for device in range(devices):
            spot = 0
            for values in (rows_ref[0], rows_ref[1], gsecond):
                width = values.shape[1] // devices
                sent_ref[device, 0:count, spot : spot + width] = values[
                    0:count, device * width : device * width + width
                ]
                spot += width
            width = 2 * hidden // devices
            part, at = divmod(device * width, hidden)
            sent_ref[device, 0:count, spot : spot + width] = gup_ref[part, 0:count, at : at + width]
            spot += width
            width = gstart.shape[1] // devices
            sent_ref[device, 0:count, spot : spot + width] = gstart[
                0:count, device * width : device * width + width
            ]
            for index in range(3):
                sent_ref[device, count : count + 1, index * width : index * width + width] = gain_ref[
                    index : index + 1, device * width : device * width + width
                ]
            used = model // 64
            sent_ref[device, count : count + 1, 3 * width : 3 * width + used] = heads[0:1, 0:used]


def map_backward(grad_attn, grad_ffn, heads, saved, gains, w_up, w_down, w_attn, w_ffn, devices, after=()):
    start, first, second, up = saved
    width, hidden, block = start.shape[1], w_down.shape[0], 384
    model = w_attn.shape[1]
    columns = -(-(2 * model + 2 * width + 2 * hidden) // devices // 128) * 128
    return call(
        map_back_kernel,
        (hidden // block,),
        [
            whole(grad_attn),
            whole(grad_ffn),
            whole(heads),
            whole(gains),
            whole(start),
            whole(first),
            whole(second),
            (up, (2, 8, block), lambda j: (0, 0, j)),
            *hidden_blocks(w_up, w_down, block),
            whole(w_attn),
            whole(w_ffn),
        ],
        [fresh((devices, 8, columns))],
        scratch=[
            pltpu.VMEM((8, width), jnp.float32),
            pltpu.VMEM((2, 8, hidden), jnp.float32),
            pltpu.VMEM((8, width), jnp.float32),
            pltpu.VMEM((8, width), jnp.float32),
            pltpu.VMEM((2, 8, model), jnp.float32),
        ],
        flops=32 * width * (3 * hidden + 2 * model),
        moved=2 * width * (3 * hidden + 2 * model),
        after=after,
    )[0]


def map_weights_kernel(
    numbers_ref,
    columns_ref,
    fourier_ref,
    table_ref,
    time_ref,
    gains_ref,
    wa_ref,
    wb_ref,
    wd_ref,
    class_ref,
    wtime_ref,
    wup_ref,
    wdown_ref,
    wgain_ref,
    wattn_ref,
    wffn_ref,
    heads_ref,
    hidden_ref,
    second_ref,
    number_rows,
    rows_ref,
):
    step = pl.program_id(0)
    devices, count = columns_ref.shape[0], rows_ref.shape[0] // columns_ref.shape[0]
    attn, ffn, second, up, start = (
        wattn_ref.shape[1],
        wffn_ref.shape[1],
        wdown_ref.shape[1],
        wup_ref.shape[1],
        class_ref.shape[1],
    )
    edges = [0]
    for width in (attn, ffn, second, up, start):
        edges.append(edges[-1] + width)

    def columns(index):
        return rows_ref[:, edges[index] : edges[index + 1]]

    @pl.when(step == 0)
    def _():
        extra = jnp.zeros((1, columns_ref.shape[2]), jnp.float32)
        for device in range(devices):
            at = slice(device * count, device * count + count)
            number_rows[at] = numbers_ref[device, 0:count]
            rows_ref[at] = columns_ref[device, 0:count]
            extra += columns_ref[device, count : count + 1]
        for index in range(3):
            wgain_ref[index : index + 1] = extra[:, index * start : index * start + start]
        heads_ref[...] = extra[:, 3 * start : 3 * start + heads_ref.shape[1]]
        numbers = number_rows[...]
        feats, one_hot, _, first, hidden = first_rows(
            numbers[:, 0:1], numbers[:, 1:2], fourier_ref, table_ref, time_ref, gains_ref
        )
        hidden_ref[...] = hidden
        second_ref[...] = first
        class_ref[...] = outer(one_hot, columns(4))
        wtime_ref[...] = outer(feats, columns(4))
        wup_ref[...] = outer(hidden, columns(3))

    hidden = hidden_ref[...]
    value, gate = mm(hidden, wa_ref[...]), mm(hidden, wb_ref[...])
    gated = (value * gate_parts(gate)[0]).astype(jnp.bfloat16)
    second_ref[...] += mm(gated, wd_ref[...])
    wdown_ref[...] = outer(gated, columns(2))

    @pl.when(step == pl.num_programs(0) - 1)
    def _():
        cond = norm_rows(second_ref[...], gains_ref[2:3].astype(jnp.float32)).astype(jnp.bfloat16)
        wattn_ref[...] = outer(cond, columns(0))
        wffn_ref[...] = outer(cond, columns(1))


def map_weights(numbers, columns, count, fourier, table, w_time, w_up, w_down, gains, model, after=()):
    devices = columns.shape[0]
    rows = devices * count
    width, hidden, block = w_time.shape[1], w_down.shape[0], 384
    own = width // devices
    return call(
        map_weights_kernel,
        (hidden // block,),
        [
            whole(numbers),
            whole(columns),
            whole(fourier[None]),
            whole(table),
            whole(w_time),
            whole(gains),
            *hidden_blocks(w_up, w_down, block),
        ],
        [
            fresh((table.shape[0], own)),
            fresh((w_time.shape[0], own)),
            fresh((width, 2 * hidden // devices)),
            (jax.ShapeDtypeStruct((hidden, own), jnp.float32), (block, own), lambda j: (j, 0)),
            fresh((3, own)),
            fresh((width, model // devices)),
            fresh((width, model // devices)),
            fresh((1, model // 64)),
        ],
        scratch=[
            pltpu.VMEM((rows, width), jnp.bfloat16),
            pltpu.VMEM((rows, width), jnp.float32),
            pltpu.VMEM((rows, 128), jnp.int32),
            pltpu.VMEM((rows, columns.shape[2]), jnp.float32),
        ],
        flops=2 * rows * width * 4 * hidden,
        moved=2 * width * (3 * hidden + 1256) + 4 * width * 400,
        after=after,
    )


class Halving:
    def __init__(self, base, dims, came=()):
        self.terms = [(base, tuple(dims))]
        self.done = []

    def side(self, name):
        if name == "core":
            return lax.axis_index("space")
        return (lax.axis_index("dp") >> name) & 1

    def total(self, fixed):
        found = None
        for base, dims in self.terms:
            where = [fixed.get(name, 0) for name in dims]
            sizes = [1 if name in fixed else 2 for name in dims]
            rest = base.shape[len(dims) :]
            part = lax.dynamic_slice(base, [*where, *([0] * len(rest))], [*sizes, *rest])
            left = [2 for name in dims if name not in fixed]
            part = part.reshape(*left, *rest).astype(jnp.float32)
            found = part if found is None else found + part
        return found

    def mine(self):
        return {name: self.side(name) for name in self.done}

    def send(self, name):
        fixed = {**self.mine(), name: 1 - self.side(name)}
        return self.total(fixed).astype(jnp.bfloat16)

    def take(self, name, came):
        first = self.terms[0][1]
        self.done.append(name)
        self.terms.append((came, tuple(n for n in first if n not in self.done)))

    def step(self, name, after=()):
        base, dims = self.terms[-1]
        self.terms[-1] = (held(base, after), dims)
        sent = self.send(name)
        self.take(name, trade(sent, name))
        return sent

    def result(self):
        return self.total(self.mine())


def trade(sent, name):
    if name == "core":
        return lax.ppermute(sent, "space", [(0, 1), (1, 0)])
    count = lax.axis_size("dp")
    return lax.ppermute(sent, "dp", [(i, i ^ (1 << name)) for i in range(count)])


def split_rows(grad, names):
    rows = grad.shape[0] // 2 ** len(names)
    return Halving(grad.reshape(*([2] * len(names)), rows, grad.shape[-1]), names)


def joined(pair, name):
    side = pair[0].side(name)
    totals = [piece.result() for piece in pair]
    sent = jnp.where(side == 1, totals[0], totals[1]).astype(jnp.bfloat16)
    kept = jnp.where(side == 1, totals[1], totals[0])
    dims = [n for n in pair[0].terms[0][1] if n not in pair[0].done]
    whole = Halving(kept, dims)
    whole.terms.append((trade(sent, name), tuple(dims)))
    return whole


def shards(
    tokens,
    cotangent,
    labels,
    sigma_index,
    fourier,
    class_table,
    w_time,
    w_map_up,
    w_map_down,
    map_gains,
    w_ada_attn,
    w_ada_ffn,
    w_qkv,
    head_scale,
    w_out,
    w_up,
    w_down,
):
    all_images, local_len, model_width = tokens.shape
    num_images = all_images // 2
    num_heads = head_scale.shape[0]
    head_dim = model_width // num_heads
    seq_len = 2 * local_len
    devices = lax.axis_size("dp") * lax.axis_size("space")
    core = lax.axis_index("space")

    def swap(value):
        return lax.ppermute(value, "space", [(0, 1), (1, 0)])

    def whole_images(value):
        kept = lax.dynamic_slice_in_dim(value, core * num_images, num_images, axis=0)
        sent = lax.dynamic_slice_in_dim(value, (1 - core) * num_images, num_images, axis=0)
        return jnp.concatenate([kept, swap(sent)], axis=1)

    def split_images(value):
        kept, came = value[:, :local_len], swap(value[:, local_len:])
        return jnp.where(
            core == 0,
            jnp.concatenate([kept, came], axis=0),
            jnp.concatenate([came, kept], axis=0),
        )

    tokens = whole_images(tokens).reshape(-1, model_width)
    cotangent = whole_images(cotangent).reshape(-1, model_width)
    cotangent_t = cotangent.T
    scale_attn, scale_ffn, *map_saved, numbers = map_forward(
        labels,
        sigma_index,
        fourier,
        class_table,
        w_time,
        w_map_up,
        w_map_down,
        map_gains,
        w_ada_attn,
        w_ada_ffn,
        devices,
    )
    tables = rope_tables(seq_len, num_heads, head_dim, GRID)
    cos, sin = [
        lax.dynamic_slice_in_dim(
            jnp.asarray(np.concatenate([table, table[:local_len]])), core * local_len, seq_len
        )
        for table in tables
    ]
    root = jnp.repeat(jnp.sqrt(head_scale.astype(jnp.float32)), head_dim)[None]

    levels = lax.axis_size("dp").bit_length() - 1
    every = [*reversed(range(levels)), "core"]
    low = list(range(levels - 2))
    swapped = [*reversed(low[:2]), *low[2:]]
    pieced = [levels - 1, *reversed(low), "core"]
    high = [levels - 2, levels - 1]

    all_numbers = lax.all_to_all(numbers, BOTH, 0, 0, tiled=True)
    normed, qkv, unit = project_qkv(tokens, scale_attn, w_qkv, cos, sin, root)
    attended, inverse, mixed, normed_ffn = attend(qkv, tokens, scale_ffn, w_out)

    def pieces(grad_up, grad_down):
        rows = grad_up.shape[1] // 2 ** (len(pieced) - 1)
        up = Halving(grad_up.reshape(*([2] * len(pieced)), rows, model_width), pieced)
        return up, split_rows(grad_down, every)

    grad_up, grad_down, partial, grad_partial = ffn(
        0,
        2,
        normed_ffn,
        cotangent,
        cotangent_t,
        w_up,
        w_down,
        mixed,
        None,
        after=[all_numbers],
    )
    up0, down0 = pieces(grad_up, grad_down)
    sent = [up0.step("core"), down0.step("core")]
    grad_up, grad_down, result, grad_nf = ffn(
        1, 2, normed_ffn, cotangent, cotangent_t, w_up, w_down, partial, grad_partial, after=sent
    )
    up1, down1 = pieces(grad_up, grad_down)
    now = [grad_nf]
    sent = [up0.step(low[0], now), down0.step(swapped[0], now), up1.step("core"), down1.step("core")]
    grad_mixed, grad_low, grad_att, grad_mod_ffn = mixed_backward(
        cotangent, mixed, grad_nf, scale_ffn, w_out, after=sent
    )
    grad_out = weight_grad(grad_low, attended)
    out = split_rows(grad_out, every)
    now = [grad_out]
    sent = [up1.step(low[0], now), down1.step(swapped[0], now), out.step("core")]
    grad_qkv, grad_scale = attention_backward(
        qkv, attended, inverse, grad_att, unit, cos, sin, root, num_images, after=sent
    )
    now = [grad_scale]
    sent = [down0.step(swapped[1], now), out.step(low[0], now)]
    grad_wide = weight_grad(grad_qkv, normed, after=sent)
    wide = split_rows(grad_wide, every)
    now = [grad_wide]
    sent = [up0.step(low[1], now), down1.step(swapped[1], now), wide.step("core")]
    grad_tokens, grad_mod_attn = tokens_backward(
        grad_qkv, w_qkv, tokens, scale_attn, grad_mixed, after=sent
    )
    now = [grad_mod_attn]
    sent = [wide.step(swapped[0], now), up1.step(low[1], now)]
    columns = lax.all_to_all(
        map_backward(
            grad_mod_attn,
            grad_mod_ffn,
            grad_scale,
            map_saved,
            map_gains,
            w_map_up,
            w_map_down,
            w_ada_attn,
            w_ada_ffn,
            devices,
            after=sent,
        ),
        BOTH,
        0,
        0,
        tiled=True,
    )
    (
        sum_class,
        sum_time,
        sum_map_up,
        sum_map_down,
        sum_gains,
        sum_ada_attn,
        sum_ada_ffn,
        sum_heads,
    ) = map_weights(
        all_numbers,
        columns,
        labels.shape[0],
        fourier,
        class_table,
        w_time,
        w_map_up,
        w_map_down,
        map_gains,
        model_width,
    )
    out.step(low[1], now)
    wide.step(swapped[1], now)
    for level in [*low[2:], *high]:
        for part in (down0, down1, out, wide):
            part.step(level, now)
    for level in low[2:]:
        up0.step(level, now)
        up1.step(level, now)
    out_tokens = split_images(
        held(result.astype(jnp.bfloat16), now).reshape(num_images, seq_len, -1)
    )
    up = joined((up0, up1), high[0])
    up.step(high[1])
    sum_up = up.result().T
    sum_down = jnp.concatenate([down0.result(), down1.result()], axis=1).T
    sum_out, sum_qkv = out.result().T, wide.result().T

    grad_tokens = split_images(grad_tokens.reshape(num_images, seq_len, -1))
    return (
        out_tokens,
        grad_tokens,
        sum_class,
        sum_time,
        sum_map_up,
        sum_map_down,
        sum_gains,
        sum_ada_attn,
        sum_ada_ffn,
        sum_qkv,
        sum_heads[0],
        sum_out,
        sum_up,
        sum_down,
    )


def solution(mesh):
    placed = (
        P("dp", "space", None),
        P("dp", "space", None),
        P(("dp", "space")),
        P(("dp", "space")),
        P(),
        P(),
        P(),
        P(),
        P(),
        P(),
        P(),
        P(),
        P(),
        P(),
        P(),
        P(),
        P(),
    )
    return jax.shard_map(
        shards,
        mesh=mesh,
        in_specs=placed,
        out_specs=(
            P("dp", "space", None),
            P("dp", "space", None),
            P(None, ("dp", "space")),
            P(None, ("dp", "space")),
            P(None, ("dp", "space")),
            P(None, ("dp", "space")),
            P(None, ("dp", "space")),
            P(None, ("dp", "space")),
            P(None, ("dp", "space")),
            P(None, ("dp", "space")),
            P(),
            P(None, ("dp", "space")),
            P(None, ("dp", "space")),
            P(None, ("dp", "space")),
        ),
        check_vma=False,
    )
```

```python
import functools
import math

import jax
import jax.numpy as jnp
import numpy as np
from jax import lax
from jax.experimental import pallas as pl
from jax.experimental.pallas import tpu as pltpu
from jax.sharding import PartitionSpec as P

NSIG = 64
GRID = 16


EPSILON = 1e-06
BOTH = ("dp", "space")
LOG_LOW = math.log(0.01)
LOG_SPAN = math.log(10000.0)


def rope_tables(tokens, heads, head_dim, side):
    quarter = head_dim // 8
    order = np.arange(quarter)[None, :] * heads + np.arange(heads)[:, None]
    frequency = np.exp(math.log(math.pi) + math.log(10.0) * order / (heads * quarter))
    places = np.arange(tokens)
    row = -1.0 + (2.0 * (places // side) + 1.0) / side
    col = -1.0 + (2.0 * (places % side) + 1.0) / side
    angles = np.concatenate(
        [row[:, None, None] * frequency[None], col[:, None, None] * frequency[None]], axis=-1
    )
    cos, sin, flat = np.cos(angles), np.sin(angles), np.zeros_like(angles)
    tables = [
        np.concatenate([cos, cos, flat + 1.0, flat + 1.0], axis=-1),
        np.concatenate([-sin, sin, flat, flat], axis=-1),
    ]
    return [table.reshape(tokens, heads * head_dim).astype(np.float32) for table in tables]


VMEM_LIMIT = 60 * 1024 * 1024
NN = (((1,), (0,)), ((), ()))
NT = (((1,), (1,)), ((), ()))
TN = (((0,), (0,)), ((), ()))


def mm(left, right, dims=NN):
    return lax.dot_general(left, right, dims, preferred_element_type=jnp.float32)


HEAVY = {'map_weights_kernel': 1000000}


def call(line, body, grid, ins, outs, scratch=(), flops=0, moved=0, prefetch=False):
    arrays = [array for array, _, _ in ins]
    least = min(range(len(arrays)), key=lambda k: arrays[k].size)
    if line:
        arrays[least] = lax.optimization_barrier((arrays[least], *line))[0]
    in_specs = [
        pl.BlockSpec(memory_space=pltpu.SMEM) if block is None else pl.BlockSpec(block, where)
        for _, block, where in ins
    ]
    out_specs = [pl.BlockSpec(block, where) for _, block, where in outs]
    if prefetch:
        layout = {
            "grid_spec": pltpu.PrefetchScalarGridSpec(
                num_scalar_prefetch=1,
                grid=grid,
                in_specs=in_specs[1:],
                out_specs=out_specs,
                scratch_shapes=list(scratch),
            )
        }
    else:
        layout = {
            "grid": grid,
            "in_specs": in_specs,
            "out_specs": out_specs,
            "scratch_shapes": list(scratch),
        }
    scale = HEAVY.get(getattr(body, "__name__", ""), 1)
    flops, moved = flops // 1000 + 1, moved // 1000 + 1
    results = pl.pallas_call(
        body,
        name=getattr(body, "__name__", "ffn_kernel"),
        out_shape=[shape for shape, _, _ in outs],
        compiler_params=pltpu.CompilerParams(
            dimension_semantics=("arbitrary",) * len(grid), vmem_limit_bytes=VMEM_LIMIT
        ),
        cost_estimate=pl.CostEstimate(flops=flops * scale, bytes_accessed=moved * scale, transcendentals=0),
        **layout,
    )(*arrays)
    line[:] = [min(results, key=lambda result: result.size)]
    return results


def whole(array):
    return (array, array.shape, lambda *j: (0,) * array.ndim)


def fresh(shape, dtype=jnp.float32):
    return (jax.ShapeDtypeStruct(shape, dtype), shape, lambda *j: (0,) * len(shape))


def scalars(array):
    return (array, None, None)


def store_parts(target, total, share):
    split = total.reshape(-1, 2, share, total.shape[1])
    for core in range(2):
        target[core] = split[:, core].reshape(target.shape[1:]).astype(jnp.bfloat16)


def head_sums(values):
    lanes = values.shape[1]
    row = lax.broadcasted_iota(jnp.int32, (lanes, lanes), 0) // (lanes // 2)
    col = lax.broadcasted_iota(jnp.int32, (lanes, lanes), 1) // (lanes // 2)
    ones = jnp.where(row == col, 1.0, 0.0).astype(jnp.bfloat16)
    high = values.astype(jnp.bfloat16)
    rest = (values - high.astype(jnp.float32)).astype(jnp.bfloat16)
    return mm(high, ones) + mm(rest, ones)


def rotate(values, cos, sin):
    lanes = values.shape[1]
    lane = lax.broadcasted_iota(jnp.int32, values.shape, 1)
    first = lane % (lanes // 2) < lanes // 8
    near = jnp.where(first, pltpu.roll(values, lanes - lanes // 8, 1), pltpu.roll(values, lanes // 8, 1))
    return values * cos + near * sin


def qkv_kernel(bits_ref, own_ref, came_ref, scale_ref, w_ref, cos_ref, sin_ref, root_ref, normed_ref, qkv_ref, unit_ref, both_ref):
    step = pl.program_id(0)
    count, seq = scale_ref.shape[0], cos_ref.shape[0]

    @pl.when(step == 0)
    def _():
        for image in range(count):
            rows = pl.ds(image * seq, seq)
            both = jnp.concatenate([own_ref[image], came_ref[image]], axis=0)
            both_ref[rows, :] = both
            tok = both.astype(jnp.float32)
            inverse = lax.rsqrt(jnp.mean(tok * tok, axis=-1, keepdims=True) + EPSILON)
            normed_ref[rows, :] = (tok * inverse * scale_ref[image]).astype(jnp.bfloat16)

    rotated = step < 2 * pl.num_programs(0) // 3

    @pl.when(rotated)
    def _():
        for image in range(count):
            rows = pl.ds(image * seq, seq)
            for lane in range(0, w_ref.shape[1], 256):
                wide = mm(normed_ref[rows, :], w_ref[:, lane : lane + 256])
                for part in range(0, 256, 128):
                    at = slice(lane + part, lane + part + 128)
                    heads = wide[:, part : part + 128]
                    unit = root_ref[:, at] * lax.rsqrt(head_sums(heads * heads) + EPSILON)
                    unit_ref[rows, at] = unit
                    turned = rotate(heads * unit, cos_ref[:, at], sin_ref[:, at])
                    qkv_ref[rows, at] = turned.astype(jnp.bfloat16)

    @pl.when(jnp.logical_not(rotated))
    def _():
        qkv_ref[...] = mm(normed_ref[...], w_ref[...]).astype(jnp.bfloat16)


def project_qkv(line, bits, tokens, came, scale_attn, w_qkv, cos, sin, root):
    count, half, width = came.shape
    rows = count * half * 2
    total, block = w_qkv.shape[1], 512
    steps = total // block
    turned = steps * 2 // 3
    per = width // block
    return call(
        line,
        qkv_kernel,
        (steps,),
        [
            scalars(bits),
            (tokens, (count, half, width), lambda j, bits: (bits[0], 0, 0)),
            whole(came),
            whole(scale_attn),
            (w_qkv, (width, block), lambda j, bits: (0, j)),
            (cos, (cos.shape[0], block), lambda j, bits: (0, j % per)),
            (sin, (sin.shape[0], block), lambda j, bits: (0, j % per)),
            (root, (1, block), lambda j, bits: (0, j % per)),
        ],
        [
            (jax.ShapeDtypeStruct((rows, width), jnp.bfloat16), (rows, width), lambda j, bits: (0, 0)),
            (jax.ShapeDtypeStruct((rows, total), jnp.bfloat16), (rows, block), lambda j, bits: (0, j)),
            (
                jax.ShapeDtypeStruct((rows, 2 * width), jnp.float32),
                (rows, block),
                lambda j, bits: (0, jnp.minimum(j, turned - 1)),
            ),
            fresh((rows, width), jnp.bfloat16),
        ],
        flops=2 * rows * width * total,
        moved=2 * width * total + 14 * rows * width,
        prefetch=True,
    )


def attention_kernel(
    bits_ref,
    q_ref,
    k_ref,
    v_ref,
    tok_ref,
    scale_ref,
    w_ref,
    own_ref,
    own_came_ref,
    other_ref,
    other_came_ref,
    att_ref,
    inv_ref,
    mixed_ref,
    nf_ref,
    cot_ref,
):
    cot_ref[0] = jnp.concatenate([own_ref[0], own_came_ref[0]], axis=0)
    cot_ref[1] = jnp.concatenate([other_came_ref[0], other_ref[0]], axis=0)
    seq, width = q_ref.shape
    left = lax.broadcasted_iota(jnp.int32, (seq, 128), 1) < 64
    for pair in range(width // 128):
        at = slice(pair * 128, pair * 128 + 128)
        queries, keys, values = q_ref[:, at], k_ref[:, at], v_ref[:, at]
        none, one = jnp.zeros_like(queries), jnp.ones_like(queries)
        weights0 = jnp.exp(mm(jnp.where(left, queries, none), keys, NT)).astype(jnp.bfloat16)
        weights1 = jnp.exp(mm(jnp.where(left, none, queries), keys, NT)).astype(jnp.bfloat16)
        both0 = mm(weights0, jnp.where(left, values, one))
        both1 = mm(weights1, jnp.where(left, one, values))
        totals = pltpu.roll(jnp.where(left, both1, both0), 64, 1)
        inverse = 1.0 / totals
        inv_ref[:, at] = inverse
        att_ref[:, at] = (jnp.where(left, both0, both1) * inverse).astype(jnp.bfloat16)
    mixed = tok_ref[...].astype(jnp.float32) + mm(att_ref[...], w_ref[...])
    mixed_ref[...] = mixed
    inverse = lax.rsqrt(jnp.mean(mixed * mixed, axis=-1, keepdims=True) + EPSILON)
    nf_ref[...] = (mixed * inverse * scale_ref[0]).astype(jnp.bfloat16)


def attend(line, bits, qkv, tokens, scale_ffn, w_out, cotangent, came):
    rows, width = tokens.shape
    images = scale_ffn.shape[0]
    seq = rows // images

    def part(index):
        return (qkv, (seq, width), lambda i, bits: (i, index))

    def result(dtype):
        return (jax.ShapeDtypeStruct((rows, width), dtype), (seq, width), lambda i, bits: (i, 0))

    return call(
        line,
        attention_kernel,
        (images,),
        [
            scalars(bits),
            part(0),
            part(1),
            part(2),
            (tokens, (seq, width), lambda i, bits: (i, 0)),
            (scale_ffn, (1, 1, width), lambda i, bits: (i, 0, 0)),
            whole(w_out),
            *[
                (array, (1, seq // 2, width), lambda i, bits, own=own: ((bits[0] if own else 1 - bits[0]) * images + i, 0, 0))
                for own in (True, False)
                for array in (cotangent, came)
            ],
        ],
        [
            result(jnp.bfloat16),
            result(jnp.float32),
            result(jnp.float32),
            result(jnp.bfloat16),
            (
                jax.ShapeDtypeStruct((2, rows, width), jnp.bfloat16),
                (2, seq, width),
                lambda i, bits: (0, i, 0),
            ),
        ],
        flops=2 * rows * width * width + 4 * rows * seq * width,
        moved=2 * width * width + 20 * rows * width,
        prefetch=True,
    )


def ffn_kernel(last, share, bits_ref, nf_ref, other_ref, cot_ref, wa_ref, wb_ref, wd_ref, *refs):
    if last:
        mixed_ref, y_in, g_in, *refs = refs
    up_own, up_sent, down_ref, *refs = refs
    if last:
        y_own, y_sent, g_own, g_sent, up_ref, y_ref, g_ref = refs
    else:
        y_out, g_out, up_ref, y_ref, g_ref = refs
    step, steps = pl.program_id(0), pl.num_programs(0)
    block = wa_ref.shape[1]
    rows, width = nf_ref.shape

    @pl.when(step == 0)
    def _():
        if last:
            y_ref[...] = y_in[...].astype(jnp.float32)
            g_ref[...] = g_in[...].astype(jnp.float32)
        else:
            y_ref[...] = jnp.zeros_like(y_ref)
            g_ref[...] = jnp.zeros_like(g_ref)

    size = 256
    found = []
    for side, inputs in enumerate((nf_ref, other_ref)):
        parts = []
        for start in range(0, rows, size):
            at = pl.ds(start, size)
            nf = inputs[at, :]
            value = mm(nf, wa_ref[...])
            gate = mm(nf, wb_ref[...])
            grad = mm(cot_ref[side, at, :], wd_ref[...], NT)
            bent, slope = gate_parts(gate)
            gated = (value * bent).astype(jnp.bfloat16)
            ga = (grad * bent).astype(jnp.bfloat16)
            gb = (grad * value * slope).astype(jnp.bfloat16)
            to = pl.ds(side * rows + start, size)
            y_ref[to, :] += mm(gated, wd_ref[...])
            g_ref[to, :] += mm(ga, wa_ref[...], NT) + mm(gb, wb_ref[...], NT)
            parts.append((ga, gb, gated))
        found.append([jnp.concatenate(part, axis=0) for part in zip(*parts)])
    for half in range(2):
        total = mm(found[0][half], nf_ref[...], TN) + mm(found[1][half], other_ref[...], TN)
        up_ref[half, pl.ds(pl.multiple_of(step * block, block), block), :] = total.astype(jnp.bfloat16)
    down = mm(cot_ref[0], found[0][2], TN) + mm(cot_ref[1], found[1][2], TN)
    down_ref[...] = down.astype(jnp.bfloat16)

    @pl.when(step == steps - 1)
    def _():
        own, other = bits_ref[1], 1 - bits_ref[1]
        group = 2 * share
        for half in range(2):
            for index in range(up_ref.shape[1] // (2 * group)):
                at = pl.ds(index * group, group)
                for side, target in ((own, up_own), (other, up_sent)):
                    spot = pl.multiple_of(index * 2 * group + side * group, group)
                    target[half, at, :] = up_ref[half, pl.ds(spot, group), :]
        if last:
            y_own[...] = mixed_ref[...] + y_ref[:rows, :]
            y_sent[...] = y_ref[rows:, :].astype(jnp.bfloat16)
            g_own[...] = g_ref[:rows, :]
            g_sent[...] = g_ref[rows:, :].astype(jnp.bfloat16)
        else:
            y_out[...] = y_ref[...].astype(jnp.bfloat16)
            g_out[...] = g_ref[...].astype(jnp.bfloat16)


def ffn(line, bits, piece, share, nf, other, cot, w_up, w_down, before=None):
    rows, width = nf.shape
    hidden, block = w_down.shape[0], 256
    across = hidden // 4
    steps = across // block
    last = before is not None

    def place(base):
        return lambda j, bits: (0, base // block + bits[0] * 2 * steps + j)

    halved = ((2, across // 2, width), jnp.bfloat16)
    down = (
        jax.ShapeDtypeStruct((width, across), jnp.bfloat16),
        (width, block),
        lambda j, bits: (0, j),
    )
    low, wide = ((rows, width), jnp.bfloat16), ((rows, width), jnp.float32)
    both = ((2 * rows, width), jnp.bfloat16)
    return call(
        line,
        functools.partial(ffn_kernel, last, share),
        (steps,),
        [
            scalars(bits),
            whole(nf),
            whole(other),
            whole(cot),
            (w_up, (width, block), place(piece * across)),
            (w_up, (width, block), place(hidden + piece * across)),
            (
                w_down,
                (block, width),
                lambda j, bits: (bits[0] * 2 * steps + piece * steps + j, 0),
            ),
            *([whole(array) for array in before] if last else []),
        ],
        [
            fresh(*halved),
            fresh(*halved),
            down,
            *([fresh(*wide), fresh(*low), fresh(*wide), fresh(*low)] if last else [fresh(*both), fresh(*both)]),
        ],
        scratch=[
            pltpu.VMEM((2, across, width), jnp.bfloat16),
            pltpu.VMEM((2 * rows, width), jnp.float32),
            pltpu.VMEM((2 * rows, width), jnp.float32),
        ],
        flops=36 * rows * width * across,
        moved=12 * width * across + 20 * rows * width,
        prefetch=True,
    )


def mixed_kernel(cot_ref, mixed_ref, gnf_ref, came_ref, scale_ref, w_ref, gm_ref, low_ref, gatt_ref, gmod_ref):
    mixed, scale = mixed_ref[...], scale_ref[0]
    inverse = lax.rsqrt(jnp.mean(mixed * mixed, axis=-1, keepdims=True) + EPSILON)
    grad = gnf_ref[...] + came_ref[...].astype(jnp.float32)
    unit = mixed * inverse
    gmod_ref[0] = jnp.sum(grad * unit, axis=0, keepdims=True)
    scaled = grad * scale
    mean = jnp.mean(scaled * unit, axis=-1, keepdims=True)
    total = cot_ref[0].astype(jnp.float32) + inverse * (scaled - unit * mean)
    gm_ref[...] = total
    low = total.astype(jnp.bfloat16)
    low_ref[...] = low
    gatt_ref[...] = mm(low, w_ref[...], NT).astype(jnp.bfloat16)


def mixed_backward(line, cot, mixed, grad_nf, came, scale_ffn, w_out):
    rows, width = mixed.shape
    images = scale_ffn.shape[0]
    seq = rows // images

    def own(array):
        return (array, (seq, width), lambda i: (i, 0))

    def result(dtype):
        return (jax.ShapeDtypeStruct((rows, width), dtype), (seq, width), lambda i: (i, 0))

    return call(
        line,
        mixed_kernel,
        (images,),
        [
            (cot, (1, seq, width), lambda i: (0, i, 0)),
            own(mixed),
            own(grad_nf),
            own(came),
            (scale_ffn, (1, 1, width), lambda i: (i, 0, 0)),
            (w_out, w_out.shape, lambda i: (0, 0)),
        ],
        [
            result(jnp.float32),
            result(jnp.bfloat16),
            result(jnp.bfloat16),
            (jax.ShapeDtypeStruct((images, 1, width), jnp.float32), (1, 1, width), lambda i: (i, 0, 0)),
        ],
        flops=2 * rows * width * width,
        moved=2 * width * width + 18 * rows * width,
    )


def attention_back_kernel(
    q_ref, k_ref, v_ref, att_ref, inv_ref, gatt_ref, uq_ref, uk_ref, cos_ref, sin_ref, root_ref, g_ref, gs_ref
):
    seq, width = q_ref.shape
    lane = lax.broadcasted_iota(jnp.int32, (seq, 128), 1)
    left = lane < 64

    @pl.when(pl.program_id(0) == 0)
    def _():
        gs_ref[...] = jnp.zeros_like(gs_ref)

    def own(mask, values):
        return jnp.where(mask, values, jnp.zeros_like(values))

    for pair in range(width // 128):
        at = slice(pair * 128, pair * 128 + 128)
        queries, keys, values = q_ref[:, at], k_ref[:, at], v_ref[:, at]
        grad = gatt_ref[:, at].astype(jnp.float32) * inv_ref[:, at]
        low = grad.astype(jnp.bfloat16)
        along = grad * att_ref[:, at].astype(jnp.float32)
        grads = [None, None, None]
        for head in range(2):
            mask = left if head == 0 else jnp.logical_not(left)
            delta = -jnp.sum(own(mask, along), axis=-1, keepdims=True)
            high = delta.astype(jnp.bfloat16).astype(jnp.float32)
            spot = 64 if head == 0 else 0
            extra = jnp.where(lane == spot, high, jnp.where(lane == spot + 1, delta - high, 0.0))
            ones = jnp.where((lane == spot) | (lane == spot + 1), 1.0, 0.0).astype(jnp.bfloat16)
            shifted = jnp.where(mask, low, extra.astype(jnp.bfloat16))
            weights = jnp.exp(mm(keys, own(mask, queries), NT))
            grad_scores = (weights * mm(jnp.where(mask, values, ones), shifted, NT)).astype(jnp.bfloat16)
            found = (
                mm(grad_scores, own(mask, keys), TN),
                mm(grad_scores, own(mask, queries)),
                mm(weights.astype(jnp.bfloat16), own(mask, low)),
            )
            grads = [new if old is None else old + new for old, new in zip(grads, found)]
        root = root_ref[:, at]
        for part, (turned, unit_ref) in enumerate(((queries, uq_ref), (keys, uk_ref))):
            grad_turned = grads[part]
            turned = turned.astype(jnp.float32)
            dots = head_sums(grad_turned * turned) / (root * root)
            gs_ref[:, at] += 0.5 * jnp.sum(dots, axis=0, keepdims=True)
            inner = rotate(grad_turned - turned * dots, cos_ref[:, at], -sin_ref[:, at])
            g_ref[:, part * width + pair * 128 : part * width + pair * 128 + 128] = (
                inner * unit_ref[:, at]
            ).astype(jnp.bfloat16)
        g_ref[:, 2 * width + pair * 128 : 2 * width + pair * 128 + 128] = grads[2].astype(jnp.bfloat16)


def attention_backward(line, qkv, attended, inverse, grad_att, unit, cos, sin, root, images):
    rows, width = attended.shape
    seq = rows // images

    def part(array, index):
        return (array, (seq, width), lambda i: (i, index))


    return call(
        line,
        attention_back_kernel,
        (images,),
        [
            part(qkv, 0),
            part(qkv, 1),
            part(qkv, 2),
            part(attended, 0),
            part(inverse, 0),
            part(grad_att, 0),
            part(unit, 0),
            part(unit, 1),
            whole(cos),
            whole(sin),
            whole(root),
        ],
        [
            (jax.ShapeDtypeStruct((rows, 3 * width), jnp.bfloat16), (seq, 3 * width), lambda i: (i, 0)),
            (jax.ShapeDtypeStruct((1, width), jnp.float32), (1, width), lambda i: (0, 0)),
        ],
        flops=10 * rows * seq * width,
        moved=30 * rows * width,
    )


def weight_kernel(grad_ref, inputs_ref, both_ref, *, rows):
    store_parts(both_ref, mm(grad_ref[...], inputs_ref[...], TN), rows)


def weight_grad(line, grad, inputs, share, block):
    rows, width = inputs.shape
    total = grad.shape[1]
    return call(
        line,
        functools.partial(weight_kernel, rows=share),
        (total // block,),
        [
            (grad, (rows, block), lambda j: (0, j)),
            whole(inputs),
        ],
        [
            (
                jax.ShapeDtypeStruct((2, total // 2, width), jnp.bfloat16),
                (2, block // 2, width),
                lambda j: (0, j, 0),
            )
        ],
        flops=2 * rows * width * total,
        moved=2 * (rows * total + rows * width + width * total),
    )[0]


def tokens_kernel(g_ref, w_ref, tok_ref, scale_ref, gm_ref, out_ref, gmod_ref, total_ref):
    step, steps = pl.program_id(0), pl.num_programs(0)
    part = mm(g_ref[...], w_ref[...], NT)

    @pl.when(step == 0)
    def _():
        total_ref[...] = part

    @pl.when(step > 0)
    def _():
        total_ref[...] += part

    @pl.when(step == steps - 1)
    def _():
        images = scale_ref.shape[0]
        seq = tok_ref.shape[0] // images
        for image in range(images):
            at = pl.ds(image * seq, seq)
            tok = tok_ref[at, :].astype(jnp.float32)
            inverse = lax.rsqrt(jnp.mean(tok * tok, axis=-1, keepdims=True) + EPSILON)
            unit = tok * inverse
            grad = total_ref[at, :]
            gmod_ref[image] = jnp.sum(grad * unit, axis=0, keepdims=True)
            scaled = grad * scale_ref[image]
            mean = jnp.mean(scaled * unit, axis=-1, keepdims=True)
            out_ref[at, :] = gm_ref[at, :] + inverse * (scaled - unit * mean)


def tokens_backward(line, grad_qkv, w_qkv, tokens, scale_attn, grad_mixed):
    rows, width = tokens.shape
    total, block = w_qkv.shape[1], 512
    images = scale_attn.shape[0]


    return call(
        line,
        tokens_kernel,
        (total // block,),
        [
            (grad_qkv, (rows, block), lambda j: (0, j)),
            (w_qkv, (width, block), lambda j: (0, j)),
            whole(tokens),
            whole(scale_attn),
            whole(grad_mixed),
        ],
        [
            (jax.ShapeDtypeStruct((rows, width), jnp.float32), (rows, width), lambda j: (0, 0)),
            (jax.ShapeDtypeStruct((images, 1, width), jnp.float32), (images, 1, width), lambda j: (0, 0, 0)),
        ],
        scratch=[pltpu.VMEM((rows, width), jnp.float32)],
        flops=2 * rows * width * total,
        moved=2 * (rows * total + width * total) + 10 * rows * width,
    )


def norm_rows(values, gain):
    return values * lax.rsqrt(jnp.mean(values * values, axis=-1, keepdims=True) + EPSILON) * gain


def norm_back(values, gain, grad):
    inverse = lax.rsqrt(jnp.mean(values * values, axis=-1, keepdims=True) + EPSILON)
    unit = values * inverse
    scaled = grad * gain
    mean = jnp.mean(scaled * unit, axis=-1, keepdims=True)
    return inverse * (scaled - unit * mean), jnp.sum(grad * unit, axis=0, keepdims=True)


def gate_parts(gate):
    normal = 0.5 + 0.5 * lax.erf(gate * math.sqrt(0.5))
    density = jnp.exp(-0.5 * gate * gate) * (1.0 / math.sqrt(2.0 * math.pi))
    return gate * normal, normal + gate * density


def halves(value):
    high = value.astype(jnp.bfloat16)
    rest = (value - high.astype(jnp.float32)).astype(jnp.bfloat16)
    return jnp.concatenate([high, rest], axis=0)


def times(rows, weight, dims=NT):
    count = rows.shape[0]
    product = mm(halves(rows), weight, dims)
    return product[:count] + product[count:]


def outer(low_rows, rows):
    return mm(halves(rows), jnp.concatenate([low_rows, low_rows], axis=0), TN)


def first_rows(label, sigma, fourier_ref, table_ref, time_ref, gains_ref):
    level = (LOG_LOW + LOG_SPAN * sigma.astype(jnp.float32) / (NSIG - 1)) / 4.0
    angles = 2.0 * math.pi * level * fourier_ref[...]
    feats = jnp.concatenate([jnp.cos(angles), jnp.sin(angles)], axis=-1).astype(jnp.bfloat16)
    classes = lax.broadcasted_iota(jnp.int32, (label.shape[0], table_ref.shape[0]), 1)
    one_hot = jnp.where(classes == label, 1.0, 0.0).astype(jnp.bfloat16)
    start = mm(feats, time_ref[...]) + mm(one_hot, table_ref[...])
    first = norm_rows(start, gains_ref[0:1].astype(jnp.float32))
    hidden = norm_rows(first, gains_ref[1:2].astype(jnp.float32)).astype(jnp.bfloat16)
    return feats, one_hot, start, first, hidden


def map_kernel(
    label_ref,
    sigma_ref,
    fourier_ref,
    table_ref,
    time_ref,
    gains_ref,
    wa_ref,
    wb_ref,
    wd_ref,
    attn_ref,
    ffn_ref,
    scale_attn_ref,
    scale_ffn_ref,
    start_ref,
    first_ref,
    second_ref,
    up_ref,
    numbers_ref,
    hidden_ref,
):
    step = pl.program_id(0)
    count = scale_attn_ref.shape[0]

    @pl.when(step == 0)
    def _():
        row = lax.broadcasted_iota(jnp.int32, (8, 1), 0)
        label, sigma = jnp.zeros((8, 1), jnp.int32), jnp.zeros((8, 1), jnp.int32)
        for image in range(count):
            label = jnp.where(row == image, label_ref[image], label)
            sigma = jnp.where(row == image, sigma_ref[image], sigma)
        lane = lax.broadcasted_iota(jnp.int32, (8, 128), 1)
        numbers = jnp.where(lane == 0, label, jnp.where(lane == 1, sigma, 0))
        numbers_ref[...] = numbers.astype(jnp.float32)
        _, _, start, first, hidden = first_rows(
            label, sigma, fourier_ref, table_ref, time_ref, gains_ref
        )
        start_ref[...] = start
        first_ref[...] = first
        second_ref[...] = first
        hidden_ref[...] = hidden.astype(jnp.float32)

    hidden = hidden_ref[...].astype(jnp.bfloat16)
    value, gate = mm(hidden, wa_ref[...]), mm(hidden, wb_ref[...])
    up_ref[0] = value
    up_ref[1] = gate
    gated = (value * gate_parts(gate)[0]).astype(jnp.bfloat16)
    second_ref[...] += mm(gated, wd_ref[...])

    @pl.when(step == pl.num_programs(0) - 1)
    def _():
        cond = norm_rows(second_ref[...], gains_ref[2:3].astype(jnp.float32)).astype(jnp.bfloat16)
        for weight, scale_ref in ((attn_ref, scale_attn_ref), (ffn_ref, scale_ffn_ref)):
            scale = 1.0 + mm(cond, weight[...])
            for image in range(count):
                scale_ref[image] = scale[image : image + 1]


def hidden_blocks(w_map_up, w_map_down, block):
    width, steps = w_map_up.shape[0], w_map_down.shape[0] // block
    return [
        (w_map_up, (width, block), lambda j: (0, j)),
        (w_map_up, (width, block), lambda j: (0, steps + j)),
        (w_map_down, (block, width), lambda j: (j, 0)),
    ]


def map_forward(line, labels, sigma, fourier, table, w_time, w_up, w_down, gains, w_attn, w_ffn):
    images, width = labels.shape[0], w_time.shape[1]
    hidden, block, model = w_down.shape[0], 384, w_attn.shape[1]
    return call(
        line,
        map_kernel,
        (hidden // block,),
        [
            scalars(labels),
            scalars(sigma),
            whole(fourier[None]),
            whole(table),
            whole(w_time),
            whole(gains),
            *hidden_blocks(w_up, w_down, block),
            whole(w_attn),
            whole(w_ffn),
        ],
        [
            fresh((images, 1, model)),
            fresh((images, 1, model)),
            fresh((8, width)),
            fresh((8, width)),
            fresh((8, width)),
            (jax.ShapeDtypeStruct((2, 8, hidden), jnp.float32), (2, 8, block), lambda j: (0, 0, j)),
            fresh((8, 128)),
        ],
        scratch=[pltpu.VMEM((8, width), jnp.float32)],
        flops=16 * width * (3 * hidden + 2 * model),
        moved=2 * width * (3 * hidden + 2 * model + 1256),
    )


def map_back_kernel(
    gattn_ref,
    gffn_ref,
    heads_ref,
    numbers_ref,
    gains_ref,
    start_ref,
    first_ref,
    second_ref,
    up_ref,
    wa_ref,
    wb_ref,
    wd_ref,
    attn_ref,
    ffn_ref,
    sent_ref,
    gsecond_ref,
    gup_ref,
    ghidden_ref,
    gain_ref,
    rows_ref,
):
    step, steps = pl.program_id(0), pl.num_programs(0)
    count = gattn_ref.shape[0]
    block = wd_ref.shape[0]
    gains = gains_ref[...].astype(jnp.float32)

    @pl.when(step == 0)
    def _():
        rows_ref[...] = jnp.zeros_like(rows_ref)
        for image in range(count):
            rows_ref[0, image : image + 1] = gattn_ref[image]
            rows_ref[1, image : image + 1] = gffn_ref[image]
        grad = times(rows_ref[0], attn_ref[...]) + times(rows_ref[1], ffn_ref[...])
        gsecond, gain = norm_back(second_ref[...], gains[2:3], grad)
        gsecond_ref[...] = gsecond
        gain_ref[2:3] = gain
        ghidden_ref[...] = jnp.zeros_like(ghidden_ref)

    grad = times(gsecond_ref[...], wd_ref[...])
    bent, slope = gate_parts(up_ref[1])
    for part, (new, weight) in enumerate(((grad * bent, wa_ref), (grad * up_ref[0] * slope, wb_ref))):
        at = pl.multiple_of(step * block, block)
        gup_ref[part, :, pl.ds(at, block)] = new
        ghidden_ref[...] += times(new, weight[...])

    @pl.when(step == steps - 1)
    def _():
        gfirst, gain = norm_back(first_ref[...], gains[1:2], ghidden_ref[...])
        gain_ref[1:2] = gain
        gsecond = gsecond_ref[...]
        gstart, gain = norm_back(start_ref[...], gains[0:1], gfirst + gsecond)
        gain_ref[0:1] = gain
        model = heads_ref.shape[1]
        lane = lax.broadcasted_iota(jnp.int32, (model, 128), 1)
        row = lax.broadcasted_iota(jnp.int32, (model, 128), 0)
        pick = jnp.where(row == lane * 64, 1.0, 0.0).astype(jnp.bfloat16)
        heads = times(jnp.concatenate([heads_ref[...], jnp.zeros((7, model))], axis=0), pick, NN)
        sent_ref[...] = jnp.zeros_like(sent_ref)
        devices = sent_ref.shape[0]
        hidden = gup_ref.shape[2]
        for device in range(devices):
            spot = 0
            for values in (rows_ref[0], rows_ref[1], gsecond):
                width = values.shape[1] // devices
                sent_ref[device, 0:count, spot : spot + width] = values[
                    0:count, device * width : device * width + width
                ]
                spot += width
            width = 2 * hidden // devices
            part, at = divmod(device * width, hidden)
            sent_ref[device, 0:count, spot : spot + width] = gup_ref[part, 0:count, at : at + width]
            spot += width
            width = gstart.shape[1] // devices
            sent_ref[device, 0:count, spot : spot + width] = gstart[
                0:count, device * width : device * width + width
            ]
            for index in range(3):
                sent_ref[device, count : count + 1, index * width : index * width + width] = gain_ref[
                    index : index + 1, device * width : device * width + width
                ]
            sent_ref[device, count + 1 : 2 * count + 1, 0:128] = numbers_ref[0:count]
            used = model // 64
            sent_ref[device, count : count + 1, 3 * width : 3 * width + used] = heads[0:1, 0:used]


def map_backward(line, grad_attn, grad_ffn, heads, saved, gains, w_up, w_down, w_attn, w_ffn, devices):
    start, first, second, up, numbers = saved
    width, hidden, block = start.shape[1], w_down.shape[0], 384
    model = w_attn.shape[1]
    columns = -(-(2 * model + 2 * width + 2 * hidden) // devices // 128) * 128
    return call(
        line,
        map_back_kernel,
        (hidden // block,),
        [
            whole(grad_attn),
            whole(grad_ffn),
            whole(heads),
            whole(numbers),
            whole(gains),
            whole(start),
            whole(first),
            whole(second),
            (up, (2, 8, block), lambda j: (0, 0, j)),
            *hidden_blocks(w_up, w_down, block),
            whole(w_attn),
            whole(w_ffn),
        ],
        [fresh((devices, 8, columns))],
        scratch=[
            pltpu.VMEM((8, width), jnp.float32),
            pltpu.VMEM((2, 8, hidden), jnp.float32),
            pltpu.VMEM((8, width), jnp.float32),
            pltpu.VMEM((8, width), jnp.float32),
            pltpu.VMEM((2, 8, model), jnp.float32),
        ],
        flops=32 * width * (3 * hidden + 2 * model),
        moved=2 * width * (3 * hidden + 2 * model),
    )[0]


def map_weights_kernel(
    columns_ref,
    fourier_ref,
    table_ref,
    time_ref,
    gains_ref,
    wa_ref,
    wb_ref,
    wd_ref,
    class_ref,
    wtime_ref,
    wup_ref,
    wdown_ref,
    wgain_ref,
    wattn_ref,
    wffn_ref,
    heads_ref,
    hidden_ref,
    second_ref,
    number_rows,
    rows_ref,
):
    step = pl.program_id(0)
    devices, count = columns_ref.shape[0], rows_ref.shape[0] // columns_ref.shape[0]
    attn, ffn, second, up, start = (
        wattn_ref.shape[0],
        wffn_ref.shape[0],
        wdown_ref.shape[0],
        wup_ref.shape[0],
        class_ref.shape[0],
    )
    edges = [0]
    for width in (attn, ffn, second, up, start):
        edges.append(edges[-1] + width)

    def columns(index):
        return rows_ref[:, edges[index] : edges[index + 1]]

    @pl.when(step == 0)
    def _():
        extra = jnp.zeros((1, columns_ref.shape[2]), jnp.float32)
        for device in range(devices):
            at = slice(device * count, device * count + count)
            number_rows[at] = columns_ref[device, count + 1 : 2 * count + 1, 0:128]
            rows_ref[at] = columns_ref[device, 0:count]
            extra += columns_ref[device, count : count + 1]
        for index in range(3):
            wgain_ref[index : index + 1] = extra[:, index * start : index * start + start]
        heads_ref[...] = extra[:, 3 * start : 3 * start + heads_ref.shape[1]]
        numbers = number_rows[...].astype(jnp.int32)
        feats, one_hot, _, first, hidden = first_rows(
            numbers[:, 0:1], numbers[:, 1:2], fourier_ref, table_ref, time_ref, gains_ref
        )
        hidden_ref[...] = hidden
        second_ref[...] = first
        class_ref[...] = outer(one_hot, columns(4))
        wtime_ref[...] = outer(feats, columns(4))
        wup_ref[...] = outer(hidden, columns(3))

    hidden = hidden_ref[...]
    value, gate = mm(hidden, wa_ref[...]), mm(hidden, wb_ref[...])
    gated = (value * gate_parts(gate)[0]).astype(jnp.bfloat16)
    second_ref[...] += mm(gated, wd_ref[...])
    wdown_ref[...] = outer(gated, columns(2))

    @pl.when(step == pl.num_programs(0) - 1)
    def _():
        cond = norm_rows(second_ref[...], gains_ref[2:3].astype(jnp.float32)).astype(jnp.bfloat16)
        wattn_ref[...] = outer(cond, columns(0))
        wffn_ref[...] = outer(cond, columns(1))


def map_weights(line, columns, count, fourier, table, w_time, w_up, w_down, gains, model):
    devices = columns.shape[0]
    rows = devices * count
    width, hidden, block = w_time.shape[1], w_down.shape[0], 384
    own = width // devices
    return call(
        line,
        map_weights_kernel,
        (hidden // block,),
        [
            whole(columns),
            whole(fourier[None]),
            whole(table),
            whole(w_time),
            whole(gains),
            *hidden_blocks(w_up, w_down, block),
        ],
        [
            fresh((own, table.shape[0])),
            fresh((own, w_time.shape[0])),
            fresh((2 * hidden // devices, width)),
            (jax.ShapeDtypeStruct((own, hidden), jnp.float32), (own, block), lambda j: (0, j)),
            fresh((3, own)),
            fresh((model // devices, width)),
            fresh((model // devices, width)),
            fresh((1, model // 64)),
        ],
        scratch=[
            pltpu.VMEM((rows, width), jnp.bfloat16),
            pltpu.VMEM((rows, width), jnp.float32),
            pltpu.VMEM((rows, 128), jnp.float32),
            pltpu.VMEM((rows, columns.shape[2]), jnp.float32),
        ],
        flops=2 * rows * width * 4 * hidden,
        moved=2 * width * (3 * hidden + 1256) + 4 * width * 400,
    )


class Sum:
    def __init__(self, terms, columns, pair=None):
        self.lists = [terms] if pair is None else [pair[0].lists[0], pair[1].lists[0]]
        self.more = []
        self.level = None
        self.done = [] if pair is None else list(pair[0].done)
        self.columns = columns
        self.lone = None if pair is None else pair[0].lone
        self.stacked = False

    def last(self):
        return self.lists[0][-1][0]

    def together(self):
        self.stacked = True
        return self

    def apart(self):
        self.stacked = False
        return self

    def dims(self):
        return self.lists[0][0][1]

    def left(self):
        return [name for name in self.dims() if name not in self.done]


def columns_of(part, start, count):
    return Sum([(array, dims, start) for array, dims, _ in part.lists[0]], count)


def paired(grad, names):
    total = lax.psum_scatter(grad, "space", scatter_dimension=0, tiled=True)
    rows = total.size // grad.shape[-1] // 2 ** len(names)
    shape = (*([2] * len(names)), rows, grad.shape[-1])
    return Sum([(total.reshape(shape), names, 0)], grad.shape[-1])


def split(own, sent, level, names, lone=None):
    came = trade(sent, level, lone)
    rows = own.size // own.shape[-1] // 2 ** len(names)
    shape = (*([2] * len(names)), rows, own.shape[-1])
    return Sum([(array.reshape(shape), names, 0) for array in (own, came)], own.shape[-1])


def joined(pair):
    return Sum(None, pair[0].columns, pair)


def combine(line, bits, jobs, steps):
    ins, outs, plan = [scalars(bits)], [], []

    def place(dims, fixed, column, width, block):
        def where(step, bits):
            spots = []
            for name in dims:
                if isinstance(name, tuple):
                    spots.append(name[1])
                elif name not in fixed:
                    spots.append(0)
                else:
                    spot = 0 if name == "core" else 1 + name
                    spots.append(bits[spot] if fixed[name] else 1 - bits[spot])
            return (*spots, 0, column // block + step)

        return where

    for part, level in jobs:
        block = part.columns // steps
        fixed = {name: True for name in part.done}
        pick = part.level
        whole_sum = isinstance(level, tuple)
        if level is not None and pick != level and not whole_sum:
            fixed[level] = False
        groups = []
        for terms in [*part.lists, part.more]:
            group = []
            for array, dims, column in terms:
                rows = array.shape[-2]
                shape = (
                    *[1 if name in fixed or isinstance(name, tuple) else 2 for name in dims],
                    rows,
                    block,
                )
                group.append(len(ins) - 1)
                ins.append((array, shape, place(dims, fixed, column, part.columns, block)))
            groups.append(group)
        dims = [name for name in part.dims() if name not in fixed]
        shape = (*[2 for _ in dims], rows, part.columns)
        if part.stacked:
            dims, shape = [("at", 0), *dims], (2, *shape)
        dtype = jnp.bfloat16 if level is not None else jnp.float32
        outs.append(
            (jax.ShapeDtypeStruct(shape, dtype), (*shape[:-1], block), place(dims, {}, 0, 0, block))
        )
        plan.append((groups, pick, pick is not None and pick == level, part.stacked))

    def combine_kernel(bits_ref, *refs):
        results = refs[len(ins) - 1 :]
        for (groups, pick, swap, both), result in zip(plan, results):

            def total(group):
                found = None
                for index in group:
                    value = refs[index][...].reshape(shape).astype(jnp.float32)
                    found = value if found is None else found + value
                return found

            shape = result.shape[1:] if both else result.shape
            if both:
                for index in range(2):
                    result[index] = total(groups[index]).astype(result.dtype)
                continue
            found = total(groups[0])
            if pick is not None:
                first = bits_ref[1 + pick] == (1 if swap else 0)
                found = jnp.where(first, found, total(groups[1]))
            if groups[-1]:
                found = found + total(groups[-1])
            result[...] = found.astype(result.dtype)

    moved = sum(array.size for array, _, _ in ins)
    return call(line, combine_kernel, (steps,), ins, outs, moved=moved, prefetch=True)


def finish(line, bits, near, up, down, first, second, out, came):
    ins, groups = [scalars(bits)], []

    def add(terms, done, block, moving):
        group = []
        for array, dims, column in terms:
            group.append(len(ins) - 1)
            shape = (*[1] * len(dims), array.shape[-2], block)

            def where(step, bits, dims=dims, column=column):
                spots = []
                for name in dims:
                    if isinstance(name, tuple):
                        spots.append(name[1])
                    else:
                        spots.append(bits[0] if name == "core" else bits[1 + name])
                return (*spots, 0, column // block + (step if moving else 0))

            ins.append((array, shape, where))
        groups.append(group)

    half = up.columns // 2
    add(up.lists[0], up.done, half, True)
    add(up.lists[1], up.done, half, True)
    add(up.more, up.done, half, True)
    add([(came[0], (), 0)], (), half, True)
    add(down.lists[0], down.done, down.columns, False)
    add(down.lists[1], down.done, down.columns, False)
    add([(came[1], (("at", 0),), 0)], (), down.columns, False)
    add([(came[1], (("at", 1),), 0)], (), down.columns, False)
    add(first.lists[0], first.done, first.columns, False)
    add(second.lists[0], second.done, second.columns, False)
    add(out.lists[0], out.done, out.columns // 2, True)
    count = len(ins) - 1
    pick = up.level

    def finish_kernel(bits_ref, *refs):
        up_ref, down_ref, wide_ref, out_ref = refs[count:]
        step = pl.program_id(0)

        def total(index):
            found = None
            for spot in groups[index]:
                value = refs[spot][...]
                value = value.reshape(value.shape[-2:]).astype(jnp.float32)
                found = value if found is None else found + value
            return found

        held = jnp.where(bits_ref[1 + pick] == 0, total(0), total(1)) + total(2)
        up_ref[...] = jnp.where(bits_ref[1 + near] == bits_ref[0], held, total(3))
        mine = jnp.concatenate([total(4), total(5)], axis=1)
        theirs = jnp.concatenate([total(6), total(7)], axis=1)
        down_ref[...] = jnp.where(step == bits_ref[0], mine, theirs)
        wide_ref[...] = jnp.where(step == 0, total(8), total(9))
        out_ref[...] = total(10)

    def share(sums, width):
        rows = sums.lists[0][0][0].shape[-2]
        return (
            jax.ShapeDtypeStruct((rows, width), jnp.float32),
            (rows, width // 2),
            lambda step, bits: (0, step),
        )

    return call(
        line,
        finish_kernel,
        (2,),
        ins,
        [share(up, up.columns), share(down, 4 * down.columns), share(first, 2 * first.columns), share(out, out.columns)],
        prefetch=True,
    )


def trade(sent, name, lone=None, first=False):
    if name == "core":
        return lax.ppermute(sent, "space", [(0, 1), (1, 0)])
    count = lax.axis_size("dp")
    if lone is None:
        return lax.ppermute(sent, "dp", [(i, i ^ (1 << name)) for i in range(count)])
    pairs = [
        (2 * i + core, 2 * (i ^ (1 << name)) + core)
        for i in range(count)
        for core in range(2)
        if (core == (i >> lone) & 1) != first
    ]
    return lax.ppermute(sent, BOTH, pairs)


def advance(line, bits, jobs, steps=2):
    for part, level in jobs:
        if len(part.lists) == 2 and part.level is None and not part.stacked:
            part.level = level
    sent = combine(line, bits, jobs, steps)
    for (part, level), value in zip(jobs, sent):
        if isinstance(level, tuple):
            part.lone = level[0]
            came = trade(value, level[0], level[0], True)
        else:
            came = trade(value, level, part.lone)
        arrived(part, level, came)


def arrived(part, level, came):
    dims = [name for name in part.left() if name != level]
    if not isinstance(level, tuple) and part.level != level:
        part.done.append(level)
    if part.stacked:
        for index in range(2):
            part.lists[index].append((came, [("at", index), *dims], 0))
    elif part.level is not None:
        part.more.append((came, dims, 0))
    else:
        part.lists[0].append((came, dims, 0))


def shards(
    tokens,
    cotangent,
    labels,
    sigma_index,
    fourier,
    class_table,
    w_time,
    w_map_up,
    w_map_down,
    map_gains,
    w_ada_attn,
    w_ada_ffn,
    w_qkv,
    head_scale,
    w_out,
    w_up,
    w_down,
):
    all_images, local_len, model_width = tokens.shape
    num_images = all_images // 2
    num_heads = head_scale.shape[0]
    head_dim = model_width // num_heads
    seq_len = 2 * local_len
    devices = lax.axis_size("dp") * lax.axis_size("space")
    core = lax.axis_index("space")

    def swap(value):
        return lax.ppermute(value, "space", [(0, 1), (1, 0)])

    def other_half(value):
        return swap(lax.dynamic_slice_in_dim(value, (1 - core) * num_images, num_images, axis=0))

    def tokens_half(value):
        return value.reshape(num_images, seq_len, -1)[:, local_len:]

    def split_images(value, came):
        kept = value.reshape(num_images, seq_len, -1)[:, :local_len]
        return jnp.where(
            core == 0,
            jnp.concatenate([kept, came], axis=0),
            jnp.concatenate([came, kept], axis=0),
        )

    levels = lax.axis_size("dp").bit_length() - 1
    dp = lax.axis_index("dp")
    bits = jnp.stack([core, *[(dp >> level) & 1 for level in range(levels)]]).astype(jnp.int32)
    every = [*reversed(range(levels))]
    low = list(range(levels - 2))
    swapped = [*reversed(low[:2]), *low[2:]]
    near, far = levels - 2, levels - 1

    tables = rope_tables(seq_len, num_heads, head_dim, GRID)
    cos, sin = [
        lax.dynamic_slice_in_dim(
            jnp.asarray(np.concatenate([table, table[:local_len]])), core * local_len, seq_len
        )
        for table in tables
    ]
    root = jnp.repeat(jnp.sqrt(head_scale.astype(jnp.float32)), head_dim)[None]
    all_cotangent = swap(cotangent)
    line = []
    scale_attn, scale_ffn, *map_saved = map_forward(
        line,
        labels,
        sigma_index,
        fourier,
        class_table,
        w_time,
        w_map_up,
        w_map_down,
        map_gains,
        w_ada_attn,
        w_ada_ffn,
    )
    normed, qkv, unit, tokens = project_qkv(
        line, bits, tokens, other_half(tokens), scale_attn, w_qkv, cos, sin, root
    )
    attended, inverse, mixed, normed_ffn, cotangent = attend(
        line, bits, qkv, tokens, scale_ffn, w_out, cotangent, all_cotangent
    )
    other_ffn = swap(normed_ffn)
    piece = low[-1]
    share = w_up.shape[1] // devices
    up_rest = [far, *reversed(low[1:-1]), "core"]
    down_all = [*every, "core"]

    def sums_of(own, sent, down):
        rows = down.shape[0] // 2 ** len(down_all)
        down = down.reshape(*([2] * len(down_all)), rows, down.shape[1])
        return (
            split(own, sent, low[0], up_rest),
            Sum([(down, down_all, 0)], down.shape[-1]),
        )

    *found, y_part, g_part = ffn(
        line, bits, 0, share, normed_ffn, other_ffn, cotangent, w_up, w_down
    )
    up0, down0 = sums_of(*found)
    *found, y_own, y_sent, g_own, g_sent = ffn(
        line,
        bits,
        1,
        share,
        normed_ffn,
        other_ffn,
        cotangent,
        w_up,
        w_down,
        (mixed, y_part, g_part),
    )
    g_came = swap(g_sent)
    up1, down1 = sums_of(*found)
    mid = low[1:-1]
    up = joined((up0, up1)).together()
    down = joined((down0, down1)).together()
    first_model = model_width // 2

    def then(*arrays):
        line.extend(arrays)

    def later(array):
        return lax.optimization_barrier((array, *line))[0]

    def step(*jobs):
        advance(line, bits, jobs)

    y_came = swap(y_sent)
    step((down, piece))
    then(up0.last())
    grad_mixed, grad_low, grad_att, grad_mod_ffn = mixed_backward(
        line, cotangent, mixed, g_own, g_came, scale_ffn, w_out
    )
    out = paired(weight_grad(line, grad_low, attended, model_width // devices, 512), every)
    grad_qkv, grad_scale = attention_backward(
        line, qkv, attended, inverse, grad_att, unit, cos, sin, root, num_images
    )
    for level in mid:
        step((up, level))
    then(y_came)
    step((up, (near,)), (down, low[0]))
    grad_tokens, grad_mod_attn = tokens_backward(
        line, grad_qkv, w_qkv, tokens, scale_attn, grad_mixed
    )
    tokens_came = swap(tokens_half(grad_tokens))
    columns = lax.all_to_all(
        map_backward(
            line,
            grad_mod_attn,
            grad_mod_ffn,
            grad_scale,
            map_saved,
            map_gains,
            w_map_up,
            w_map_down,
            w_ada_attn,
            w_ada_ffn,
            devices,
        ),
        BOTH,
        0,
        0,
        tiled=True,
    )
    for level in mid:
        step((down, level))
    step((down, near))
    wide = paired(weight_grad(line, grad_qkv, normed, 3 * model_width // devices, 768), every)
    first = columns_of(wide, 0, first_model)
    second = columns_of(wide, first_model, first_model)
    then(up.last(), tokens_came)
    (
        sum_class,
        sum_time,
        sum_map_up,
        sum_map_down,
        sum_gains,
        sum_ada_attn,
        sum_ada_ffn,
        sum_heads,
    ) = map_weights(
        line,
        columns,
        labels.shape[0],
        fourier,
        class_table,
        w_time,
        w_map_up,
        w_map_down,
        map_gains,
        model_width,
    )
    step((up.apart(), piece), (down, far))
    step((first, low[0]), (second, near), (out, piece))
    grad_tokens = split_images(later(grad_tokens), tokens_came)
    out_tokens = (later(y_own) + y_came.astype(jnp.float32)).astype(jnp.bfloat16)
    out_tokens = split_images(out_tokens, swap(tokens_half(out_tokens)))
    for level in mid:
        step((first, level), (second, level), (out, level))
    (down_sent,) = combine(line, bits, [(down, "core")], 2)
    step((first, piece), (second, low[0]), (out, low[0]), (up, far))
    down_came = swap(down_sent)
    down.done.append("core")
    step((first, near), (second, piece), (out, near))
    others = (first, second, out)
    *sent, up_sent = combine(line, bits, [(part, far) for part in others] + [(up, "core")], 2)
    for part, value in zip(others, sent):
        arrived(part, far, trade(value, far))
    came = [swap(up_sent), down_came]
    up.done.append("core")
    sum_up, sum_down, sum_qkv, sum_out = [
        total.T for total in finish(line, bits, near, up, down, first, second, out, came)
    ]
    return (
        out_tokens,
        grad_tokens,
        sum_class.T,
        sum_time.T,
        sum_map_up.T,
        sum_map_down.T,
        sum_gains,
        sum_ada_attn.T,
        sum_ada_ffn.T,
        sum_qkv,
        sum_heads[0],
        sum_out,
        sum_up,
        sum_down,
    )


def solution(mesh):
    placed = (
        P("dp", "space", None),
        P("dp", "space", None),
        P(("dp", "space")),
        P(("dp", "space")),
        P(),
        P(),
        P(),
        P(),
        P(),
        P(),
        P(),
        P(),
        P(),
        P(),
        P(),
        P(),
        P(),
    )
    return jax.shard_map(
        shards,
        mesh=mesh,
        in_specs=placed,
        out_specs=(
            P("dp", "space", None),
            P("dp", "space", None),
            P(None, ("dp", "space")),
            P(None, ("dp", "space")),
            P(None, ("dp", "space")),
            P(None, ("dp", "space")),
            P(None, ("dp", "space")),
            P(None, ("dp", "space")),
            P(None, ("dp", "space")),
            P(None, ("dp", "space")),
            P(),
            P(None, ("dp", "space")),
            P(None, ("dp", "space")),
            P(None, ("dp", "space")),
        ),
        check_vma=False,
    )
```

```python
import functools
import math

import jax
import jax.numpy as jnp
import numpy as np
from jax import lax
from jax.experimental import pallas as pl
from jax.experimental.pallas import tpu as pltpu
from jax.sharding import PartitionSpec as P

NSIG = 64
GRID = 16


EPSILON = 1e-06
BOTH = ("dp", "space")
LOG_LOW = math.log(0.01)
LOG_SPAN = math.log(10000.0)


def rope_tables(tokens, heads, head_dim, side):
    quarter = head_dim // 8
    order = np.arange(quarter)[None, :] * heads + np.arange(heads)[:, None]
    frequency = np.exp(math.log(math.pi) + math.log(10.0) * order / (heads * quarter))
    places = np.arange(tokens)
    row = -1.0 + (2.0 * (places // side) + 1.0) / side
    col = -1.0 + (2.0 * (places % side) + 1.0) / side
    angles = np.concatenate(
        [row[:, None, None] * frequency[None], col[:, None, None] * frequency[None]], axis=-1
    )
    cos, sin, flat = np.cos(angles), np.sin(angles), np.zeros_like(angles)
    tables = [
        np.concatenate([cos, cos, flat + 1.0, flat + 1.0], axis=-1),
        np.concatenate([-sin, sin, flat, flat], axis=-1),
    ]
    return [table.reshape(tokens, heads * head_dim).astype(np.float32) for table in tables]


VMEM_LIMIT = 60 * 1024 * 1024
NN = (((1,), (0,)), ((), ()))
NT = (((1,), (1,)), ((), ()))
TN = (((0,), (0,)), ((), ()))


def mm(left, right, dims=NN):
    return lax.dot_general(left, right, dims, preferred_element_type=jnp.float32)


SPARE = 12 * 1024 * 1024
SMALL = set()
HEAVY = {'attention_back_kernel': 1000000, 'tokens_kernel': 1000000, 'map_back_kernel': 1000000, 'map_weights_kernel': 1000000}


def call(line, body, grid, ins, outs, scratch=(), flops=0, moved=0, prefetch=False, spare=SPARE):
    arrays = [array for array, _, _ in ins]
    least = min(range(len(arrays)), key=lambda k: arrays[k].size)
    if line:
        arrays[least] = lax.optimization_barrier((arrays[least], *line))[0]
    in_specs = [
        pl.BlockSpec(memory_space=pltpu.SMEM) if block is None else pl.BlockSpec(block, where)
        for _, block, where in ins
    ]
    out_specs = [pl.BlockSpec(block, where) for _, block, where in outs]
    if prefetch:
        layout = {
            "grid_spec": pltpu.PrefetchScalarGridSpec(
                num_scalar_prefetch=1,
                grid=grid,
                in_specs=in_specs[1:],
                out_specs=out_specs,
                scratch_shapes=list(scratch),
            )
        }
    else:
        layout = {
            "grid": grid,
            "in_specs": in_specs,
            "out_specs": out_specs,
            "scratch_shapes": list(scratch),
        }
    blocks = [(array, block) for array, block, _ in [*ins, *outs] if block is not None]
    room = sum(math.prod(block) * array.dtype.itemsize for array, block in blocks)
    room = min(VMEM_LIMIT, 2 * room + sum(a.dtype.itemsize * math.prod(a.shape) for a in scratch) + spare)
    name = getattr(body, "func", body).__name__
    scale = HEAVY.get(name, 1)
    if name not in SMALL:
        room = VMEM_LIMIT
    flops, moved = flops // 1000 + 1, moved // 1000 + 1
    results = pl.pallas_call(
        body,
        name=name,
        out_shape=[shape for shape, _, _ in outs],
        compiler_params=pltpu.CompilerParams(
            dimension_semantics=("arbitrary",) * len(grid), vmem_limit_bytes=room
        ),
        cost_estimate=pl.CostEstimate(flops=flops * scale, bytes_accessed=moved * scale, transcendentals=0),
        **layout,
    )(*arrays)
    line[:] = [min(results, key=lambda result: result.size)]
    return results


def whole(array):
    return (array, array.shape, lambda *j: (0,) * array.ndim)


def fresh(shape, dtype=jnp.float32):
    return (jax.ShapeDtypeStruct(shape, dtype), shape, lambda *j: (0,) * len(shape))


def scalars(array):
    return (array, None, None)


def head_sums(values):
    lanes = values.shape[1]
    row = lax.broadcasted_iota(jnp.int32, (2 * lanes, lanes), 0) % lanes // (lanes // 2)
    col = lax.broadcasted_iota(jnp.int32, (2 * lanes, lanes), 1) // (lanes // 2)
    ones = jnp.where(row == col, 1.0, 0.0).astype(jnp.bfloat16)
    high = values.astype(jnp.bfloat16)
    rest = (values - high.astype(jnp.float32)).astype(jnp.bfloat16)
    return mm(jnp.concatenate([high, rest], axis=1), ones)


def rotate(values, cos, sin):
    lanes = values.shape[1]
    lane = lax.broadcasted_iota(jnp.int32, values.shape, 1)
    first = lane % (lanes // 2) < lanes // 8
    near = jnp.where(first, pltpu.roll(values, lanes - lanes // 8, 1), pltpu.roll(values, lanes // 8, 1))
    return values * cos + near * sin


def qkv_kernel(bits_ref, own_ref, came_ref, scale_ref, w_ref, cos_ref, sin_ref, root_ref, normed_ref, qkv_ref, unit_ref, both_ref):
    step = pl.program_id(0)
    count, seq = scale_ref.shape[0], cos_ref.shape[0]

    @pl.when(step == 0)
    def _():
        for image in range(count):
            rows = pl.ds(image * seq, seq)
            both = jnp.concatenate([own_ref[image], came_ref[image]], axis=0)
            both_ref[rows, :] = both
            tok = both.astype(jnp.float32)
            inverse = lax.rsqrt(jnp.mean(tok * tok, axis=-1, keepdims=True) + EPSILON)
            normed_ref[rows, :] = (tok * inverse * scale_ref[image]).astype(jnp.bfloat16)

    rotated = step < 2 * pl.num_programs(0) // 3

    @pl.when(rotated)
    def _():
        wide = mm(normed_ref[...], w_ref[...])
        for lane in range(0, w_ref.shape[1], 128):
            at = slice(lane, lane + 128)
            heads = wide[:, at]
            unit = root_ref[:, at] * lax.rsqrt(head_sums(heads * heads) + EPSILON)
            unit_ref[:, at] = unit
            heads = heads * unit
            for image in range(count):
                turned = rotate(heads[image * seq : image * seq + seq], cos_ref[:, at], sin_ref[:, at])
                qkv_ref[pl.ds(image * seq, seq), at] = turned.astype(jnp.bfloat16)

    @pl.when(jnp.logical_not(rotated))
    def _():
        qkv_ref[...] = mm(normed_ref[...], w_ref[...]).astype(jnp.bfloat16)


def project_qkv(line, bits, tokens, came, scale_attn, w_qkv, cos, sin, root):
    count, half, width = came.shape
    rows = count * half * 2
    total, block = w_qkv.shape[1], width
    steps = total // block
    turned = steps * 2 // 3
    per = width // block
    return call(
        line,
        qkv_kernel,
        (steps,),
        [
            scalars(bits),
            (tokens, (count, half, width), lambda j, bits: (bits[0], 0, 0)),
            whole(came),
            whole(scale_attn),
            (w_qkv, (width, block), lambda j, bits: (0, j)),
            (cos, (cos.shape[0], block), lambda j, bits: (0, j % per)),
            (sin, (sin.shape[0], block), lambda j, bits: (0, j % per)),
            (root, (1, block), lambda j, bits: (0, j % per)),
        ],
        [
            (jax.ShapeDtypeStruct((rows, width), jnp.bfloat16), (rows, width), lambda j, bits: (0, 0)),
            (jax.ShapeDtypeStruct((rows, total), jnp.bfloat16), (rows, block), lambda j, bits: (0, j)),
            (
                jax.ShapeDtypeStruct((rows, 2 * width), jnp.float32),
                (rows, block),
                lambda j, bits: (0, jnp.minimum(j, turned - 1)),
            ),
            fresh((rows, width), jnp.bfloat16),
        ],
        flops=2 * rows * width * total,
        moved=2 * width * total + 14 * rows * width,
        prefetch=True,
    )


def attention_kernel(
    bits_ref,
    q_ref,
    k_ref,
    v_ref,
    tok_ref,
    scale_ref,
    w_ref,
    own_ref,
    own_came_ref,
    other_ref,
    other_came_ref,
    att_ref,
    inv_ref,
    mixed_ref,
    nf_ref,
    cot_ref,
):
    cot_ref[0] = jnp.concatenate([own_ref[0], own_came_ref[0]], axis=0)
    cot_ref[1] = jnp.concatenate([other_came_ref[0], other_ref[0]], axis=0)
    seq, width = q_ref.shape
    left = lax.broadcasted_iota(jnp.int32, (seq, 128), 1) < 64
    for pair in range(width // 128):
        at = slice(pair * 128, pair * 128 + 128)
        queries, keys, values = q_ref[:, at], k_ref[:, at], v_ref[:, at]
        none, one = jnp.zeros_like(queries), jnp.ones_like(queries)
        weights0 = jnp.exp(mm(jnp.where(left, queries, none), keys, NT)).astype(jnp.bfloat16)
        weights1 = jnp.exp(mm(jnp.where(left, none, queries), keys, NT)).astype(jnp.bfloat16)
        both0 = mm(weights0, jnp.where(left, values, one))
        both1 = mm(weights1, jnp.where(left, one, values))
        totals = pltpu.roll(jnp.where(left, both1, both0), 64, 1)
        inverse = 1.0 / totals
        inv_ref[:, at] = inverse
        att_ref[:, at] = (jnp.where(left, both0, both1) * inverse).astype(jnp.bfloat16)
    mixed = tok_ref[...].astype(jnp.float32) + mm(att_ref[...], w_ref[...])
    mixed_ref[...] = mixed
    inverse = lax.rsqrt(jnp.mean(mixed * mixed, axis=-1, keepdims=True) + EPSILON)
    nf_ref[...] = (mixed * inverse * scale_ref[0]).astype(jnp.bfloat16)


def attend(line, bits, qkv, tokens, scale_ffn, w_out, cotangent, came):
    rows, width = tokens.shape
    images = scale_ffn.shape[0]
    seq = rows // images

    def part(index):
        return (qkv, (seq, width), lambda i, bits: (i, index))

    def result(dtype):
        return (jax.ShapeDtypeStruct((rows, width), dtype), (seq, width), lambda i, bits: (i, 0))

    return call(
        line,
        attention_kernel,
        (images,),
        [
            scalars(bits),
            part(0),
            part(1),
            part(2),
            (tokens, (seq, width), lambda i, bits: (i, 0)),
            (scale_ffn, (1, 1, width), lambda i, bits: (i, 0, 0)),
            whole(w_out),
            *[
                (array, (1, seq // 2, width), lambda i, bits, own=own: ((bits[0] if own else 1 - bits[0]) * images + i, 0, 0))
                for own in (True, False)
                for array in (cotangent, came)
            ],
        ],
        [
            result(jnp.bfloat16),
            result(jnp.float32),
            result(jnp.float32),
            result(jnp.bfloat16),
            (
                jax.ShapeDtypeStruct((2, rows, width), jnp.bfloat16),
                (2, seq, width),
                lambda i, bits: (0, i, 0),
            ),
        ],
        flops=2 * rows * width * width + 4 * rows * seq * width,
        moved=2 * width * width + 20 * rows * width,
        prefetch=True,
    )


def ffn_kernel(last, share, bits_ref, nf_ref, other_ref, cot_ref, wa_ref, wb_ref, wd_ref, *refs):
    if last:
        mixed_ref, y_in, g_in, *refs = refs
    up_own, *refs = refs
    if not last:
        up_sent, *refs = refs
    down_ref, *refs = refs
    if last:
        y_own, y_sent, g_own, g_sent, up_ref, y_ref, g_ref = refs
    else:
        y_out, g_out, up_ref, y_ref, g_ref = refs
    step, steps = pl.program_id(0), pl.num_programs(0)
    block = wa_ref.shape[1]
    rows, width = nf_ref.shape

    @pl.when(step == 0)
    def _():
        if last:
            y_ref[...] = y_in[...].astype(jnp.float32)
            g_ref[...] = g_in[...].astype(jnp.float32)
        else:
            y_ref[...] = jnp.zeros_like(y_ref)
            g_ref[...] = jnp.zeros_like(g_ref)

    size = 256
    found = []
    for side, inputs in enumerate((nf_ref, other_ref)):
        parts = []
        for start in range(0, rows, size):
            at = pl.ds(start, size)
            nf = inputs[at, :]
            value = mm(nf, wa_ref[...])
            gate = mm(nf, wb_ref[...])
            grad = mm(cot_ref[side, at, :], wd_ref[...], NT)
            bent, slope = gate_parts(gate)
            gated = (value * bent).astype(jnp.bfloat16)
            ga = (grad * bent).astype(jnp.bfloat16)
            gb = (grad * value * slope).astype(jnp.bfloat16)
            to = pl.ds(side * rows + start, size)
            y_ref[to, :] += mm(gated, wd_ref[...])
            g_ref[to, :] += mm(ga, wa_ref[...], NT) + mm(gb, wb_ref[...], NT)
            parts.append((ga, gb, gated))
        found.append([jnp.concatenate(part, axis=0) for part in zip(*parts)])
    for half in range(2):
        total = mm(found[0][half], nf_ref[...], TN) + mm(found[1][half], other_ref[...], TN)
        up_ref[half, pl.ds(pl.multiple_of(step * block, block), block), :] = total.astype(jnp.bfloat16)
    down = mm(cot_ref[0], found[0][2], TN) + mm(cot_ref[1], found[1][2], TN)
    down_ref[...] = down.astype(jnp.bfloat16)

    @pl.when(step == steps - 1)
    def _():
        own, other = bits_ref[1], 1 - bits_ref[1]
        group = 2 * share
        for half in range(2):
            if last:
                up_own[half] = up_ref[half]
                continue
            for index in range(up_ref.shape[1] // (2 * group)):
                at = pl.ds(index * group, group)
                for side, target in ((own, up_own), (other, up_sent)):
                    spot = pl.multiple_of(index * 2 * group + side * group, group)
                    target[half, at, :] = up_ref[half, pl.ds(spot, group), :]
        if last:
            y_own[...] = mixed_ref[...] + y_ref[:rows, :]
            y_sent[...] = y_ref[rows:, :].astype(jnp.bfloat16)
            g_own[...] = g_ref[:rows, :]
            g_sent[...] = g_ref[rows:, :].astype(jnp.bfloat16)
        else:
            y_out[...] = y_ref[...].astype(jnp.bfloat16)
            g_out[...] = g_ref[...].astype(jnp.bfloat16)


def ffn(line, bits, piece, share, nf, other, cot, w_up, w_down, before=None):
    rows, width = nf.shape
    hidden, block = w_down.shape[0], w_down.shape[0] // 4
    across = hidden // 4
    steps = across // block
    last = before is not None

    def place(base):
        return lambda j, bits: (0, base // block + bits[0] * 2 * steps + j)

    halved = ((2, across // 2, width), jnp.bfloat16)
    down = (
        jax.ShapeDtypeStruct((width, across), jnp.bfloat16),
        (width, block),
        lambda j, bits: (0, j),
    )
    low, wide = ((rows, width), jnp.bfloat16), ((rows, width), jnp.float32)
    both = ((2 * rows, width), jnp.bfloat16)
    return call(
        line,
        functools.partial(ffn_kernel, last, share),
        (steps,),
        [
            scalars(bits),
            whole(nf),
            whole(other),
            whole(cot),
            (w_up, (width, block), place(piece * across)),
            (w_up, (width, block), place(hidden + piece * across)),
            (
                w_down,
                (block, width),
                lambda j, bits: (bits[0] * 2 * steps + piece * steps + j, 0),
            ),
            *([whole(array) for array in before] if last else []),
        ],
        [
            *([fresh((2, across, width), jnp.bfloat16)] if last else [fresh(*halved), fresh(*halved)]),
            down,
            *([fresh(*wide), fresh(*low), fresh(*wide), fresh(*low)] if last else [fresh(*both), fresh(*both)]),
        ],
        scratch=[
            pltpu.VMEM((2, across, width), jnp.bfloat16),
            pltpu.VMEM((2 * rows, width), jnp.float32),
            pltpu.VMEM((2 * rows, width), jnp.float32),
        ],
        flops=36 * rows * width * across,
        moved=12 * width * across + 20 * rows * width,
        prefetch=True,
    )


def mixed_kernel(cot_ref, mixed_ref, gnf_ref, came_ref, scale_ref, w_ref, gm_ref, low_ref, gatt_ref, gmod_ref):
    mixed, scale = mixed_ref[...], scale_ref[0]
    inverse = lax.rsqrt(jnp.mean(mixed * mixed, axis=-1, keepdims=True) + EPSILON)
    grad = gnf_ref[...] + came_ref[...].astype(jnp.float32)
    unit = mixed * inverse
    gmod_ref[0] = jnp.sum(grad * unit, axis=0, keepdims=True)
    scaled = grad * scale
    mean = jnp.mean(scaled * unit, axis=-1, keepdims=True)
    total = cot_ref[0].astype(jnp.float32) + inverse * (scaled - unit * mean)
    gm_ref[...] = total
    low = total.astype(jnp.bfloat16)
    low_ref[...] = low
    gatt_ref[...] = mm(low, w_ref[...], NT).astype(jnp.bfloat16)


def mixed_backward(line, cot, mixed, grad_nf, came, scale_ffn, w_out):
    rows, width = mixed.shape
    images = scale_ffn.shape[0]
    seq = rows // images

    def own(array):
        return (array, (seq, width), lambda i: (i, 0))

    def result(dtype):
        return (jax.ShapeDtypeStruct((rows, width), dtype), (seq, width), lambda i: (i, 0))

    return call(
        line,
        mixed_kernel,
        (images,),
        [
            (cot, (1, seq, width), lambda i: (0, i, 0)),
            own(mixed),
            own(grad_nf),
            own(came),
            (scale_ffn, (1, 1, width), lambda i: (i, 0, 0)),
            (w_out, w_out.shape, lambda i: (0, 0)),
        ],
        [
            result(jnp.float32),
            result(jnp.bfloat16),
            result(jnp.bfloat16),
            (jax.ShapeDtypeStruct((images, 1, width), jnp.float32), (1, 1, width), lambda i: (i, 0, 0)),
        ],
        flops=2 * rows * width * width,
        moved=2 * width * width + 18 * rows * width,
    )


def attention_back_kernel(
    q_ref, k_ref, v_ref, att_ref, inv_ref, gatt_ref, uq_ref, uk_ref, cos_ref, sin_ref, root_ref, g_ref, gs_ref
):
    seq, width = q_ref.shape
    lane = lax.broadcasted_iota(jnp.int32, (seq, 128), 1)
    left = lane < 64

    @pl.when(pl.program_id(0) == 0)
    def _():
        gs_ref[...] = jnp.zeros_like(gs_ref)

    def own(mask, values):
        return jnp.where(mask, values, jnp.zeros_like(values))

    for pair in range(width // 128):
        at = slice(pair * 128, pair * 128 + 128)
        queries, keys, values = q_ref[:, at], k_ref[:, at], v_ref[:, at]
        grad = gatt_ref[:, at].astype(jnp.float32) * inv_ref[:, at]
        low = grad.astype(jnp.bfloat16)
        along = grad * att_ref[:, at].astype(jnp.float32)
        grads = [None, None, None]
        for head in range(2):
            mask = left if head == 0 else jnp.logical_not(left)
            delta = -jnp.sum(own(mask, along), axis=-1, keepdims=True)
            high = delta.astype(jnp.bfloat16).astype(jnp.float32)
            spot = 64 if head == 0 else 0
            extra = jnp.where(lane == spot, high, jnp.where(lane == spot + 1, delta - high, 0.0))
            ones = jnp.where((lane == spot) | (lane == spot + 1), 1.0, 0.0).astype(jnp.bfloat16)
            shifted = jnp.where(mask, low, extra.astype(jnp.bfloat16))
            weights = jnp.exp(mm(keys, own(mask, queries), NT))
            grad_scores = (weights * mm(jnp.where(mask, values, ones), shifted, NT)).astype(jnp.bfloat16)
            found = (
                mm(grad_scores, own(mask, keys), TN),
                mm(grad_scores, own(mask, queries)),
                mm(weights.astype(jnp.bfloat16), own(mask, low)),
            )
            grads = [new if old is None else old + new for old, new in zip(grads, found)]
        root = root_ref[:, at]
        for part, (turned, unit_ref) in enumerate(((queries, uq_ref), (keys, uk_ref))):
            grad_turned = grads[part]
            turned = turned.astype(jnp.float32)
            dots = head_sums(grad_turned * turned) / (root * root)
            gs_ref[:, at] += 0.5 * jnp.sum(dots, axis=0, keepdims=True)
            inner = rotate(grad_turned - turned * dots, cos_ref[:, at], -sin_ref[:, at])
            g_ref[:, part * width + pair * 128 : part * width + pair * 128 + 128] = (
                inner * unit_ref[:, at]
            ).astype(jnp.bfloat16)
        g_ref[:, 2 * width + pair * 128 : 2 * width + pair * 128 + 128] = grads[2].astype(jnp.bfloat16)


def attention_backward(line, qkv, attended, inverse, grad_att, unit, cos, sin, root, images):
    rows, width = attended.shape
    seq = rows // images

    def part(array, index):
        return (array, (seq, width), lambda i: (i, index))


    return call(
        line,
        attention_back_kernel,
        (images,),
        [
            part(qkv, 0),
            part(qkv, 1),
            part(qkv, 2),
            part(attended, 0),
            part(inverse, 0),
            part(grad_att, 0),
            part(unit, 0),
            part(unit, 1),
            whole(cos),
            whole(sin),
            whole(root),
        ],
        [
            (jax.ShapeDtypeStruct((rows, 3 * width), jnp.bfloat16), (seq, 3 * width), lambda i: (i, 0)),
            (jax.ShapeDtypeStruct((1, width), jnp.float32), (1, width), lambda i: (0, 0)),
        ],
        flops=10 * rows * seq * width,
        moved=30 * rows * width,
    )


def weight_kernel(bits_ref, grad_ref, inputs_ref, low_ref, attended_ref, own_ref, sent_ref):
    step, steps = pl.program_id(0), pl.num_programs(0)
    groups, _, width = own_ref.shape
    wide = (steps - 1) * grad_ref.shape[1] // (2 * groups)

    def store(total, at, start):
        rows = total.shape[0] // (2 * at.size)
        split = total.reshape(at.size, 2, rows, width)
        low, high = split[:, 0], split[:, 1]
        mine = bits_ref[0] == 0
        own_ref[at, start : start + rows, :] = jnp.where(mine, low, high).astype(jnp.bfloat16)
        sent_ref[at, start : start + rows, :] = jnp.where(mine, high, low).astype(jnp.bfloat16)

    @pl.when(step < steps - 1)
    def _():
        count = groups // (steps - 1)
        store(mm(grad_ref[...], inputs_ref[...], TN), pl.ds(step * count, count), 0)

    @pl.when(step == steps - 1)
    def _():
        store(mm(low_ref[...], attended_ref[...], TN), pl.ds(0, groups), wide)


def weight_grads(line, bits, groups, grad, inputs, low, attended):
    rows, width = inputs.shape
    total, block = grad.shape[1], 768
    steps = total // block
    share = (total + low.shape[1]) // (2 * groups)
    return call(
        line,
        weight_kernel,
        (steps + 1,),
        [
            scalars(bits),
            (grad, (rows, block), lambda j: (0, jnp.minimum(j, steps - 1))),
            whole(inputs),
            whole(low),
            whole(attended),
        ],
        [fresh((groups, share, width), jnp.bfloat16)] * 2,
        flops=2 * rows * width * total,
        moved=2 * (rows * total + rows * width + width * total),
    )


def tokens_kernel(g_ref, w_ref, tok_ref, scale_ref, gm_ref, out_ref, gmod_ref, total_ref):
    step, steps = pl.program_id(0), pl.num_programs(0)
    part = mm(g_ref[...], w_ref[...], NT)

    @pl.when(step == 0)
    def _():
        total_ref[...] = part

    @pl.when(step > 0)
    def _():
        total_ref[...] += part

    @pl.when(step == steps - 1)
    def _():
        images = scale_ref.shape[0]
        seq = tok_ref.shape[0] // images
        for image in range(images):
            at = pl.ds(image * seq, seq)
            tok = tok_ref[at, :].astype(jnp.float32)
            inverse = lax.rsqrt(jnp.mean(tok * tok, axis=-1, keepdims=True) + EPSILON)
            unit = tok * inverse
            grad = total_ref[at, :]
            gmod_ref[image] = jnp.sum(grad * unit, axis=0, keepdims=True)
            scaled = grad * scale_ref[image]
            mean = jnp.mean(scaled * unit, axis=-1, keepdims=True)
            out_ref[at, :] = gm_ref[at, :] + inverse * (scaled - unit * mean)


def tokens_backward(line, grad_qkv, w_qkv, tokens, scale_attn, grad_mixed):
    rows, width = tokens.shape
    total, block = w_qkv.shape[1], w_qkv.shape[1] // 2
    images = scale_attn.shape[0]


    return call(
        line,
        tokens_kernel,
        (total // block,),
        [
            (grad_qkv, (rows, block), lambda j: (0, j)),
            (w_qkv, (width, block), lambda j: (0, j)),
            whole(tokens),
            whole(scale_attn),
            whole(grad_mixed),
        ],
        [
            (jax.ShapeDtypeStruct((rows, width), jnp.float32), (rows, width), lambda j: (0, 0)),
            (jax.ShapeDtypeStruct((images, 1, width), jnp.float32), (images, 1, width), lambda j: (0, 0, 0)),
        ],
        scratch=[pltpu.VMEM((rows, width), jnp.float32)],
        flops=2 * rows * width * total,
        moved=2 * (rows * total + width * total) + 10 * rows * width,
    )


def norm_rows(values, gain):
    return values * lax.rsqrt(jnp.mean(values * values, axis=-1, keepdims=True) + EPSILON) * gain


def norm_back(values, gain, grad):
    inverse = lax.rsqrt(jnp.mean(values * values, axis=-1, keepdims=True) + EPSILON)
    unit = values * inverse
    scaled = grad * gain
    mean = jnp.mean(scaled * unit, axis=-1, keepdims=True)
    return inverse * (scaled - unit * mean), jnp.sum(grad * unit, axis=0, keepdims=True)


def gate_parts(gate):
    normal = 0.5 + 0.5 * lax.erf(gate * math.sqrt(0.5))
    density = jnp.exp(-0.5 * gate * gate) * (1.0 / math.sqrt(2.0 * math.pi))
    return gate * normal, normal + gate * density


def halves(value):
    high = value.astype(jnp.bfloat16)
    rest = (value - high.astype(jnp.float32)).astype(jnp.bfloat16)
    return jnp.concatenate([high, rest], axis=0)


def times(rows, weight, dims=NT):
    count = rows.shape[0]
    product = mm(halves(rows), weight, dims)
    return product[:count] + product[count:]


def outer(low_rows, rows):
    return mm(halves(rows), jnp.concatenate([low_rows, low_rows], axis=0), TN)


def first_rows(label, sigma, fourier_ref, table_ref, time_ref, gains_ref):
    level = (LOG_LOW + LOG_SPAN * sigma.astype(jnp.float32) / (NSIG - 1)) / 4.0
    angles = 2.0 * math.pi * level * fourier_ref[...]
    feats = jnp.concatenate([jnp.cos(angles), jnp.sin(angles)], axis=-1).astype(jnp.bfloat16)
    classes = lax.broadcasted_iota(jnp.int32, (label.shape[0], table_ref.shape[0]), 1)
    one_hot = jnp.where(classes == label, 1.0, 0.0).astype(jnp.bfloat16)
    start = mm(feats, time_ref[...]) + mm(one_hot, table_ref[...])
    first = norm_rows(start, gains_ref[0:1].astype(jnp.float32))
    hidden = norm_rows(first, gains_ref[1:2].astype(jnp.float32)).astype(jnp.bfloat16)
    return feats, one_hot, start, first, hidden


def map_kernel(
    label_ref,
    sigma_ref,
    fourier_ref,
    table_ref,
    time_ref,
    gains_ref,
    wa_ref,
    wb_ref,
    wd_ref,
    attn_ref,
    ffn_ref,
    scale_attn_ref,
    scale_ffn_ref,
    start_ref,
    first_ref,
    second_ref,
    up_ref,
    numbers_ref,
    hidden_ref,
):
    step = pl.program_id(0)
    count = scale_attn_ref.shape[0]

    @pl.when(step == 0)
    def _():
        row = lax.broadcasted_iota(jnp.int32, (8, 1), 0)
        label, sigma = jnp.zeros((8, 1), jnp.int32), jnp.zeros((8, 1), jnp.int32)
        for image in range(count):
            label = jnp.where(row == image, label_ref[image], label)
            sigma = jnp.where(row == image, sigma_ref[image], sigma)
        lane = lax.broadcasted_iota(jnp.int32, (8, 128), 1)
        numbers = jnp.where(lane == 0, label, jnp.where(lane == 1, sigma, 0))
        numbers_ref[...] = numbers.astype(jnp.float32)
        _, _, start, first, hidden = first_rows(
            label, sigma, fourier_ref, table_ref, time_ref, gains_ref
        )
        start_ref[...] = start
        first_ref[...] = first
        second_ref[...] = first
        hidden_ref[...] = hidden.astype(jnp.float32)

    hidden = hidden_ref[...].astype(jnp.bfloat16)
    value, gate = mm(hidden, wa_ref[...]), mm(hidden, wb_ref[...])
    up_ref[0] = value
    up_ref[1] = gate
    gated = (value * gate_parts(gate)[0]).astype(jnp.bfloat16)
    second_ref[...] += mm(gated, wd_ref[...])

    @pl.when(step == pl.num_programs(0) - 1)
    def _():
        cond = norm_rows(second_ref[...], gains_ref[2:3].astype(jnp.float32)).astype(jnp.bfloat16)
        for weight, scale_ref in ((attn_ref, scale_attn_ref), (ffn_ref, scale_ffn_ref)):
            scale = 1.0 + mm(cond, weight[...])
            for image in range(count):
                scale_ref[image] = scale[image : image + 1]


def hidden_blocks(w_map_up, w_map_down, block):
    width, steps = w_map_up.shape[0], w_map_down.shape[0] // block
    return [
        (w_map_up, (width, block), lambda j: (0, j)),
        (w_map_up, (width, block), lambda j: (0, steps + j)),
        (w_map_down, (block, width), lambda j: (j, 0)),
    ]


def map_forward(line, labels, sigma, fourier, table, w_time, w_up, w_down, gains, w_attn, w_ffn):
    images, width = labels.shape[0], w_time.shape[1]
    hidden, block, model = w_down.shape[0], 384, w_attn.shape[1]
    return call(
        line,
        map_kernel,
        (hidden // block,),
        [
            scalars(labels),
            scalars(sigma),
            whole(fourier[None]),
            whole(table),
            whole(w_time),
            whole(gains),
            *hidden_blocks(w_up, w_down, block),
            whole(w_attn),
            whole(w_ffn),
        ],
        [
            fresh((images, 1, model)),
            fresh((images, 1, model)),
            fresh((8, width)),
            fresh((8, width)),
            fresh((8, width)),
            (jax.ShapeDtypeStruct((2, 8, hidden), jnp.float32), (2, 8, block), lambda j: (0, 0, j)),
            fresh((8, 128)),
        ],
        scratch=[pltpu.VMEM((8, width), jnp.float32)],
        flops=16 * width * (3 * hidden + 2 * model),
        moved=2 * width * (3 * hidden + 2 * model + 1256),
    )


def map_back_kernel(
    gattn_ref,
    gffn_ref,
    heads_ref,
    numbers_ref,
    gains_ref,
    start_ref,
    first_ref,
    second_ref,
    up_ref,
    wa_ref,
    wb_ref,
    wd_ref,
    attn_ref,
    ffn_ref,
    sent_ref,
    gsecond_ref,
    gup_ref,
    ghidden_ref,
    gain_ref,
    rows_ref,
):
    step, steps = pl.program_id(0), pl.num_programs(0)
    count = gattn_ref.shape[0]
    block = wd_ref.shape[0]
    gains = gains_ref[...].astype(jnp.float32)

    @pl.when(step == 0)
    def _():
        rows_ref[...] = jnp.zeros_like(rows_ref)
        for image in range(count):
            rows_ref[0, image : image + 1] = gattn_ref[image]
            rows_ref[1, image : image + 1] = gffn_ref[image]
        grad = times(rows_ref[0], attn_ref[...]) + times(rows_ref[1], ffn_ref[...])
        gsecond, gain = norm_back(second_ref[...], gains[2:3], grad)
        gsecond_ref[...] = gsecond
        gain_ref[2:3] = gain
        ghidden_ref[...] = jnp.zeros_like(ghidden_ref)

    grad = times(gsecond_ref[...], wd_ref[...])
    bent, slope = gate_parts(up_ref[1])
    for part, (new, weight) in enumerate(((grad * bent, wa_ref), (grad * up_ref[0] * slope, wb_ref))):
        at = pl.multiple_of(step * block, block)
        gup_ref[part, :, pl.ds(at, block)] = new
        ghidden_ref[...] += times(new, weight[...])

    @pl.when(step == steps - 1)
    def _():
        gfirst, gain = norm_back(first_ref[...], gains[1:2], ghidden_ref[...])
        gain_ref[1:2] = gain
        gsecond = gsecond_ref[...]
        gstart, gain = norm_back(start_ref[...], gains[0:1], gfirst + gsecond)
        gain_ref[0:1] = gain
        model = heads_ref.shape[1]
        lane = lax.broadcasted_iota(jnp.int32, (model, 128), 1)
        row = lax.broadcasted_iota(jnp.int32, (model, 128), 0)
        pick = jnp.where(row == lane * 64, 1.0, 0.0).astype(jnp.bfloat16)
        heads = times(jnp.concatenate([heads_ref[...], jnp.zeros((7, model))], axis=0), pick, NN)
        sent_ref[...] = jnp.zeros_like(sent_ref)
        devices = sent_ref.shape[0]
        hidden = gup_ref.shape[2]
        for device in range(devices):
            spot = 0
            for values in (rows_ref[0], rows_ref[1], gsecond):
                width = values.shape[1] // devices
                sent_ref[device, 0:count, spot : spot + width] = values[
                    0:count, device * width : device * width + width
                ]
                spot += width
            width = 2 * hidden // devices
            part, at = divmod(device * width, hidden)
            sent_ref[device, 0:count, spot : spot + width] = gup_ref[part, 0:count, at : at + width]
            spot += width
            width = gstart.shape[1] // devices
            sent_ref[device, 0:count, spot : spot + width] = gstart[
                0:count, device * width : device * width + width
            ]
            for index in range(3):
                sent_ref[device, count : count + 1, index * width : index * width + width] = gain_ref[
                    index : index + 1, device * width : device * width + width
                ]
            sent_ref[device, count + 1 : 2 * count + 1, 0:128] = numbers_ref[0:count]
            used = model // 64
            sent_ref[device, count : count + 1, 3 * width : 3 * width + used] = heads[0:1, 0:used]


def map_backward(line, grad_attn, grad_ffn, heads, saved, gains, w_up, w_down, w_attn, w_ffn, devices):
    start, first, second, up, numbers = saved
    width, hidden, block = start.shape[1], w_down.shape[0], 384
    model = w_attn.shape[1]
    columns = -(-(2 * model + 2 * width + 2 * hidden) // devices // 128) * 128
    return call(
        line,
        map_back_kernel,
        (hidden // block,),
        [
            whole(grad_attn),
            whole(grad_ffn),
            whole(heads),
            whole(numbers),
            whole(gains),
            whole(start),
            whole(first),
            whole(second),
            (up, (2, 8, block), lambda j: (0, 0, j)),
            *hidden_blocks(w_up, w_down, block),
            whole(w_attn),
            whole(w_ffn),
        ],
        [fresh((devices, 8, columns))],
        scratch=[
            pltpu.VMEM((8, width), jnp.float32),
            pltpu.VMEM((2, 8, hidden), jnp.float32),
            pltpu.VMEM((8, width), jnp.float32),
            pltpu.VMEM((8, width), jnp.float32),
            pltpu.VMEM((2, 8, model), jnp.float32),
        ],
        flops=32 * width * (3 * hidden + 2 * model),
        moved=2 * width * (3 * hidden + 2 * model),
    )[0]


def map_weights_kernel(
    columns_ref,
    fourier_ref,
    table_ref,
    time_ref,
    gains_ref,
    wa_ref,
    wb_ref,
    wd_ref,
    class_ref,
    wtime_ref,
    wup_ref,
    wdown_ref,
    wgain_ref,
    wattn_ref,
    wffn_ref,
    heads_ref,
    hidden_ref,
    second_ref,
    number_rows,
    rows_ref,
):
    step = pl.program_id(0)
    devices, count = columns_ref.shape[0], rows_ref.shape[0] // columns_ref.shape[0]
    attn, ffn, second, up, start = (
        wattn_ref.shape[0],
        wffn_ref.shape[0],
        wdown_ref.shape[0],
        wup_ref.shape[0],
        class_ref.shape[0],
    )
    edges = [0]
    for width in (attn, ffn, second, up, start):
        edges.append(edges[-1] + width)

    def columns(index):
        return rows_ref[:, edges[index] : edges[index + 1]]

    @pl.when(step == 0)
    def _():
        extra = jnp.zeros((1, columns_ref.shape[2]), jnp.float32)
        for device in range(devices):
            at = slice(device * count, device * count + count)
            number_rows[at] = columns_ref[device, count + 1 : 2 * count + 1, 0:128]
            rows_ref[at] = columns_ref[device, 0:count]
            extra += columns_ref[device, count : count + 1]
        for index in range(3):
            wgain_ref[index : index + 1] = extra[:, index * start : index * start + start]
        heads_ref[...] = extra[:, 3 * start : 3 * start + heads_ref.shape[1]]
        numbers = number_rows[...].astype(jnp.int32)
        feats, one_hot, _, first, hidden = first_rows(
            numbers[:, 0:1], numbers[:, 1:2], fourier_ref, table_ref, time_ref, gains_ref
        )
        hidden_ref[...] = hidden
        second_ref[...] = first
        class_ref[...] = outer(one_hot, columns(4))
        wtime_ref[...] = outer(feats, columns(4))
        wup_ref[...] = outer(hidden, columns(3))

    hidden = hidden_ref[...]
    value, gate = mm(hidden, wa_ref[...]), mm(hidden, wb_ref[...])
    gated = (value * gate_parts(gate)[0]).astype(jnp.bfloat16)
    second_ref[...] += mm(gated, wd_ref[...])
    wdown_ref[...] = outer(gated, columns(2))

    @pl.when(step == pl.num_programs(0) - 1)
    def _():
        cond = norm_rows(second_ref[...], gains_ref[2:3].astype(jnp.float32)).astype(jnp.bfloat16)
        wattn_ref[...] = outer(cond, columns(0))
        wffn_ref[...] = outer(cond, columns(1))


def map_weights(line, columns, count, fourier, table, w_time, w_up, w_down, gains, model):
    devices = columns.shape[0]
    rows = devices * count
    width, hidden, block = w_time.shape[1], w_down.shape[0], 384
    own = width // devices
    return call(
        line,
        map_weights_kernel,
        (hidden // block,),
        [
            whole(columns),
            whole(fourier[None]),
            whole(table),
            whole(w_time),
            whole(gains),
            *hidden_blocks(w_up, w_down, block),
        ],
        [
            fresh((own, table.shape[0])),
            fresh((own, w_time.shape[0])),
            fresh((2 * hidden // devices, width)),
            (jax.ShapeDtypeStruct((own, hidden), jnp.float32), (own, block), lambda j: (0, j)),
            fresh((3, own)),
            fresh((model // devices, width)),
            fresh((model // devices, width)),
            fresh((1, model // 64)),
        ],
        scratch=[
            pltpu.VMEM((rows, width), jnp.bfloat16),
            pltpu.VMEM((rows, width), jnp.float32),
            pltpu.VMEM((rows, 128), jnp.float32),
            pltpu.VMEM((rows, columns.shape[2]), jnp.float32),
        ],
        flops=2 * rows * width * 4 * hidden,
        moved=2 * width * (3 * hidden + 1256) + 4 * width * 400,
    )


class Sum:
    def __init__(self, terms, columns, pair=None):
        self.lists = [terms] if pair is None else [pair[0].lists[0], pair[1].lists[0]]
        self.more = []
        self.level = None
        self.done = [] if pair is None else [*{*pair[0].done, *pair[1].done}]
        self.columns = columns
        self.lone = None if pair is None else pair[0].lone
        self.stacked = False

    def last(self):
        return self.lists[0][-1][0]

    def together(self):
        self.stacked = True
        return self

    def apart(self):
        self.stacked = False
        return self

    def dims(self):
        return self.lists[0][0][1]

    def left(self):
        return [name for name in self.dims() if name not in self.done]


def columns_of(part, start, count):
    return Sum([(array, dims, start) for array, dims, _ in part.lists[0]], count)


def split(own, sent, level, names, lone=None):
    came = trade(sent, level, lone)
    rows = own.size // own.shape[-1] // 2 ** len(names)
    shape = (*([2] * len(names)), rows, own.shape[-1])
    return Sum([(array.reshape(shape), names, 0) for array in (own, came)], own.shape[-1])


def lone_sum(sent, bit, names):
    came = trade(sent, bit, bit, True)
    rows = sent.size // sent.shape[-1] // 2 ** len(names)
    shape = (*([2] * len(names)), rows, sent.shape[-1])
    found = Sum([(array.reshape(shape), names, 0) for array in (sent, came)], sent.shape[-1])
    found.lone = bit
    return found


def joined(pair):
    return Sum(None, pair[0].columns, pair)


def combine(line, bits, jobs, steps):
    ins, outs, plan = [scalars(bits)], [], []

    def place(dims, fixed, column, width, block):
        def where(step, bits):
            spots = []
            for name in dims:
                if isinstance(name, tuple):
                    spots.append(name[1])
                elif name not in fixed:
                    spots.append(0)
                else:
                    spot = 0 if name == "core" else 1 + name
                    spots.append(bits[spot] if fixed[name] else 1 - bits[spot])
            return (*spots, 0, column // block + step)

        return where

    for part, level in jobs:
        block = part.columns // steps
        fixed = {name: True for name in part.done}
        pick = part.level
        whole_sum = isinstance(level, tuple)
        if level is not None and pick != level and not whole_sum:
            fixed[level] = False
        groups = []
        for terms in [*part.lists, part.more]:
            group = []
            for array, dims, column in terms:
                rows = array.shape[-2]
                shape = (
                    *[1 if name in fixed or isinstance(name, tuple) else 2 for name in dims],
                    rows,
                    block,
                )
                group.append(len(ins) - 1)
                ins.append((array, shape, place(dims, fixed, column, part.columns, block)))
            groups.append(group)
        dims = [name for name in part.dims() if name not in fixed]
        shape = (*[2 for _ in dims], rows, part.columns)
        if part.stacked:
            dims, shape = [("at", 0), *dims], (2, *shape)
        dtype = jnp.bfloat16 if level is not None else jnp.float32
        outs.append(
            (jax.ShapeDtypeStruct(shape, dtype), (*shape[:-1], block), place(dims, {}, 0, 0, block))
        )
        plan.append((groups, pick, pick is not None and pick == level, part.stacked))

    def combine_kernel(bits_ref, *refs):
        results = refs[len(ins) - 1 :]
        for (groups, pick, swap, both), result in zip(plan, results):

            def total(group):
                found = None
                for index in group:
                    value = refs[index][...].reshape(shape).astype(jnp.float32)
                    found = value if found is None else found + value
                return found

            shape = result.shape[1:] if both else result.shape
            if both:
                for index in range(2):
                    result[index] = total(groups[index]).astype(result.dtype)
                continue
            found = total(groups[0])
            if pick is not None:
                first = bits_ref[1 + pick] == (1 if swap else 0)
                found = jnp.where(first, found, total(groups[1]))
            if groups[-1]:
                found = found + total(groups[-1])
            result[...] = found.astype(result.dtype)

    moved = sum(array.size for array, _, _ in ins)
    return call(line, combine_kernel, (steps,), ins, outs, moved=moved, prefetch=True)


def finish(line, bits, near, up, down, first, second, across, came):
    ins, groups = [scalars(bits)], []

    def add(terms, done, block, moving):
        group = []
        for array, dims, column in terms:
            group.append(len(ins) - 1)
            shape = (*[1] * len(dims), array.shape[-2], block)

            def where(step, bits, dims=dims, column=column):
                spots = []
                for name in dims:
                    if isinstance(name, tuple):
                        spots.append(name[1])
                    else:
                        spots.append(bits[0] if name == "core" else bits[1 + name])
                return (*spots, 0, column // block + (step if moving else 0))

            ins.append((array, shape, where))
        groups.append(group)

    half = up.columns // 2
    add(up.lists[0], up.done, half, True)
    add(up.lists[1], up.done, half, True)
    add(up.more, up.done, half, True)
    add([(came[0], (), 0)], (), half, True)
    add(down.lists[0], down.done, down.columns, False)
    add(down.lists[1], down.done, down.columns, False)
    add([(came[1], (("at", 0),), 0)], (), down.columns, False)
    add([(came[1], (("at", 1),), 0)], (), down.columns, False)
    add(first.lists[0], first.done, first.columns, False)
    add(second.lists[0], second.done, second.columns, False)
    count = len(ins) - 1
    pick = up.level

    def finish_kernel(bits_ref, *refs):
        up_ref, down_ref, wide_ref, out_ref = refs[count:]
        step = pl.program_id(0)

        def total(index):
            found = None
            for spot in groups[index]:
                value = refs[spot][...]
                value = value.reshape(value.shape[-2:]).astype(jnp.float32)
                found = value if found is None else found + value
            return found

        held = jnp.where(bits_ref[1 + pick] == 0, total(0), total(1)) + total(2)
        up_ref[...] = jnp.where(bits_ref[1 + near] == bits_ref[0], held, total(3))
        mine = jnp.concatenate([total(4), total(5)], axis=1)
        theirs = jnp.concatenate([total(6), total(7)], axis=1)
        down_ref[...] = jnp.where(step == bits_ref[0], mine, theirs)
        both = jnp.where(step == 0, total(8), total(9))
        wide_ref[...] = both[:across]
        out_ref[...] = both[across:]

    def share(rows, width):
        return (
            jax.ShapeDtypeStruct((rows, width), jnp.float32),
            (rows, width // 2),
            lambda step, bits: (0, step),
        )

    return call(
        line,
        finish_kernel,
        (2,),
        ins,
        [
            share(up.lists[0][0][0].shape[-2], up.columns),
            share(down.lists[0][0][0].shape[-2], 4 * down.columns),
            share(across, 2 * first.columns),
            share(first.lists[0][0][0].shape[-2] - across, 2 * first.columns),
        ],
        prefetch=True,
    )


def trade(sent, name, lone=None, first=False):
    if name == "core":
        return lax.ppermute(sent, "space", [(0, 1), (1, 0)])
    count = lax.axis_size("dp")
    if lone is None:
        return lax.ppermute(sent, "dp", [(i, i ^ (1 << name)) for i in range(count)])
    pairs = [
        (2 * i + core, 2 * (i ^ (1 << name)) + core)
        for i in range(count)
        for core in range(2)
        if (core == (i >> lone) & 1) != first
    ]
    return lax.ppermute(sent, BOTH, pairs)


def advance(line, bits, jobs, steps=2):
    for part, level in jobs:
        if len(part.lists) == 2 and part.level is None and not part.stacked:
            part.level = level
    sent = combine(line, bits, jobs, steps)
    for (part, level), value in zip(jobs, sent):
        if isinstance(level, tuple):
            part.lone = level[0]
            came = trade(value, level[0], level[0], True)
        else:
            came = trade(value, level, part.lone)
        arrived(part, level, came)


def arrived(part, level, came):
    dims = [name for name in part.left() if name != level]
    if not isinstance(level, tuple) and part.level != level:
        part.done.append(level)
    if part.stacked:
        for index in range(2):
            part.lists[index].append((came, [("at", index), *dims], 0))
    elif part.level is not None:
        part.more.append((came, dims, 0))
    else:
        part.lists[0].append((came, dims, 0))


def shards(
    tokens,
    cotangent,
    labels,
    sigma_index,
    fourier,
    class_table,
    w_time,
    w_map_up,
    w_map_down,
    map_gains,
    w_ada_attn,
    w_ada_ffn,
    w_qkv,
    head_scale,
    w_out,
    w_up,
    w_down,
):
    all_images, local_len, model_width = tokens.shape
    num_images = all_images // 2
    num_heads = head_scale.shape[0]
    head_dim = model_width // num_heads
    seq_len = 2 * local_len
    devices = lax.axis_size("dp") * lax.axis_size("space")
    core = lax.axis_index("space")

    def swap(value):
        return lax.ppermute(value, "space", [(0, 1), (1, 0)])

    def other_half(value):
        return swap(lax.dynamic_slice_in_dim(value, (1 - core) * num_images, num_images, axis=0))

    def tokens_half(value):
        return value.reshape(num_images, seq_len, -1)[:, local_len:]

    def split_images(value, came):
        kept = value.reshape(num_images, seq_len, -1)[:, :local_len]
        return jnp.where(
            core == 0,
            jnp.concatenate([kept, came], axis=0),
            jnp.concatenate([came, kept], axis=0),
        )

    levels = lax.axis_size("dp").bit_length() - 1
    dp = lax.axis_index("dp")
    bits = jnp.stack([core, *[(dp >> level) & 1 for level in range(levels)]]).astype(jnp.int32)
    every = [*reversed(range(levels))]
    low = list(range(levels - 2))
    swapped = [*reversed(low[:2]), *low[2:]]
    near, far = levels - 2, levels - 1

    tables = rope_tables(seq_len, num_heads, head_dim, GRID)
    cos, sin = [
        lax.dynamic_slice_in_dim(
            jnp.asarray(np.concatenate([table, table[:local_len]])), core * local_len, seq_len
        )
        for table in tables
    ]
    root = jnp.repeat(jnp.sqrt(head_scale.astype(jnp.float32)), head_dim)[None]
    all_cotangent = swap(cotangent)
    line = []
    scale_attn, scale_ffn, *map_saved = map_forward(
        line,
        labels,
        sigma_index,
        fourier,
        class_table,
        w_time,
        w_map_up,
        w_map_down,
        map_gains,
        w_ada_attn,
        w_ada_ffn,
    )
    normed, qkv, unit, tokens = project_qkv(
        line, bits, tokens, other_half(tokens), scale_attn, w_qkv, cos, sin, root
    )
    attended, inverse, mixed, normed_ffn, cotangent = attend(
        line, bits, qkv, tokens, scale_ffn, w_out, cotangent, all_cotangent
    )
    other_ffn = swap(normed_ffn)
    piece = low[-1]
    share = w_up.shape[1] // devices
    up_rest = [far, *reversed(low[1:-1]), "core"]
    down_all = [*every, "core"]

    up_all = [far, *reversed(low[:-1]), "core"]

    def down_sum(down):
        rows = down.shape[0] // 2 ** len(down_all)
        down = down.reshape(*([2] * len(down_all)), rows, down.shape[1])
        return Sum([(down, down_all, 0)], down.shape[-1])

    own, sent, down0, y_part, g_part = ffn(
        line, bits, 0, share, normed_ffn, other_ffn, cotangent, w_up, w_down
    )
    up0 = split(own, sent, low[0], up_rest)
    sent, down1, y_own, y_sent, g_own, g_sent = ffn(
        line,
        bits,
        1,
        share,
        normed_ffn,
        other_ffn,
        cotangent,
        w_up,
        w_down,
        (mixed, y_part, g_part),
    )
    g_came = swap(g_sent)
    up1 = lone_sum(sent, near, up_all)
    mid = low[1:-1]
    down = joined((down_sum(down0), down_sum(down1))).together()
    first_model = model_width // 2

    def then(*arrays):
        line.extend(arrays)

    def later(array):
        return lax.optimization_barrier((array, *line))[0]

    def step(*jobs):
        advance(line, bits, jobs)

    y_came = swap(y_sent)
    step((down, piece))
    then(up0.last())
    grad_mixed, grad_low, grad_att, grad_mod_ffn = mixed_backward(
        line, cotangent, mixed, g_own, g_came, scale_ffn, w_out
    )
    grad_qkv, grad_scale = attention_backward(
        line, qkv, attended, inverse, grad_att, unit, cos, sin, root, num_images
    )
    step((up0, (near,)), (up1, low[0]), (down, low[0]))
    for level in mid:
        step((up0, level), (up1, level), (down, level))
    up = joined((up0, up1))
    groups = devices // 2
    own, sent = weight_grads(line, bits, groups, grad_qkv, normed, grad_low, attended)
    shape = (*([2] * levels), *own.shape[1:])
    terms = [(array.reshape(shape), every) for array in (own, swap(sent))]
    first, second = [
        Sum([(array, dims, start) for array, dims in terms], first_model)
        for start in (0, first_model)
    ]
    then(y_came)
    grad_tokens, grad_mod_attn = tokens_backward(
        line, grad_qkv, w_qkv, tokens, scale_attn, grad_mixed
    )
    step((first, piece), (second, near))
    step((up, piece), (down, near))
    tokens_came = swap(tokens_half(later(grad_tokens)))
    columns = lax.all_to_all(
        map_backward(
            line,
            grad_mod_attn,
            grad_mod_ffn,
            grad_scale,
            map_saved,
            map_gains,
            w_map_up,
            w_map_down,
            w_ada_attn,
            w_ada_ffn,
            devices,
        ),
        BOTH,
        0,
        0,
        tiled=True,
    )
    for level in mid:
        step((first, level), (second, level))
    then(tokens_came)
    step((first, near), (second, low[0]), (down, far))
    grad_tokens = split_images(later(grad_tokens), tokens_came)
    (
        sum_class,
        sum_time,
        sum_map_up,
        sum_map_down,
        sum_gains,
        sum_ada_attn,
        sum_ada_ffn,
        sum_heads,
    ) = map_weights(
        line,
        columns,
        labels.shape[0],
        fourier,
        class_table,
        w_time,
        w_map_up,
        w_map_down,
        map_gains,
        model_width,
    )
    step((first, low[0]), (second, piece), (up, far))
    out_tokens = (later(y_own) + y_came.astype(jnp.float32)).astype(jnp.bfloat16)
    out_came = swap(tokens_half(out_tokens))
    out_tokens = split_images(out_tokens, out_came)
    *sent, up_sent, down_sent = combine(
        line, bits, [(first, far), (second, far), (up, "core"), (down, "core")], 2
    )
    for part, value in zip((first, second), sent):
        arrived(part, far, trade(value, far))
    came = [swap(up_sent), swap(down_sent)]
    up.done.append("core")
    down.done.append("core")
    sum_up, sum_down, sum_qkv, sum_out = [
        total.T for total in finish(
            line, bits, near, up, down, first, second, 3 * model_width // devices, came
        )
    ]
    return (
        out_tokens,
        grad_tokens,
        sum_class.T,
        sum_time.T,
        sum_map_up.T,
        sum_map_down.T,
        sum_gains,
        sum_ada_attn.T,
        sum_ada_ffn.T,
        sum_qkv,
        sum_heads[0],
        sum_out,
        sum_up,
        sum_down,
    )


def solution(mesh):
    placed = (
        P("dp", "space", None),
        P("dp", "space", None),
        P(("dp", "space")),
        P(("dp", "space")),
        P(),
        P(),
        P(),
        P(),
        P(),
        P(),
        P(),
        P(),
        P(),
        P(),
        P(),
        P(),
        P(),
    )
    return jax.shard_map(
        shards,
        mesh=mesh,
        in_specs=placed,
        out_specs=(
            P("dp", "space", None),
            P("dp", "space", None),
            P(None, ("dp", "space")),
            P(None, ("dp", "space")),
            P(None, ("dp", "space")),
            P(None, ("dp", "space")),
            P(None, ("dp", "space")),
            P(None, ("dp", "space")),
            P(None, ("dp", "space")),
            P(None, ("dp", "space")),
            P(),
            P(None, ("dp", "space")),
            P(None, ("dp", "space")),
            P(None, ("dp", "space")),
        ),
        check_vma=False,
    )
```

```python
import functools
import math

import jax
import jax.numpy as jnp
import numpy as np
from jax import lax
from jax.experimental import pallas as pl
from jax.experimental.pallas import tpu as pltpu
from jax.sharding import PartitionSpec as P

NSIG = 64
GRID = 16


EPSILON = 1e-06
BOTH = ("dp", "space")
LOG_LOW = math.log(0.01)
LOG_SPAN = math.log(10000.0)


def rope_tables(tokens, heads, head_dim, side):
    quarter = head_dim // 8
    order = np.arange(quarter)[None, :] * heads + np.arange(heads)[:, None]
    frequency = np.exp(math.log(math.pi) + math.log(10.0) * order / (heads * quarter))
    places = np.arange(tokens)
    row = -1.0 + (2.0 * (places // side) + 1.0) / side
    col = -1.0 + (2.0 * (places % side) + 1.0) / side
    angles = np.concatenate(
        [row[:, None, None] * frequency[None], col[:, None, None] * frequency[None]], axis=-1
    )
    cos, sin, flat = np.cos(angles), np.sin(angles), np.zeros_like(angles)
    tables = [
        np.concatenate([cos, cos, flat + 1.0, flat + 1.0], axis=-1),
        np.concatenate([-sin, sin, flat, flat], axis=-1),
    ]
    return [table.reshape(tokens, heads * head_dim).astype(np.float32) for table in tables]


VMEM_LIMIT = 60 * 1024 * 1024
NN = (((1,), (0,)), ((), ()))
NT = (((1,), (1,)), ((), ()))
TN = (((0,), (0,)), ((), ()))


def mm(left, right, dims=NN):
    return lax.dot_general(left, right, dims, preferred_element_type=jnp.float32)


SPARE = 12 * 1024 * 1024
SMALL = set()
HEAVY = {'back_kernel': 1000000, 'tokens_kernel': 1000000, 'map_back_kernel': 1000000, 'map_weights_kernel': 1000000}


def call(line, body, grid, ins, outs, scratch=(), flops=0, moved=0, prefetch=False, spare=SPARE):
    arrays = [array for array, _, _ in ins]
    least = min(range(len(arrays)), key=lambda k: arrays[k].size)
    if line:
        arrays[least] = lax.optimization_barrier((arrays[least], *line))[0]
    in_specs = [
        pl.BlockSpec(memory_space=pltpu.SMEM) if block is None else pl.BlockSpec(block, where)
        for _, block, where in ins
    ]
    out_specs = [pl.BlockSpec(block, where) for _, block, where in outs]
    if prefetch:
        layout = {
            "grid_spec": pltpu.PrefetchScalarGridSpec(
                num_scalar_prefetch=1,
                grid=grid,
                in_specs=in_specs[1:],
                out_specs=out_specs,
                scratch_shapes=list(scratch),
            )
        }
    else:
        layout = {
            "grid": grid,
            "in_specs": in_specs,
            "out_specs": out_specs,
            "scratch_shapes": list(scratch),
        }
    blocks = [(array, block) for array, block, _ in [*ins, *outs] if block is not None]
    room = sum(math.prod(block) * array.dtype.itemsize for array, block in blocks)
    room = min(VMEM_LIMIT, 2 * room + sum(a.dtype.itemsize * math.prod(a.shape) for a in scratch) + spare)
    name = getattr(body, "func", body).__name__
    scale = HEAVY.get(name, 1)
    if name not in SMALL:
        room = VMEM_LIMIT
    flops, moved = flops // 1000 + 1, moved // 1000 + 1
    results = pl.pallas_call(
        body,
        name=name,
        out_shape=[shape for shape, _, _ in outs],
        compiler_params=pltpu.CompilerParams(
            dimension_semantics=("arbitrary",) * len(grid), vmem_limit_bytes=room
        ),
        cost_estimate=pl.CostEstimate(flops=flops * scale, bytes_accessed=moved * scale, transcendentals=0),
        **layout,
    )(*arrays)
    line[:] = [min(results, key=lambda result: result.size)]
    return results


def whole(array):
    return (array, array.shape, lambda *j: (0,) * array.ndim)


def fresh(shape, dtype=jnp.float32):
    return (jax.ShapeDtypeStruct(shape, dtype), shape, lambda *j: (0,) * len(shape))


def scalars(array):
    return (array, None, None)


def head_sums(values):
    lanes = values.shape[1]
    row = lax.broadcasted_iota(jnp.int32, (2 * lanes, lanes), 0) % lanes // (lanes // 2)
    col = lax.broadcasted_iota(jnp.int32, (2 * lanes, lanes), 1) // (lanes // 2)
    ones = jnp.where(row == col, 1.0, 0.0).astype(jnp.bfloat16)
    high = values.astype(jnp.bfloat16)
    rest = (values - high.astype(jnp.float32)).astype(jnp.bfloat16)
    return mm(jnp.concatenate([high, rest], axis=1), ones)


def rotate(values, cos, sin):
    lanes = values.shape[1]
    lane = lax.broadcasted_iota(jnp.int32, values.shape, 1)
    first = lane % (lanes // 2) < lanes // 8
    near = jnp.where(first, pltpu.roll(values, lanes - lanes // 8, 1), pltpu.roll(values, lanes // 8, 1))
    return values * cos + near * sin


def by_place(pair, at):
    return jnp.concatenate([pair[0][:, at], pair[1][:, at]], axis=0)


def table_blocks(table, block, column):
    half = table.shape[0] // 2
    return [
        (table, (half, block), lambda *grid: (grid[-1][0], column(*grid[:-1]))),
        (table, (half, block), lambda *grid: (1 - grid[-1][0], column(*grid[:-1]))),
    ]


def qkv_kernel(
    bits_ref, own_ref, came_ref, scale_ref, w_ref, cos_a, cos_b, sin_a, sin_b, root_ref, normed_ref, qkv_ref, unit_ref, both_ref
):
    step = pl.program_id(0)
    count, seq = scale_ref.shape[0], 2 * own_ref.shape[1]

    @pl.when(step == 0)
    def _():
        for image in range(count):
            rows = pl.ds(image * seq, seq)
            both = jnp.concatenate([own_ref[image], came_ref[image]], axis=0)
            both_ref[rows, :] = both
            tok = both.astype(jnp.float32)
            inverse = lax.rsqrt(jnp.mean(tok * tok, axis=-1, keepdims=True) + EPSILON)
            normed_ref[rows, :] = (tok * inverse * scale_ref[image]).astype(jnp.bfloat16)

    rotated = step < 2 * pl.num_programs(0) // 3

    @pl.when(rotated)
    def _():
        wide = mm(normed_ref[...], w_ref[...])
        for lane in range(0, w_ref.shape[1], 128):
            at = slice(lane, lane + 128)
            heads = wide[:, at]
            unit = root_ref[:, at] * lax.rsqrt(head_sums(heads * heads) + EPSILON)
            unit_ref[:, at] = unit
            heads = heads * unit
            cos, sin = by_place((cos_a, cos_b), at), by_place((sin_a, sin_b), at)
            for image in range(count):
                turned = rotate(heads[image * seq : image * seq + seq], cos, sin)
                qkv_ref[pl.ds(image * seq, seq), at] = turned.astype(jnp.bfloat16)

    @pl.when(jnp.logical_not(rotated))
    def _():
        qkv_ref[...] = mm(normed_ref[...], w_ref[...]).astype(jnp.bfloat16)


def project_qkv(line, bits, tokens, came, scale_attn, w_qkv, cos, sin, root):
    count, half, width = came.shape
    rows = count * half * 2
    total, block = w_qkv.shape[1], width
    steps = total // block
    turned = steps * 2 // 3
    per = width // block
    return call(
        line,
        qkv_kernel,
        (steps,),
        [
            scalars(bits),
            (tokens, (count, half, width), lambda j, bits: (bits[0], 0, 0)),
            whole(came),
            whole(scale_attn),
            (w_qkv, (width, block), lambda j, bits: (0, j)),
            *table_blocks(cos, block, lambda j: j % per),
            *table_blocks(sin, block, lambda j: j % per),
            (root, (1, block), lambda j, bits: (0, j % per)),
        ],
        [
            (jax.ShapeDtypeStruct((rows, width), jnp.bfloat16), (rows, width), lambda j, bits: (0, 0)),
            (jax.ShapeDtypeStruct((rows, total), jnp.bfloat16), (rows, block), lambda j, bits: (0, j)),
            (
                jax.ShapeDtypeStruct((rows, 2 * width), jnp.float32),
                (rows, block),
                lambda j, bits: (0, jnp.minimum(j, turned - 1)),
            ),
            fresh((rows, width), jnp.bfloat16),
        ],
        flops=2 * rows * width * total,
        moved=2 * width * total + 14 * rows * width,
        prefetch=True,
    )


def attention_kernel(
    bits_ref,
    q_ref,
    k_ref,
    v_ref,
    tok_ref,
    scale_ref,
    w_ref,
    own_ref,
    own_came_ref,
    other_ref,
    other_came_ref,
    att_ref,
    inv_ref,
    mixed_ref,
    nf_ref,
    cot_ref,
):
    part = pl.program_id(1)

    @pl.when(part == 0)
    def _():
        cot_ref[0] = jnp.concatenate([own_ref[0], own_came_ref[0]], axis=0)
        cot_ref[1] = jnp.concatenate([other_came_ref[0], other_ref[0]], axis=0)
        mixed_ref[...] = tok_ref[...].astype(jnp.float32)

    seq, width = q_ref.shape
    left = lax.broadcasted_iota(jnp.int32, (seq, 128), 1) < 64
    for pair in range(width // 128):
        at = slice(pair * 128, pair * 128 + 128)
        queries, keys, values = q_ref[:, at], k_ref[:, at], v_ref[:, at]
        none, one = jnp.zeros_like(queries), jnp.ones_like(queries)
        weights0 = jnp.exp(mm(jnp.where(left, queries, none), keys, NT)).astype(jnp.bfloat16)
        weights1 = jnp.exp(mm(jnp.where(left, none, queries), keys, NT)).astype(jnp.bfloat16)
        both0 = mm(weights0, jnp.where(left, values, one))
        both1 = mm(weights1, jnp.where(left, one, values))
        totals = pltpu.roll(jnp.where(left, both1, both0), 64, 1)
        inverse = 1.0 / totals
        inv_ref[:, at] = inverse
        att_ref[:, at] = (jnp.where(left, both0, both1) * inverse).astype(jnp.bfloat16)
    mixed = mixed_ref[...] + mm(att_ref[...], w_ref[...])
    mixed_ref[...] = mixed

    @pl.when(part == pl.num_programs(1) - 1)
    def _():
        inverse = lax.rsqrt(jnp.mean(mixed * mixed, axis=-1, keepdims=True) + EPSILON)
        nf_ref[...] = (mixed * inverse * scale_ref[0]).astype(jnp.bfloat16)


def attend(line, bits, qkv, tokens, scale_ffn, w_out, cotangent, came):
    rows, width = tokens.shape
    images = scale_ffn.shape[0]
    seq, parts = rows // images, 1
    block = width // parts

    def part(index):
        return (qkv, (seq, block), lambda i, h, bits: (i, index * parts + h))

    def result(dtype):
        return (jax.ShapeDtypeStruct((rows, width), dtype), (seq, width), lambda i, h, bits: (i, 0))

    def half(dtype):
        return (jax.ShapeDtypeStruct((rows, width), dtype), (seq, block), lambda i, h, bits: (i, h))

    return call(
        line,
        attention_kernel,
        (images, parts),
        [
            scalars(bits),
            part(0),
            part(1),
            part(2),
            (tokens, (seq, width), lambda i, h, bits: (i, 0)),
            (scale_ffn, (1, 1, width), lambda i, h, bits: (i, 0, 0)),
            (w_out, (block, width), lambda i, h, bits: (h, 0)),
            *[
                (array, (1, seq // 2, width), lambda i, h, bits, own=own: ((bits[0] if own else 1 - bits[0]) * images + i, 0, 0))
                for own in (True, False)
                for array in (cotangent, came)
            ],
        ],
        [
            half(jnp.bfloat16),
            half(jnp.float32),
            result(jnp.float32),
            result(jnp.bfloat16),
            (
                jax.ShapeDtypeStruct((2, rows, width), jnp.bfloat16),
                (2, seq, width),
                lambda i, h, bits: (0, i, 0),
            ),
        ],
        flops=2 * rows * width * width + 4 * rows * seq * width,
        moved=2 * width * width + 20 * rows * width,
        prefetch=True,
    )


def ffn_kernel(last, share, bits_ref, nf_ref, other_ref, cot_ref, wa_ref, wb_ref, wd_ref, *refs):
    if last:
        mixed_ref, y_in, g_in, *refs = refs
    up_own, *refs = refs
    if not last:
        up_sent, *refs = refs
    down_ref, *refs = refs
    if last:
        y_own, y_sent, g_own, g_sent, up_ref, y_ref, g_ref = refs
    else:
        y_out, g_out, up_ref, y_ref, g_ref = refs
    step, steps = pl.program_id(0), pl.num_programs(0)
    block = wa_ref.shape[1]
    rows, width = nf_ref.shape

    @pl.when(step == 0)
    def _():
        if last:
            y_ref[...] = y_in[...].astype(jnp.float32)
            g_ref[...] = g_in[...].astype(jnp.float32)
        else:
            y_ref[...] = jnp.zeros_like(y_ref)
            g_ref[...] = jnp.zeros_like(g_ref)

    size = 256
    found = []
    for side, inputs in enumerate((nf_ref, other_ref)):
        parts = []
        for start in range(0, rows, size):
            at = pl.ds(start, size)
            nf = inputs[at, :]
            value = mm(nf, wa_ref[...])
            gate = mm(nf, wb_ref[...])
            grad = mm(cot_ref[side, at, :], wd_ref[...], NT)
            bent, slope = gate_parts(gate)
            gated = (value * bent).astype(jnp.bfloat16)
            ga = (grad * bent).astype(jnp.bfloat16)
            gb = (grad * value * slope).astype(jnp.bfloat16)
            to = pl.ds(side * rows + start, size)
            y_ref[to, :] += mm(gated, wd_ref[...])
            g_ref[to, :] += mm(ga, wa_ref[...], NT) + mm(gb, wb_ref[...], NT)
            parts.append((ga, gb, gated))
        found.append([jnp.concatenate(part, axis=0) for part in zip(*parts)])
    for half in range(2):
        total = mm(found[0][half], nf_ref[...], TN) + mm(found[1][half], other_ref[...], TN)
        up_ref[half, pl.ds(pl.multiple_of(step * block, block), block), :] = total.astype(jnp.bfloat16)
    down = mm(cot_ref[0], found[0][2], TN) + mm(cot_ref[1], found[1][2], TN)
    down_ref[...] = down.astype(jnp.bfloat16)

    @pl.when(step == steps - 1)
    def _():
        own, other = bits_ref[1], 1 - bits_ref[1]
        group = 2 * share
        for half in range(2):
            if last:
                up_own[half] = up_ref[half]
                continue
            for index in range(up_ref.shape[1] // (2 * group)):
                at = pl.ds(index * group, group)
                for side, target in ((own, up_own), (other, up_sent)):
                    spot = pl.multiple_of(index * 2 * group + side * group, group)
                    target[half, at, :] = up_ref[half, pl.ds(spot, group), :]
        if last:
            y_own[...] = mixed_ref[...] + y_ref[:rows, :]
            y_sent[...] = y_ref[rows:, :].astype(jnp.bfloat16)
            g_own[...] = g_ref[:rows, :]
            g_sent[...] = g_ref[rows:, :].astype(jnp.bfloat16)
        else:
            y_out[...] = y_ref[...].astype(jnp.bfloat16)
            g_out[...] = g_ref[...].astype(jnp.bfloat16)


def ffn(line, bits, piece, share, nf, other, cot, w_up, w_down, before=None):
    rows, width = nf.shape
    hidden, block = w_down.shape[0], w_down.shape[0] // 4
    across = hidden // 4
    steps = across // block
    last = before is not None

    def place(base):
        return lambda j, bits: (0, base // block + bits[0] * 2 * steps + j)

    halved = ((2, across // 2, width), jnp.bfloat16)
    down = (
        jax.ShapeDtypeStruct((width, across), jnp.bfloat16),
        (width, block),
        lambda j, bits: (0, j),
    )
    low, wide = ((rows, width), jnp.bfloat16), ((rows, width), jnp.float32)
    both = ((2 * rows, width), jnp.bfloat16)
    return call(
        line,
        functools.partial(ffn_kernel, last, share),
        (steps,),
        [
            scalars(bits),
            whole(nf),
            whole(other),
            whole(cot),
            (w_up, (width, block), place(piece * across)),
            (w_up, (width, block), place(hidden + piece * across)),
            (
                w_down,
                (block, width),
                lambda j, bits: (bits[0] * 2 * steps + piece * steps + j, 0),
            ),
            *([whole(array) for array in before] if last else []),
        ],
        [
            *([fresh((2, across, width), jnp.bfloat16)] if last else [fresh(*halved), fresh(*halved)]),
            down,
            *([fresh(*wide), fresh(*low), fresh(*wide), fresh(*low)] if last else [fresh(*both), fresh(*both)]),
        ],
        scratch=[
            pltpu.VMEM((2, across, width), jnp.bfloat16),
            pltpu.VMEM((2 * rows, width), jnp.float32),
            pltpu.VMEM((2 * rows, width), jnp.float32),
        ],
        flops=36 * rows * width * across,
        moved=12 * width * across + 20 * rows * width,
        prefetch=True,
    )


def back_kernel(
    bits_ref,
    cot_ref,
    mixed_ref,
    gnf_ref,
    came_ref,
    scale_ref,
    w_ref,
    q_ref,
    k_ref,
    v_ref,
    att_ref,
    inv_ref,
    uq_ref,
    uk_ref,
    cos_a,
    cos_b,
    sin_a,
    sin_b,
    root_ref,
    gm_ref,
    low_ref,
    g_ref,
    gs_ref,
    gmod_ref,
    gatt_ref,
):
    image, part = pl.program_id(0), pl.program_id(1)
    seq, block = q_ref.shape
    width = gm_ref.shape[1]
    lane = lax.broadcasted_iota(jnp.int32, (seq, 128), 1)
    left = lane < 64

    @pl.when((image == 0) & (part == 0))
    def _():
        gs_ref[...] = jnp.zeros_like(gs_ref)

    @pl.when(part == 0)
    def _():
        mixed, scale = mixed_ref[...], scale_ref[0]
        inverse = lax.rsqrt(jnp.mean(mixed * mixed, axis=-1, keepdims=True) + EPSILON)
        grad = gnf_ref[...] + came_ref[...].astype(jnp.float32)
        unit = mixed * inverse
        gmod_ref[0] = jnp.sum(grad * unit, axis=0, keepdims=True)
        scaled = grad * scale
        mean = jnp.mean(scaled * unit, axis=-1, keepdims=True)
        total = cot_ref[0].astype(jnp.float32) + inverse * (scaled - unit * mean)
        gm_ref[...] = total
        low = total.astype(jnp.bfloat16)
        low_ref[...] = low
        gatt_ref[...] = mm(low, w_ref[...], NT).astype(jnp.bfloat16)

    def own(mask, values):
        return jnp.where(mask, values, jnp.zeros_like(values))

    for pair in range(block // 128):
        at = slice(pair * 128, pair * 128 + 128)
        start = part * block + pair * 128
        to = pl.ds(pl.multiple_of(start, 128), 128)
        queries, keys, values = q_ref[:, at], k_ref[:, at], v_ref[:, at]
        grad = gatt_ref[:, to].astype(jnp.float32) * inv_ref[:, at]
        low = grad.astype(jnp.bfloat16)
        along = grad * att_ref[:, at].astype(jnp.float32)
        grads = [None, None, None]
        for head in range(2):
            mask = left if head == 0 else jnp.logical_not(left)
            delta = -jnp.sum(own(mask, along), axis=-1, keepdims=True)
            high = delta.astype(jnp.bfloat16).astype(jnp.float32)
            spot = 64 if head == 0 else 0
            extra = jnp.where(lane == spot, high, jnp.where(lane == spot + 1, delta - high, 0.0))
            ones = jnp.where((lane == spot) | (lane == spot + 1), 1.0, 0.0).astype(jnp.bfloat16)
            shifted = jnp.where(mask, low, extra.astype(jnp.bfloat16))
            weights = jnp.exp(mm(keys, own(mask, queries), NT))
            grad_scores = (weights * mm(jnp.where(mask, values, ones), shifted, NT)).astype(jnp.bfloat16)
            found = (
                mm(grad_scores, own(mask, keys), TN),
                mm(grad_scores, own(mask, queries)),
                mm(weights.astype(jnp.bfloat16), own(mask, low)),
            )
            grads = [new if old is None else old + new for old, new in zip(grads, found)]
        root = root_ref[:, at]
        cos, sin = by_place((cos_a, cos_b), at), by_place((sin_a, sin_b), at)
        for index, (turned, unit_ref) in enumerate(((queries, uq_ref), (keys, uk_ref))):
            grad_turned = grads[index]
            turned = turned.astype(jnp.float32)
            dots = head_sums(grad_turned * turned) / (root * root)
            gs_ref[:, to] += 0.5 * jnp.sum(dots, axis=0, keepdims=True)
            inner = rotate(grad_turned - turned * dots, cos, -sin)
            spot = pl.ds(pl.multiple_of(index * width + start, 128), 128)
            g_ref[:, spot] = (inner * unit_ref[:, at]).astype(jnp.bfloat16)
        spot = pl.ds(pl.multiple_of(2 * width + start, 128), 128)
        g_ref[:, spot] = grads[2].astype(jnp.bfloat16)


def back(line, bits, cot, mixed, grad_nf, came, scale_ffn, w_out, qkv, attended, inverse, unit, cos, sin, root):
    rows, width = mixed.shape
    images, parts = scale_ffn.shape[0], 2
    seq, block = rows // images, width // parts

    def own(array):
        return (array, (seq, width), lambda i, h, bits: (i, 0))

    def half(array, index):
        return (array, (seq, block), lambda i, h, bits: (i, index * parts + h))

    def result(columns, dtype):
        shape = jax.ShapeDtypeStruct((rows, columns), dtype)
        return (shape, (seq, columns), lambda i, h, bits: (i, 0))

    each = (1, 1, width), lambda i, h, bits: (i, 0, 0)
    return call(
        line,
        back_kernel,
        (images, parts),
        [
            scalars(bits),
            (cot, (1, seq, width), lambda i, h, bits: (0, i, 0)),
            own(mixed),
            own(grad_nf),
            own(came),
            (scale_ffn, *each),
            whole(w_out),
            half(qkv, 0),
            half(qkv, 1),
            half(qkv, 2),
            half(attended, 0),
            half(inverse, 0),
            half(unit, 0),
            half(unit, 1),
            *table_blocks(cos, block, lambda i, h: h),
            *table_blocks(sin, block, lambda i, h: h),
            (root, (1, block), lambda i, h, bits: (0, h)),
        ],
        [
            result(width, jnp.float32),
            result(width, jnp.bfloat16),
            result(3 * width, jnp.bfloat16),
            fresh((1, width)),
            (jax.ShapeDtypeStruct((images, 1, width), jnp.float32), *each),
        ],
        scratch=[pltpu.VMEM((seq, width), jnp.bfloat16)],
        flops=2 * rows * width * width + 10 * rows * seq * width,
        moved=2 * width * width + 48 * rows * width,
        prefetch=True,
    )


def weight_kernel(bits_ref, grad_ref, inputs_ref, low_ref, attended_ref, own_ref, sent_ref):
    step, steps = pl.program_id(0), pl.num_programs(0)
    groups, _, width = own_ref.shape
    wide = (steps - 1) * grad_ref.shape[1] // (2 * groups)

    def store(total, at, start):
        rows = total.shape[0] // (2 * at.size)
        split = total.reshape(at.size, 2, rows, width)
        low, high = split[:, 0], split[:, 1]
        mine = bits_ref[0] == 0
        own_ref[at, start : start + rows, :] = jnp.where(mine, low, high).astype(jnp.bfloat16)
        sent_ref[at, start : start + rows, :] = jnp.where(mine, high, low).astype(jnp.bfloat16)

    @pl.when(step < steps - 1)
    def _():
        count = groups // (steps - 1)
        store(mm(grad_ref[...], inputs_ref[...], TN), pl.ds(step * count, count), 0)

    @pl.when(step == steps - 1)
    def _():
        store(mm(low_ref[...], attended_ref[...], TN), pl.ds(0, groups), wide)


def weight_grads(line, bits, groups, grad, inputs, low, attended):
    rows, width = inputs.shape
    total, block = grad.shape[1], 768
    steps = total // block
    share = (total + low.shape[1]) // (2 * groups)
    return call(
        line,
        weight_kernel,
        (steps + 1,),
        [
            scalars(bits),
            (grad, (rows, block), lambda j: (0, jnp.minimum(j, steps - 1))),
            whole(inputs),
            whole(low),
            whole(attended),
        ],
        [fresh((groups, share, width), jnp.bfloat16)] * 2,
        flops=2 * rows * width * total,
        moved=2 * (rows * total + rows * width + width * total),
    )


def tokens_kernel(g_ref, w_ref, tok_ref, scale_ref, gm_ref, out_ref, gmod_ref, total_ref):
    step, steps = pl.program_id(0), pl.num_programs(0)
    part = mm(g_ref[...], w_ref[...], NT)

    @pl.when(step == 0)
    def _():
        total_ref[...] = part

    @pl.when(step > 0)
    def _():
        total_ref[...] += part

    @pl.when(step == steps - 1)
    def _():
        images = scale_ref.shape[0]
        seq = tok_ref.shape[0] // images
        for image in range(images):
            at = pl.ds(image * seq, seq)
            tok = tok_ref[at, :].astype(jnp.float32)
            inverse = lax.rsqrt(jnp.mean(tok * tok, axis=-1, keepdims=True) + EPSILON)
            unit = tok * inverse
            grad = total_ref[at, :]
            gmod_ref[image] = jnp.sum(grad * unit, axis=0, keepdims=True)
            scaled = grad * scale_ref[image]
            mean = jnp.mean(scaled * unit, axis=-1, keepdims=True)
            out_ref[at, :] = gm_ref[at, :] + inverse * (scaled - unit * mean)


def tokens_backward(line, grad_qkv, w_qkv, tokens, scale_attn, grad_mixed):
    rows, width = tokens.shape
    total, block = w_qkv.shape[1], w_qkv.shape[1] // 2
    images = scale_attn.shape[0]


    return call(
        line,
        tokens_kernel,
        (total // block,),
        [
            (grad_qkv, (rows, block), lambda j: (0, j)),
            (w_qkv, (width, block), lambda j: (0, j)),
            whole(tokens),
            whole(scale_attn),
            whole(grad_mixed),
        ],
        [
            (jax.ShapeDtypeStruct((rows, width), jnp.float32), (rows, width), lambda j: (0, 0)),
            (jax.ShapeDtypeStruct((images, 1, width), jnp.float32), (images, 1, width), lambda j: (0, 0, 0)),
        ],
        scratch=[pltpu.VMEM((rows, width), jnp.float32)],
        flops=2 * rows * width * total,
        moved=2 * (rows * total + width * total) + 10 * rows * width,
    )


def norm_rows(values, gain):
    return values * lax.rsqrt(jnp.mean(values * values, axis=-1, keepdims=True) + EPSILON) * gain


def norm_back(values, gain, grad):
    inverse = lax.rsqrt(jnp.mean(values * values, axis=-1, keepdims=True) + EPSILON)
    unit = values * inverse
    scaled = grad * gain
    mean = jnp.mean(scaled * unit, axis=-1, keepdims=True)
    return inverse * (scaled - unit * mean), jnp.sum(grad * unit, axis=0, keepdims=True)


def gate_parts(gate):
    normal = 0.5 + 0.5 * lax.erf(gate * math.sqrt(0.5))
    density = jnp.exp(-0.5 * gate * gate) * (1.0 / math.sqrt(2.0 * math.pi))
    return gate * normal, normal + gate * density


def halves(value):
    high = value.astype(jnp.bfloat16)
    rest = (value - high.astype(jnp.float32)).astype(jnp.bfloat16)
    return jnp.concatenate([high, rest], axis=0)


def times(rows, weight, dims=NT):
    count = rows.shape[0]
    product = mm(halves(rows), weight, dims)
    return product[:count] + product[count:]


def outer(low_rows, rows):
    return mm(halves(rows), jnp.concatenate([low_rows, low_rows], axis=0), TN)


def first_rows(label, sigma, fourier_ref, table_ref, time_ref, gains_ref):
    level = (LOG_LOW + LOG_SPAN * sigma.astype(jnp.float32) / (NSIG - 1)) / 4.0
    angles = 2.0 * math.pi * level * fourier_ref[...]
    feats = jnp.concatenate([jnp.cos(angles), jnp.sin(angles)], axis=-1).astype(jnp.bfloat16)
    classes = lax.broadcasted_iota(jnp.int32, (label.shape[0], table_ref.shape[0]), 1)
    one_hot = jnp.where(classes == label, 1.0, 0.0).astype(jnp.bfloat16)
    start = mm(feats, time_ref[...]) + mm(one_hot, table_ref[...])
    first = norm_rows(start, gains_ref[0:1].astype(jnp.float32))
    hidden = norm_rows(first, gains_ref[1:2].astype(jnp.float32)).astype(jnp.bfloat16)
    return feats, one_hot, start, first, hidden


def map_kernel(
    label_ref,
    sigma_ref,
    fourier_ref,
    table_ref,
    time_ref,
    gains_ref,
    wa_ref,
    wb_ref,
    wd_ref,
    attn_ref,
    ffn_ref,
    scale_attn_ref,
    scale_ffn_ref,
    start_ref,
    first_ref,
    second_ref,
    up_ref,
    numbers_ref,
    hidden_ref,
):
    step = pl.program_id(0)
    count = scale_attn_ref.shape[0]

    @pl.when(step == 0)
    def _():
        row = lax.broadcasted_iota(jnp.int32, (8, 1), 0)
        label, sigma = jnp.zeros((8, 1), jnp.int32), jnp.zeros((8, 1), jnp.int32)
        for image in range(count):
            label = jnp.where(row == image, label_ref[image], label)
            sigma = jnp.where(row == image, sigma_ref[image], sigma)
        lane = lax.broadcasted_iota(jnp.int32, (8, 128), 1)
        numbers = jnp.where(lane == 0, label, jnp.where(lane == 1, sigma, 0))
        numbers_ref[...] = numbers.astype(jnp.float32)
        _, _, start, first, hidden = first_rows(
            label, sigma, fourier_ref, table_ref, time_ref, gains_ref
        )
        start_ref[...] = start
        first_ref[...] = first
        second_ref[...] = first
        hidden_ref[...] = hidden.astype(jnp.float32)

    hidden = hidden_ref[...].astype(jnp.bfloat16)
    value, gate = mm(hidden, wa_ref[...]), mm(hidden, wb_ref[...])
    up_ref[0] = value
    up_ref[1] = gate
    gated = (value * gate_parts(gate)[0]).astype(jnp.bfloat16)
    second_ref[...] += mm(gated, wd_ref[...])

    @pl.when(step == pl.num_programs(0) - 1)
    def _():
        cond = norm_rows(second_ref[...], gains_ref[2:3].astype(jnp.float32)).astype(jnp.bfloat16)
        for weight, scale_ref in ((attn_ref, scale_attn_ref), (ffn_ref, scale_ffn_ref)):
            scale = 1.0 + mm(cond, weight[...])
            for image in range(count):
                scale_ref[image] = scale[image : image + 1]


def hidden_blocks(w_map_up, w_map_down, block):
    width, steps = w_map_up.shape[0], w_map_down.shape[0] // block
    return [
        (w_map_up, (width, block), lambda j: (0, j)),
        (w_map_up, (width, block), lambda j: (0, steps + j)),
        (w_map_down, (block, width), lambda j: (j, 0)),
    ]


def map_forward(line, labels, sigma, fourier, table, w_time, w_up, w_down, gains, w_attn, w_ffn):
    images, width = labels.shape[0], w_time.shape[1]
    hidden, block, model = w_down.shape[0], 384, w_attn.shape[1]
    return call(
        line,
        map_kernel,
        (hidden // block,),
        [
            scalars(labels),
            scalars(sigma),
            whole(fourier[None]),
            whole(table),
            whole(w_time),
            whole(gains),
            *hidden_blocks(w_up, w_down, block),
            whole(w_attn),
            whole(w_ffn),
        ],
        [
            fresh((images, 1, model)),
            fresh((images, 1, model)),
            fresh((8, width)),
            fresh((8, width)),
            fresh((8, width)),
            (jax.ShapeDtypeStruct((2, 8, hidden), jnp.float32), (2, 8, block), lambda j: (0, 0, j)),
            fresh((8, 128)),
        ],
        scratch=[pltpu.VMEM((8, width), jnp.float32)],
        flops=16 * width * (3 * hidden + 2 * model),
        moved=2 * width * (3 * hidden + 2 * model + 1256),
    )


def map_back_kernel(
    gattn_ref,
    gffn_ref,
    heads_ref,
    numbers_ref,
    gains_ref,
    start_ref,
    first_ref,
    second_ref,
    up_ref,
    wa_ref,
    wb_ref,
    wd_ref,
    attn_ref,
    ffn_ref,
    sent_ref,
    gsecond_ref,
    gup_ref,
    ghidden_ref,
    gain_ref,
    rows_ref,
):
    step, steps = pl.program_id(0), pl.num_programs(0)
    count = gattn_ref.shape[0]
    block = wd_ref.shape[0]
    gains = gains_ref[...].astype(jnp.float32)

    @pl.when(step == 0)
    def _():
        rows_ref[...] = jnp.zeros_like(rows_ref)
        for image in range(count):
            rows_ref[0, image : image + 1] = gattn_ref[image]
            rows_ref[1, image : image + 1] = gffn_ref[image]
        grad = times(rows_ref[0], attn_ref[...]) + times(rows_ref[1], ffn_ref[...])
        gsecond, gain = norm_back(second_ref[...], gains[2:3], grad)
        gsecond_ref[...] = gsecond
        gain_ref[2:3] = gain
        ghidden_ref[...] = jnp.zeros_like(ghidden_ref)

    grad = times(gsecond_ref[...], wd_ref[...])
    bent, slope = gate_parts(up_ref[1])
    for part, (new, weight) in enumerate(((grad * bent, wa_ref), (grad * up_ref[0] * slope, wb_ref))):
        at = pl.multiple_of(step * block, block)
        gup_ref[part, :, pl.ds(at, block)] = new
        ghidden_ref[...] += times(new, weight[...])

    @pl.when(step == steps - 1)
    def _():
        gfirst, gain = norm_back(first_ref[...], gains[1:2], ghidden_ref[...])
        gain_ref[1:2] = gain
        gsecond = gsecond_ref[...]
        gstart, gain = norm_back(start_ref[...], gains[0:1], gfirst + gsecond)
        gain_ref[0:1] = gain
        model = heads_ref.shape[1]
        lane = lax.broadcasted_iota(jnp.int32, (model, 128), 1)
        row = lax.broadcasted_iota(jnp.int32, (model, 128), 0)
        pick = jnp.where(row == lane * 64, 1.0, 0.0).astype(jnp.bfloat16)
        heads = times(jnp.concatenate([heads_ref[...], jnp.zeros((7, model))], axis=0), pick, NN)
        sent_ref[...] = jnp.zeros_like(sent_ref)
        devices = sent_ref.shape[0]
        hidden = gup_ref.shape[2]
        for device in range(devices):
            spot = 0
            for values in (rows_ref[0], rows_ref[1], gsecond):
                width = values.shape[1] // devices
                sent_ref[device, 0:count, spot : spot + width] = values[
                    0:count, device * width : device * width + width
                ]
                spot += width
            width = 2 * hidden // devices
            part, at = divmod(device * width, hidden)
            sent_ref[device, 0:count, spot : spot + width] = gup_ref[part, 0:count, at : at + width]
            spot += width
            width = gstart.shape[1] // devices
            sent_ref[device, 0:count, spot : spot + width] = gstart[
                0:count, device * width : device * width + width
            ]
            for index in range(3):
                sent_ref[device, count : count + 1, index * width : index * width + width] = gain_ref[
                    index : index + 1, device * width : device * width + width
                ]
            sent_ref[device, count + 1 : 2 * count + 1, 0:128] = numbers_ref[0:count]
            used = model // 64
            sent_ref[device, count : count + 1, 3 * width : 3 * width + used] = heads[0:1, 0:used]


def map_backward(line, grad_attn, grad_ffn, heads, saved, gains, w_up, w_down, w_attn, w_ffn, devices):
    start, first, second, up, numbers = saved
    width, hidden, block = start.shape[1], w_down.shape[0], 384
    model = w_attn.shape[1]
    columns = -(-(2 * model + 2 * width + 2 * hidden) // devices // 128) * 128
    return call(
        line,
        map_back_kernel,
        (hidden // block,),
        [
            whole(grad_attn),
            whole(grad_ffn),
            whole(heads),
            whole(numbers),
            whole(gains),
            whole(start),
            whole(first),
            whole(second),
            (up, (2, 8, block), lambda j: (0, 0, j)),
            *hidden_blocks(w_up, w_down, block),
            whole(w_attn),
            whole(w_ffn),
        ],
        [fresh((devices, 8, columns))],
        scratch=[
            pltpu.VMEM((8, width), jnp.float32),
            pltpu.VMEM((2, 8, hidden), jnp.float32),
            pltpu.VMEM((8, width), jnp.float32),
            pltpu.VMEM((8, width), jnp.float32),
            pltpu.VMEM((2, 8, model), jnp.float32),
        ],
        flops=32 * width * (3 * hidden + 2 * model),
        moved=2 * width * (3 * hidden + 2 * model),
    )[0]


def map_weights_kernel(
    columns_ref,
    fourier_ref,
    table_ref,
    time_ref,
    gains_ref,
    wa_ref,
    wb_ref,
    wd_ref,
    class_ref,
    wtime_ref,
    wup_ref,
    wdown_ref,
    wgain_ref,
    wattn_ref,
    wffn_ref,
    heads_ref,
    hidden_ref,
    second_ref,
    number_rows,
    rows_ref,
):
    step = pl.program_id(0)
    devices, count = columns_ref.shape[0], rows_ref.shape[0] // columns_ref.shape[0]
    attn, ffn, second, up, start = (
        wattn_ref.shape[0],
        wffn_ref.shape[0],
        wdown_ref.shape[0],
        wup_ref.shape[0],
        class_ref.shape[0],
    )
    edges = [0]
    for width in (attn, ffn, second, up, start):
        edges.append(edges[-1] + width)

    def columns(index):
        return rows_ref[:, edges[index] : edges[index + 1]]

    @pl.when(step == 0)
    def _():
        extra = jnp.zeros((1, columns_ref.shape[2]), jnp.float32)
        for device in range(devices):
            at = slice(device * count, device * count + count)
            number_rows[at] = columns_ref[device, count + 1 : 2 * count + 1, 0:128]
            rows_ref[at] = columns_ref[device, 0:count]
            extra += columns_ref[device, count : count + 1]
        for index in range(3):
            wgain_ref[index : index + 1] = extra[:, index * start : index * start + start]
        heads_ref[...] = extra[:, 3 * start : 3 * start + heads_ref.shape[1]]
        numbers = number_rows[...].astype(jnp.int32)
        feats, one_hot, _, first, hidden = first_rows(
            numbers[:, 0:1], numbers[:, 1:2], fourier_ref, table_ref, time_ref, gains_ref
        )
        hidden_ref[...] = hidden
        second_ref[...] = first
        class_ref[...] = outer(one_hot, columns(4))
        wtime_ref[...] = outer(feats, columns(4))
        wup_ref[...] = outer(hidden, columns(3))

    hidden = hidden_ref[...]
    value, gate = mm(hidden, wa_ref[...]), mm(hidden, wb_ref[...])
    gated = (value * gate_parts(gate)[0]).astype(jnp.bfloat16)
    second_ref[...] += mm(gated, wd_ref[...])
    wdown_ref[...] = outer(gated, columns(2))

    @pl.when(step == pl.num_programs(0) - 1)
    def _():
        cond = norm_rows(second_ref[...], gains_ref[2:3].astype(jnp.float32)).astype(jnp.bfloat16)
        wattn_ref[...] = outer(cond, columns(0))
        wffn_ref[...] = outer(cond, columns(1))


def map_weights(line, columns, count, fourier, table, w_time, w_up, w_down, gains, model):
    devices = columns.shape[0]
    rows = devices * count
    width, hidden, block = w_time.shape[1], w_down.shape[0], 384
    own = width // devices
    return call(
        line,
        map_weights_kernel,
        (hidden // block,),
        [
            whole(columns),
            whole(fourier[None]),
            whole(table),
            whole(w_time),
            whole(gains),
            *hidden_blocks(w_up, w_down, block),
        ],
        [
            fresh((own, table.shape[0])),
            fresh((own, w_time.shape[0])),
            fresh((2 * hidden // devices, width)),
            (jax.ShapeDtypeStruct((own, hidden), jnp.float32), (own, block), lambda j: (0, j)),
            fresh((3, own)),
            fresh((model // devices, width)),
            fresh((model // devices, width)),
            fresh((1, model // 64)),
        ],
        scratch=[
            pltpu.VMEM((rows, width), jnp.bfloat16),
            pltpu.VMEM((rows, width), jnp.float32),
            pltpu.VMEM((rows, 128), jnp.float32),
            pltpu.VMEM((rows, columns.shape[2]), jnp.float32),
        ],
        flops=2 * rows * width * 4 * hidden,
        moved=2 * width * (3 * hidden + 1256) + 4 * width * 400,
    )


class Sum:
    def __init__(self, terms, columns, pair=None):
        self.lists = [terms] if pair is None else [pair[0].lists[0], pair[1].lists[0]]
        self.more = []
        self.level = None
        self.done = [] if pair is None else [*{*pair[0].done, *pair[1].done}]
        self.columns = columns
        self.lone = None if pair is None else pair[0].lone
        self.stacked = False

    def last(self):
        return self.lists[0][-1][0]

    def together(self):
        self.stacked = True
        return self

    def apart(self):
        self.stacked = False
        return self

    def dims(self):
        return self.lists[0][0][1]

    def left(self):
        return [name for name in self.dims() if name not in self.done]


def columns_of(part, start, count):
    return Sum([(array, dims, start) for array, dims, _ in part.lists[0]], count)


def split(own, sent, level, names, lone=None):
    came = trade(sent, level, lone)
    rows = own.size // own.shape[-1] // 2 ** len(names)
    shape = (*([2] * len(names)), rows, own.shape[-1])
    return Sum([(array.reshape(shape), names, 0) for array in (own, came)], own.shape[-1])


def lone_sum(sent, bit, names):
    came = trade(sent, bit, bit, True)
    rows = sent.size // sent.shape[-1] // 2 ** len(names)
    shape = (*([2] * len(names)), rows, sent.shape[-1])
    found = Sum([(array.reshape(shape), names, 0) for array in (sent, came)], sent.shape[-1])
    found.lone = bit
    return found


def joined(pair):
    return Sum(None, pair[0].columns, pair)


def combine(line, bits, jobs, steps):
    ins, outs, plan = [scalars(bits)], [], []

    def place(dims, fixed, column, width, block):
        def where(step, bits):
            spots = []
            for name in dims:
                if isinstance(name, tuple):
                    spots.append(name[1])
                elif name not in fixed:
                    spots.append(0)
                else:
                    spot = 0 if name == "core" else 1 + name
                    spots.append(bits[spot] if fixed[name] else 1 - bits[spot])
            return (*spots, 0, column // block + step)

        return where

    for part, level in jobs:
        block = part.columns // steps
        fixed = {name: True for name in part.done}
        pick = part.level
        whole_sum = isinstance(level, tuple)
        if level is not None and pick != level and not whole_sum:
            fixed[level] = False
        groups = []
        for terms in [*part.lists, part.more]:
            group = []
            for array, dims, column in terms:
                rows = array.shape[-2]
                shape = (
                    *[1 if name in fixed or isinstance(name, tuple) else 2 for name in dims],
                    rows,
                    block,
                )
                group.append(len(ins) - 1)
                ins.append((array, shape, place(dims, fixed, column, part.columns, block)))
            groups.append(group)
        dims = [name for name in part.dims() if name not in fixed]
        shape = (*[2 for _ in dims], rows, part.columns)
        if part.stacked:
            dims, shape = [("at", 0), *dims], (2, *shape)
        dtype = jnp.bfloat16 if level is not None else jnp.float32
        outs.append(
            (jax.ShapeDtypeStruct(shape, dtype), (*shape[:-1], block), place(dims, {}, 0, 0, block))
        )
        plan.append((groups, pick, pick is not None and pick == level, part.stacked))

    def combine_kernel(bits_ref, *refs):
        results = refs[len(ins) - 1 :]
        for (groups, pick, swap, both), result in zip(plan, results):

            def total(group):
                found = None
                for index in group:
                    value = refs[index][...].reshape(shape).astype(jnp.float32)
                    found = value if found is None else found + value
                return found

            shape = result.shape[1:] if both else result.shape
            if both:
                for index in range(2):
                    result[index] = total(groups[index]).astype(result.dtype)
                continue
            found = total(groups[0])
            if pick is not None:
                first = bits_ref[1 + pick] == (1 if swap else 0)
                found = jnp.where(first, found, total(groups[1]))
            if groups[-1]:
                found = found + total(groups[-1])
            result[...] = found.astype(result.dtype)

    moved = sum(array.size for array, _, _ in ins)
    return call(line, combine_kernel, (steps,), ins, outs, moved=moved, prefetch=True)


def finish(line, bits, near, up, down, first, second, across, came):
    ins, groups = [scalars(bits)], []

    def add(terms, done, block, moving):
        group = []
        for array, dims, column in terms:
            group.append(len(ins) - 1)
            shape = (*[1] * len(dims), array.shape[-2], block)

            def where(step, bits, dims=dims, column=column):
                spots = []
                for name in dims:
                    if isinstance(name, tuple):
                        spots.append(name[1])
                    else:
                        spots.append(bits[0] if name == "core" else bits[1 + name])
                return (*spots, 0, column // block + (step if moving else 0))

            ins.append((array, shape, where))
        groups.append(group)

    half = up.columns // 2
    add(up.lists[0], up.done, half, True)
    add(up.lists[1], up.done, half, True)
    add(up.more, up.done, half, True)
    add([(came[0], (), 0)], (), half, True)
    add(down.lists[0], down.done, down.columns, False)
    add(down.lists[1], down.done, down.columns, False)
    add([(came[1], (("at", 0),), 0)], (), down.columns, False)
    add([(came[1], (("at", 1),), 0)], (), down.columns, False)
    add(first.lists[0], first.done, first.columns, False)
    add(second.lists[0], second.done, second.columns, False)
    count = len(ins) - 1
    pick = up.level

    def finish_kernel(bits_ref, *refs):
        up_ref, down_ref, wide_ref, out_ref = refs[count:]
        step = pl.program_id(0)

        def total(index):
            found = None
            for spot in groups[index]:
                value = refs[spot][...]
                value = value.reshape(value.shape[-2:]).astype(jnp.float32)
                found = value if found is None else found + value
            return found

        held = jnp.where(bits_ref[1 + pick] == 0, total(0), total(1)) + total(2)
        up_ref[...] = jnp.where(bits_ref[1 + near] == bits_ref[0], held, total(3))
        mine = jnp.concatenate([total(4), total(5)], axis=1)
        theirs = jnp.concatenate([total(6), total(7)], axis=1)
        down_ref[...] = jnp.where(step == bits_ref[0], mine, theirs)
        both = jnp.where(step == 0, total(8), total(9))
        wide_ref[...] = both[:across]
        out_ref[...] = both[across:]

    def share(rows, width):
        return (
            jax.ShapeDtypeStruct((rows, width), jnp.float32),
            (rows, width // 2),
            lambda step, bits: (0, step),
        )

    return call(
        line,
        finish_kernel,
        (2,),
        ins,
        [
            share(up.lists[0][0][0].shape[-2], up.columns),
            share(down.lists[0][0][0].shape[-2], 4 * down.columns),
            share(across, 2 * first.columns),
            share(first.lists[0][0][0].shape[-2] - across, 2 * first.columns),
        ],
        prefetch=True,
    )


def trade(sent, name, lone=None, first=False):
    if name == "core":
        return lax.ppermute(sent, "space", [(0, 1), (1, 0)])
    count = lax.axis_size("dp")
    if lone is None:
        return lax.ppermute(sent, "dp", [(i, i ^ (1 << name)) for i in range(count)])
    pairs = [
        (2 * i + core, 2 * (i ^ (1 << name)) + core)
        for i in range(count)
        for core in range(2)
        if (core == (i >> lone) & 1) != first
    ]
    return lax.ppermute(sent, BOTH, pairs)


def advance(line, bits, jobs, steps=2):
    for part, level in jobs:
        if len(part.lists) == 2 and part.level is None and not part.stacked:
            part.level = level
    sent = combine(line, bits, jobs, steps)
    for (part, level), value in zip(jobs, sent):
        if isinstance(level, tuple):
            part.lone = level[0]
            came = trade(value, level[0], level[0], True)
        else:
            came = trade(value, level, part.lone)
        arrived(part, level, came)


def arrived(part, level, came):
    dims = [name for name in part.left() if name != level]
    if not isinstance(level, tuple) and part.level != level:
        part.done.append(level)
    if part.stacked:
        for index in range(2):
            part.lists[index].append((came, [("at", index), *dims], 0))
    elif part.level is not None:
        part.more.append((came, dims, 0))
    else:
        part.lists[0].append((came, dims, 0))


def shards(
    tokens,
    cotangent,
    labels,
    sigma_index,
    fourier,
    class_table,
    w_time,
    w_map_up,
    w_map_down,
    map_gains,
    w_ada_attn,
    w_ada_ffn,
    w_qkv,
    head_scale,
    w_out,
    w_up,
    w_down,
):
    all_images, local_len, model_width = tokens.shape
    num_images = all_images // 2
    num_heads = head_scale.shape[0]
    head_dim = model_width // num_heads
    seq_len = 2 * local_len
    devices = lax.axis_size("dp") * lax.axis_size("space")
    core = lax.axis_index("space")

    def swap(value):
        return lax.ppermute(value, "space", [(0, 1), (1, 0)])

    def other_half(value):
        return swap(lax.dynamic_slice_in_dim(value, (1 - core) * num_images, num_images, axis=0))

    def tokens_half(value):
        return value.reshape(num_images, seq_len, -1)[:, local_len:]

    def split_images(value, came):
        kept = value.reshape(num_images, seq_len, -1)[:, :local_len]
        return jnp.where(
            core == 0,
            jnp.concatenate([kept, came], axis=0),
            jnp.concatenate([came, kept], axis=0),
        )

    levels = lax.axis_size("dp").bit_length() - 1
    dp = lax.axis_index("dp")
    bits = jnp.stack([core, *[(dp >> level) & 1 for level in range(levels)]]).astype(jnp.int32)
    every = [*reversed(range(levels))]
    low = list(range(levels - 2))
    swapped = [*reversed(low[:2]), *low[2:]]
    near, far = levels - 2, levels - 1

    cos, sin = [jnp.asarray(table) for table in rope_tables(seq_len, num_heads, head_dim, GRID)]
    root = jnp.repeat(jnp.sqrt(head_scale.astype(jnp.float32)), head_dim)[None]
    all_cotangent = swap(cotangent)
    line = []
    scale_attn, scale_ffn, *map_saved = map_forward(
        line,
        labels,
        sigma_index,
        fourier,
        class_table,
        w_time,
        w_map_up,
        w_map_down,
        map_gains,
        w_ada_attn,
        w_ada_ffn,
    )
    normed, qkv, unit, tokens = project_qkv(
        line, bits, tokens, other_half(tokens), scale_attn, w_qkv, cos, sin, root
    )
    attended, inverse, mixed, normed_ffn, cotangent = attend(
        line, bits, qkv, tokens, scale_ffn, w_out, cotangent, all_cotangent
    )
    other_ffn = swap(normed_ffn)
    piece = low[-1]
    share = w_up.shape[1] // devices
    up_rest = [far, *reversed(low[1:-1]), "core"]
    down_all = [*every, "core"]

    up_all = [far, *reversed(low[:-1]), "core"]

    def down_sum(down):
        rows = down.shape[0] // 2 ** len(down_all)
        down = down.reshape(*([2] * len(down_all)), rows, down.shape[1])
        return Sum([(down, down_all, 0)], down.shape[-1])

    own, sent, down0, y_part, g_part = ffn(
        line, bits, 0, share, normed_ffn, other_ffn, cotangent, w_up, w_down
    )
    up0 = split(own, sent, low[0], up_rest)
    sent, down1, y_own, y_sent, g_own, g_sent = ffn(
        line,
        bits,
        1,
        share,
        normed_ffn,
        other_ffn,
        cotangent,
        w_up,
        w_down,
        (mixed, y_part, g_part),
    )
    g_came = swap(g_sent)
    up1 = lone_sum(sent, near, up_all)
    mid = low[1:-1]
    down = joined((down_sum(down0), down_sum(down1))).together()
    first_model = model_width // 2

    def then(*arrays):
        line.extend(arrays)

    def later(array):
        return lax.optimization_barrier((array, *line))[0]

    def step(*jobs):
        advance(line, bits, jobs)

    y_came = swap(y_sent)
    step((down, piece))
    then(up0.last())
    grad_mixed, grad_low, grad_qkv, grad_scale, grad_mod_ffn = back(
        line,
        bits,
        cotangent,
        mixed,
        g_own,
        g_came,
        scale_ffn,
        w_out,
        qkv,
        attended,
        inverse,
        unit,
        cos,
        sin,
        root,
    )
    groups = devices // 2
    own, sent = weight_grads(line, bits, groups, grad_qkv, normed, grad_low, attended)
    shape = (*([2] * levels), *own.shape[1:])
    terms = [(array.reshape(shape), every) for array in (own, swap(sent))]
    first, second = [
        Sum([(array, dims, start) for array, dims in terms], first_model)
        for start in (0, first_model)
    ]
    then(down.last())
    step((up0, (near,)), (up1, low[0]))
    for level in mid:
        step((up0, level), (up1, level), (down, level))
    up = joined((up0, up1))
    then(y_came)
    grad_tokens, grad_mod_attn = tokens_backward(
        line, grad_qkv, w_qkv, tokens, scale_attn, grad_mixed
    )
    tokens_came = swap(tokens_half(grad_tokens))
    step((first, piece), (second, near))
    then(tokens_came)
    step((up, piece), (down, low[0]))
    columns = lax.all_to_all(
        map_backward(
            line,
            grad_mod_attn,
            grad_mod_ffn,
            grad_scale,
            map_saved,
            map_gains,
            w_map_up,
            w_map_down,
            w_ada_attn,
            w_ada_ffn,
            devices,
        ),
        BOTH,
        0,
        0,
        tiled=True,
    )
    for level in mid:
        step((first, level), (second, level))
    step((first, near), (second, low[0]), (up, far), (down, near))
    (
        sum_class,
        sum_time,
        sum_map_up,
        sum_map_down,
        sum_gains,
        sum_ada_attn,
        sum_ada_ffn,
        sum_heads,
    ) = map_weights(
        line,
        columns,
        labels.shape[0],
        fourier,
        class_table,
        w_time,
        w_map_up,
        w_map_down,
        map_gains,
        model_width,
    )
    out_tokens = (later(y_own) + y_came.astype(jnp.float32)).astype(jnp.bfloat16)
    out_came = swap(tokens_half(out_tokens))
    out_tokens = split_images(out_tokens, out_came)
    step((first, low[0]), (second, piece), (down, far))
    grad_tokens = split_images(later(grad_tokens), tokens_came)
    *sent, up_sent, down_sent = combine(
        line, bits, [(first, far), (second, far), (up, "core"), (down, "core")], 2
    )
    for part, value in zip((first, second), sent):
        arrived(part, far, trade(value, far))
    came = [swap(up_sent), swap(down_sent)]
    up.done.append("core")
    down.done.append("core")
    sum_up, sum_down, sum_qkv, sum_out = [
        total.T for total in finish(
            line, bits, near, up, down, first, second, 3 * model_width // devices, came
        )
    ]
    return (
        out_tokens,
        grad_tokens,
        sum_class.T,
        sum_time.T,
        sum_map_up.T,
        sum_map_down.T,
        sum_gains,
        sum_ada_attn.T,
        sum_ada_ffn.T,
        sum_qkv,
        sum_heads[0],
        sum_out,
        sum_up,
        sum_down,
    )


def solution(mesh):
    placed = (
        P("dp", "space", None),
        P("dp", "space", None),
        P(("dp", "space")),
        P(("dp", "space")),
        P(),
        P(),
        P(),
        P(),
        P(),
        P(),
        P(),
        P(),
        P(),
        P(),
        P(),
        P(),
        P(),
    )
    return jax.shard_map(
        shards,
        mesh=mesh,
        in_specs=placed,
        out_specs=(
            P("dp", "space", None),
            P("dp", "space", None),
            P(None, ("dp", "space")),
            P(None, ("dp", "space")),
            P(None, ("dp", "space")),
            P(None, ("dp", "space")),
            P(None, ("dp", "space")),
            P(None, ("dp", "space")),
            P(None, ("dp", "space")),
            P(None, ("dp", "space")),
            P(),
            P(None, ("dp", "space")),
            P(None, ("dp", "space")),
            P(None, ("dp", "space")),
        ),
        check_vma=False,
    )
```

```python
import functools
import math

import jax
import jax.numpy as jnp
import numpy as np
from jax import lax
from jax.experimental import pallas as pl
from jax.experimental.pallas import tpu as pltpu
from jax.sharding import PartitionSpec as P

NSIG = 64
GRID = 16


EPSILON = 1e-06
BOTH = ("dp", "space")
LOG_LOW = math.log(0.01)
LOG_SPAN = math.log(10000.0)


def rope_tables(tokens, heads, head_dim, side):
    quarter = head_dim // 8
    order = np.arange(quarter)[None, :] * heads + np.arange(heads)[:, None]
    frequency = np.exp(math.log(math.pi) + math.log(10.0) * order / (heads * quarter))
    places = np.arange(tokens)
    row = -1.0 + (2.0 * (places // side) + 1.0) / side
    col = -1.0 + (2.0 * (places % side) + 1.0) / side
    angles = np.concatenate(
        [row[:, None, None] * frequency[None], col[:, None, None] * frequency[None]], axis=-1
    )
    cos, sin, flat = np.cos(angles), np.sin(angles), np.zeros_like(angles)
    tables = [
        np.concatenate([cos, cos, flat + 1.0, flat + 1.0], axis=-1),
        np.concatenate([-sin, sin, flat, flat], axis=-1),
    ]
    return [table.reshape(tokens, heads * head_dim).astype(np.float32) for table in tables]


VMEM_LIMIT = 60 * 1024 * 1024
NN = (((1,), (0,)), ((), ()))
NT = (((1,), (1,)), ((), ()))
TN = (((0,), (0,)), ((), ()))


def mm(left, right, dims=NN):
    return lax.dot_general(left, right, dims, preferred_element_type=jnp.float32)


SPARE = 12 * 1024 * 1024
SMALL = set()
HEAVY = {'back_kernel': 1000000, 'tokens_kernel': 1000000, 'map_back_kernel': 1000000, 'map_weights_kernel': 1000000}


def call(line, body, grid, ins, outs, scratch=(), flops=0, moved=0, prefetch=False, spare=SPARE):
    arrays = [array for array, _, _ in ins]
    least = min(range(len(arrays)), key=lambda k: arrays[k].size)
    if line:
        arrays[least] = lax.optimization_barrier((arrays[least], *line))[0]
    in_specs = [
        pl.BlockSpec(memory_space=pltpu.SMEM) if block is None else pl.BlockSpec(block, where)
        for _, block, where in ins
    ]
    out_specs = [pl.BlockSpec(block, where) for _, block, where in outs]
    if prefetch:
        layout = {
            "grid_spec": pltpu.PrefetchScalarGridSpec(
                num_scalar_prefetch=1,
                grid=grid,
                in_specs=in_specs[1:],
                out_specs=out_specs,
                scratch_shapes=list(scratch),
            )
        }
    else:
        layout = {
            "grid": grid,
            "in_specs": in_specs,
            "out_specs": out_specs,
            "scratch_shapes": list(scratch),
        }
    blocks = [(array, block) for array, block, _ in [*ins, *outs] if block is not None]
    room = sum(math.prod(block) * array.dtype.itemsize for array, block in blocks)
    room = min(VMEM_LIMIT, 2 * room + sum(a.dtype.itemsize * math.prod(a.shape) for a in scratch) + spare)
    name = getattr(body, "func", body).__name__
    scale = HEAVY.get(name, 1)
    if name not in SMALL:
        room = VMEM_LIMIT
    flops, moved = flops // 1000 + 1, moved // 1000 + 1
    results = pl.pallas_call(
        body,
        name=name,
        out_shape=[shape for shape, _, _ in outs],
        compiler_params=pltpu.CompilerParams(
            dimension_semantics=("arbitrary",) * len(grid), vmem_limit_bytes=room
        ),
        cost_estimate=pl.CostEstimate(flops=flops * scale, bytes_accessed=moved * scale, transcendentals=0),
        **layout,
    )(*arrays)
    line[:] = [min(results, key=lambda result: result.size)]
    return results


def whole(array):
    return (array, array.shape, lambda *j: (0,) * array.ndim)


def fresh(shape, dtype=jnp.float32):
    return (jax.ShapeDtypeStruct(shape, dtype), shape, lambda *j: (0,) * len(shape))


def scalars(array):
    return (array, None, None)


def head_sums(values):
    lanes = values.shape[1]
    row = lax.broadcasted_iota(jnp.int32, (2 * lanes, lanes), 0) % lanes // (lanes // 2)
    col = lax.broadcasted_iota(jnp.int32, (2 * lanes, lanes), 1) // (lanes // 2)
    ones = jnp.where(row == col, 1.0, 0.0).astype(jnp.bfloat16)
    high = values.astype(jnp.bfloat16)
    rest = (values - high.astype(jnp.float32)).astype(jnp.bfloat16)
    return mm(jnp.concatenate([high, rest], axis=1), ones)


def rotate(values, cos, sin):
    lanes = values.shape[1]
    lane = lax.broadcasted_iota(jnp.int32, values.shape, 1)
    first = lane % (lanes // 2) < lanes // 8
    near = jnp.where(first, pltpu.roll(values, lanes - lanes // 8, 1), pltpu.roll(values, lanes // 8, 1))
    return values * cos + near * sin


def by_place(pair, at):
    return jnp.concatenate([pair[0][:, at], pair[1][:, at]], axis=0)


def table_blocks(table, block, column):
    half = table.shape[0] // 2
    return [
        (table, (half, block), lambda *grid: (grid[-1][0], column(*grid[:-1]))),
        (table, (half, block), lambda *grid: (1 - grid[-1][0], column(*grid[:-1]))),
    ]


def qkv_kernel(
    bits_ref, own_ref, came_ref, scale_ref, w_ref, cos_a, cos_b, sin_a, sin_b, root_ref, normed_ref, qkv_ref, unit_ref, both_ref
):
    step = pl.program_id(0)
    count, seq = scale_ref.shape[0], 2 * own_ref.shape[1]

    @pl.when(step == 0)
    def _():
        for image in range(count):
            rows = pl.ds(image * seq, seq)
            both = jnp.concatenate([own_ref[image], came_ref[image]], axis=0)
            both_ref[rows, :] = both
            tok = both.astype(jnp.float32)
            inverse = lax.rsqrt(jnp.mean(tok * tok, axis=-1, keepdims=True) + EPSILON)
            normed_ref[rows, :] = (tok * inverse * scale_ref[image]).astype(jnp.bfloat16)

    rotated = step < 2 * pl.num_programs(0) // 3

    @pl.when(rotated)
    def _():
        wide = mm(normed_ref[...], w_ref[...])
        for lane in range(0, w_ref.shape[1], 128):
            at = slice(lane, lane + 128)
            heads = wide[:, at]
            unit = root_ref[:, at] * lax.rsqrt(head_sums(heads * heads) + EPSILON)
            unit_ref[:, at] = unit
            heads = heads * unit
            cos, sin = by_place((cos_a, cos_b), at), by_place((sin_a, sin_b), at)
            for image in range(count):
                turned = rotate(heads[image * seq : image * seq + seq], cos, sin)
                qkv_ref[pl.ds(image * seq, seq), at] = turned.astype(jnp.bfloat16)

    @pl.when(jnp.logical_not(rotated))
    def _():
        qkv_ref[...] = mm(normed_ref[...], w_ref[...]).astype(jnp.bfloat16)


def project_qkv(line, bits, tokens, came, scale_attn, w_qkv, cos, sin, root):
    count, half, width = came.shape
    rows = count * half * 2
    total, block = w_qkv.shape[1], width
    steps = total // block
    turned = steps * 2 // 3
    per = width // block
    return call(
        line,
        qkv_kernel,
        (steps,),
        [
            scalars(bits),
            (tokens, (count, half, width), lambda j, bits: (bits[0], 0, 0)),
            whole(came),
            whole(scale_attn),
            (w_qkv, (width, block), lambda j, bits: (0, j)),
            *table_blocks(cos, block, lambda j: j % per),
            *table_blocks(sin, block, lambda j: j % per),
            (root, (1, block), lambda j, bits: (0, j % per)),
        ],
        [
            (jax.ShapeDtypeStruct((rows, width), jnp.bfloat16), (rows, width), lambda j, bits: (0, 0)),
            (jax.ShapeDtypeStruct((rows, total), jnp.bfloat16), (rows, block), lambda j, bits: (0, j)),
            (
                jax.ShapeDtypeStruct((rows, 2 * width), jnp.float32),
                (rows, block),
                lambda j, bits: (0, jnp.minimum(j, turned - 1)),
            ),
            fresh((rows, width), jnp.bfloat16),
        ],
        flops=2 * rows * width * total,
        moved=2 * width * total + 14 * rows * width,
        prefetch=True,
    )


def attention_kernel(
    bits_ref,
    q_ref,
    k_ref,
    v_ref,
    tok_ref,
    scale_ref,
    w_ref,
    own_ref,
    own_came_ref,
    other_ref,
    other_came_ref,
    att_ref,
    inv_ref,
    mixed_ref,
    nf_ref,
    cot_ref,
):
    part = pl.program_id(1)

    @pl.when(part == 0)
    def _():
        cot_ref[0] = jnp.concatenate([own_ref[0], own_came_ref[0]], axis=0)
        cot_ref[1] = jnp.concatenate([other_came_ref[0], other_ref[0]], axis=0)
        mixed_ref[...] = tok_ref[...].astype(jnp.float32)

    seq, width = q_ref.shape
    left = lax.broadcasted_iota(jnp.int32, (seq, 128), 1) < 64
    for pair in range(width // 128):
        at = slice(pair * 128, pair * 128 + 128)
        queries, keys, values = q_ref[:, at], k_ref[:, at], v_ref[:, at]
        none, one = jnp.zeros_like(queries), jnp.ones_like(queries)
        weights0 = jnp.exp(mm(jnp.where(left, queries, none), keys, NT)).astype(jnp.bfloat16)
        weights1 = jnp.exp(mm(jnp.where(left, none, queries), keys, NT)).astype(jnp.bfloat16)
        both0 = mm(weights0, jnp.where(left, values, one))
        both1 = mm(weights1, jnp.where(left, one, values))
        totals = pltpu.roll(jnp.where(left, both1, both0), 64, 1)
        inverse = 1.0 / totals
        inv_ref[:, at] = inverse
        att_ref[:, at] = (jnp.where(left, both0, both1) * inverse).astype(jnp.bfloat16)
    mixed = mixed_ref[...] + mm(att_ref[...], w_ref[...])
    mixed_ref[...] = mixed

    @pl.when(part == pl.num_programs(1) - 1)
    def _():
        inverse = lax.rsqrt(jnp.mean(mixed * mixed, axis=-1, keepdims=True) + EPSILON)
        nf_ref[...] = (mixed * inverse * scale_ref[0]).astype(jnp.bfloat16)


def attend(line, bits, qkv, tokens, scale_ffn, w_out, cotangent, came):
    rows, width = tokens.shape
    images = scale_ffn.shape[0]
    seq, parts = rows // images, 1
    block = width // parts

    def part(index):
        return (qkv, (seq, block), lambda i, h, bits: (i, index * parts + h))

    def result(dtype):
        return (jax.ShapeDtypeStruct((rows, width), dtype), (seq, width), lambda i, h, bits: (i, 0))

    def half(dtype):
        return (jax.ShapeDtypeStruct((rows, width), dtype), (seq, block), lambda i, h, bits: (i, h))

    return call(
        line,
        attention_kernel,
        (images, parts),
        [
            scalars(bits),
            part(0),
            part(1),
            part(2),
            (tokens, (seq, width), lambda i, h, bits: (i, 0)),
            (scale_ffn, (1, 1, width), lambda i, h, bits: (i, 0, 0)),
            (w_out, (block, width), lambda i, h, bits: (h, 0)),
            *[
                (array, (1, seq // 2, width), lambda i, h, bits, own=own: ((bits[0] if own else 1 - bits[0]) * images + i, 0, 0))
                for own in (True, False)
                for array in (cotangent, came)
            ],
        ],
        [
            half(jnp.bfloat16),
            half(jnp.float32),
            result(jnp.float32),
            result(jnp.bfloat16),
            (
                jax.ShapeDtypeStruct((2, rows, width), jnp.bfloat16),
                (2, seq, width),
                lambda i, h, bits: (0, i, 0),
            ),
        ],
        flops=2 * rows * width * width + 4 * rows * seq * width,
        moved=2 * width * width + 20 * rows * width,
        prefetch=True,
    )


def ffn_kernel(last, share, bits_ref, nf_ref, other_ref, cot_ref, wa_ref, wb_ref, wd_ref, *refs):
    if last:
        mixed_ref, y_in, g_in, *refs = refs
    up_own, *refs = refs
    if not last:
        up_sent, *refs = refs
    down_ref, *refs = refs
    if last:
        y_own, y_sent, g_own, g_sent, up_ref, y_ref, g_ref = refs
    else:
        y_out, g_out, up_ref, y_ref, g_ref = refs
    step, steps = pl.program_id(0), pl.num_programs(0)
    block = wa_ref.shape[1]
    rows, width = nf_ref.shape

    @pl.when(step == 0)
    def _():
        if last:
            y_ref[...] = y_in[...].astype(jnp.float32)
            g_ref[...] = g_in[...].astype(jnp.float32)
        else:
            y_ref[...] = jnp.zeros_like(y_ref)
            g_ref[...] = jnp.zeros_like(g_ref)

    size = 256
    found = []
    for side, inputs in enumerate((nf_ref, other_ref)):
        parts = []
        for start in range(0, rows, size):
            at = pl.ds(start, size)
            nf = inputs[at, :]
            value = mm(nf, wa_ref[...])
            gate = mm(nf, wb_ref[...])
            grad = mm(cot_ref[side, at, :], wd_ref[...], NT)
            bent, slope = gate_parts(gate)
            gated = (value * bent).astype(jnp.bfloat16)
            ga = (grad * bent).astype(jnp.bfloat16)
            gb = (grad * value * slope).astype(jnp.bfloat16)
            to = pl.ds(side * rows + start, size)
            y_ref[to, :] += mm(gated, wd_ref[...])
            g_ref[to, :] += mm(ga, wa_ref[...], NT) + mm(gb, wb_ref[...], NT)
            parts.append((ga, gb, gated))
        found.append([jnp.concatenate(part, axis=0) for part in zip(*parts)])
    for half in range(2):
        total = mm(found[0][half], nf_ref[...], TN) + mm(found[1][half], other_ref[...], TN)
        up_ref[half, pl.ds(pl.multiple_of(step * block, block), block), :] = total.astype(jnp.bfloat16)
    down = mm(cot_ref[0], found[0][2], TN) + mm(cot_ref[1], found[1][2], TN)
    down_ref[...] = down.astype(jnp.bfloat16)

    @pl.when(step == steps - 1)
    def _():
        own, other = bits_ref[1], 1 - bits_ref[1]
        group = 2 * share
        for half in range(2):
            if last:
                up_own[half] = up_ref[half]
                continue
            for index in range(up_ref.shape[1] // (2 * group)):
                at = pl.ds(index * group, group)
                for side, target in ((own, up_own), (other, up_sent)):
                    spot = pl.multiple_of(index * 2 * group + side * group, group)
                    target[half, at, :] = up_ref[half, pl.ds(spot, group), :]
        if last:
            y_own[...] = mixed_ref[...] + y_ref[:rows, :]
            y_sent[...] = y_ref[rows:, :].astype(jnp.bfloat16)
            g_own[...] = g_ref[:rows, :]
            g_sent[...] = g_ref[rows:, :].astype(jnp.bfloat16)
        else:
            y_out[...] = y_ref[...].astype(jnp.bfloat16)
            g_out[...] = g_ref[...].astype(jnp.bfloat16)


def ffn(line, bits, piece, share, nf, other, cot, w_up, w_down, before=None):
    rows, width = nf.shape
    hidden, block = w_down.shape[0], w_down.shape[0] // 4
    across = hidden // 4
    steps = across // block
    last = before is not None

    def place(base):
        return lambda j, bits: (0, base // block + bits[0] * 2 * steps + j)

    halved = ((2, across // 2, width), jnp.bfloat16)
    down = (
        jax.ShapeDtypeStruct((width, across), jnp.bfloat16),
        (width, block),
        lambda j, bits: (0, j),
    )
    low, wide = ((rows, width), jnp.bfloat16), ((rows, width), jnp.float32)
    both = ((2 * rows, width), jnp.bfloat16)
    return call(
        line,
        functools.partial(ffn_kernel, last, share),
        (steps,),
        [
            scalars(bits),
            whole(nf),
            whole(other),
            whole(cot),
            (w_up, (width, block), place(piece * across)),
            (w_up, (width, block), place(hidden + piece * across)),
            (
                w_down,
                (block, width),
                lambda j, bits: (bits[0] * 2 * steps + piece * steps + j, 0),
            ),
            *([whole(array) for array in before] if last else []),
        ],
        [
            *([fresh((2, across, width), jnp.bfloat16)] if last else [fresh(*halved), fresh(*halved)]),
            down,
            *([fresh(*wide), fresh(*low), fresh(*wide), fresh(*low)] if last else [fresh(*both), fresh(*both)]),
        ],
        scratch=[
            pltpu.VMEM((2, across, width), jnp.bfloat16),
            pltpu.VMEM((2 * rows, width), jnp.float32),
            pltpu.VMEM((2 * rows, width), jnp.float32),
        ],
        flops=36 * rows * width * across,
        moved=12 * width * across + 20 * rows * width,
        prefetch=True,
    )


def back_kernel(
    bits_ref,
    cot_ref,
    mixed_ref,
    gnf_ref,
    came_ref,
    scale_ref,
    w_ref,
    q_ref,
    k_ref,
    v_ref,
    att_ref,
    inv_ref,
    uq_ref,
    uk_ref,
    cos_a,
    cos_b,
    sin_a,
    sin_b,
    root_ref,
    gm_ref,
    low_ref,
    g_ref,
    gs_ref,
    gmod_ref,
    gatt_ref,
):
    image, part = pl.program_id(0), pl.program_id(1)
    seq, block = q_ref.shape
    width = gm_ref.shape[1]
    lane = lax.broadcasted_iota(jnp.int32, (seq, 128), 1)
    left = lane < 64

    @pl.when((image == 0) & (part == 0))
    def _():
        gs_ref[...] = jnp.zeros_like(gs_ref)

    @pl.when(part == 0)
    def _():
        mixed, scale = mixed_ref[...], scale_ref[0]
        inverse = lax.rsqrt(jnp.mean(mixed * mixed, axis=-1, keepdims=True) + EPSILON)
        grad = gnf_ref[...] + came_ref[...].astype(jnp.float32)
        unit = mixed * inverse
        gmod_ref[0] = jnp.sum(grad * unit, axis=0, keepdims=True)
        scaled = grad * scale
        mean = jnp.mean(scaled * unit, axis=-1, keepdims=True)
        total = cot_ref[0].astype(jnp.float32) + inverse * (scaled - unit * mean)
        gm_ref[...] = total
        low = total.astype(jnp.bfloat16)
        low_ref[...] = low
        gatt_ref[...] = mm(low, w_ref[...], NT).astype(jnp.bfloat16)

    def own(mask, values):
        return jnp.where(mask, values, jnp.zeros_like(values))

    for pair in range(block // 128):
        at = slice(pair * 128, pair * 128 + 128)
        start = part * block + pair * 128
        to = pl.ds(pl.multiple_of(start, 128), 128)
        queries, keys, values = q_ref[:, at], k_ref[:, at], v_ref[:, at]
        grad = gatt_ref[:, to].astype(jnp.float32) * inv_ref[:, at]
        low = grad.astype(jnp.bfloat16)
        along = grad * att_ref[:, at].astype(jnp.float32)
        grads = [None, None, None]
        for head in range(2):
            mask = left if head == 0 else jnp.logical_not(left)
            delta = -jnp.sum(own(mask, along), axis=-1, keepdims=True)
            high = delta.astype(jnp.bfloat16).astype(jnp.float32)
            spot = 64 if head == 0 else 0
            extra = jnp.where(lane == spot, high, jnp.where(lane == spot + 1, delta - high, 0.0))
            ones = jnp.where((lane == spot) | (lane == spot + 1), 1.0, 0.0).astype(jnp.bfloat16)
            shifted = jnp.where(mask, low, extra.astype(jnp.bfloat16))
            weights = jnp.exp(mm(keys, own(mask, queries), NT))
            grad_scores = (weights * mm(jnp.where(mask, values, ones), shifted, NT)).astype(jnp.bfloat16)
            found = (
                mm(grad_scores, own(mask, keys), TN),
                mm(grad_scores, own(mask, queries)),
                mm(weights.astype(jnp.bfloat16), own(mask, low)),
            )
            grads = [new if old is None else old + new for old, new in zip(grads, found)]
        root = root_ref[:, at]
        cos, sin = by_place((cos_a, cos_b), at), by_place((sin_a, sin_b), at)
        for index, (turned, unit_ref) in enumerate(((queries, uq_ref), (keys, uk_ref))):
            grad_turned = grads[index]
            turned = turned.astype(jnp.float32)
            dots = head_sums(grad_turned * turned) / (root * root)
            gs_ref[:, to] += 0.5 * jnp.sum(dots, axis=0, keepdims=True)
            inner = rotate(grad_turned - turned * dots, cos, -sin)
            spot = pl.ds(pl.multiple_of(index * width + start, 128), 128)
            g_ref[:, spot] = (inner * unit_ref[:, at]).astype(jnp.bfloat16)
        spot = pl.ds(pl.multiple_of(2 * width + start, 128), 128)
        g_ref[:, spot] = grads[2].astype(jnp.bfloat16)


def back(line, bits, cot, mixed, grad_nf, came, scale_ffn, w_out, qkv, attended, inverse, unit, cos, sin, root):
    rows, width = mixed.shape
    images, parts = scale_ffn.shape[0], 2
    seq, block = rows // images, width // parts

    def own(array):
        return (array, (seq, width), lambda i, h, bits: (i, 0))

    def half(array, index):
        return (array, (seq, block), lambda i, h, bits: (i, index * parts + h))

    def result(columns, dtype):
        shape = jax.ShapeDtypeStruct((rows, columns), dtype)
        return (shape, (seq, columns), lambda i, h, bits: (i, 0))

    each = (1, 1, width), lambda i, h, bits: (i, 0, 0)
    return call(
        line,
        back_kernel,
        (images, parts),
        [
            scalars(bits),
            (cot, (1, seq, width), lambda i, h, bits: (0, i, 0)),
            own(mixed),
            own(grad_nf),
            own(came),
            (scale_ffn, *each),
            whole(w_out),
            half(qkv, 0),
            half(qkv, 1),
            half(qkv, 2),
            half(attended, 0),
            half(inverse, 0),
            half(unit, 0),
            half(unit, 1),
            *table_blocks(cos, block, lambda i, h: h),
            *table_blocks(sin, block, lambda i, h: h),
            (root, (1, block), lambda i, h, bits: (0, h)),
        ],
        [
            result(width, jnp.float32),
            result(width, jnp.bfloat16),
            result(3 * width, jnp.bfloat16),
            fresh((1, width)),
            (jax.ShapeDtypeStruct((images, 1, width), jnp.float32), *each),
        ],
        scratch=[pltpu.VMEM((seq, width), jnp.bfloat16)],
        flops=2 * rows * width * width + 10 * rows * seq * width,
        moved=2 * width * width + 48 * rows * width,
        prefetch=True,
    )


def weight_kernel(bits_ref, grad_ref, inputs_ref, low_ref, attended_ref, own_ref, sent_ref):
    step, steps = pl.program_id(0), pl.num_programs(0)
    groups, _, width = own_ref.shape
    wide = (steps - 1) * grad_ref.shape[1] // (2 * groups)

    def store(total, at, start):
        rows = total.shape[0] // (2 * at.size)
        split = total.reshape(at.size, 2, rows, width)
        low, high = split[:, 0], split[:, 1]
        mine = bits_ref[0] == 0
        own_ref[at, start : start + rows, :] = jnp.where(mine, low, high).astype(jnp.bfloat16)
        sent_ref[at, start : start + rows, :] = jnp.where(mine, high, low).astype(jnp.bfloat16)

    @pl.when(step < steps - 1)
    def _():
        count = groups // (steps - 1)
        store(mm(grad_ref[...], inputs_ref[...], TN), pl.ds(step * count, count), 0)

    @pl.when(step == steps - 1)
    def _():
        store(mm(low_ref[...], attended_ref[...], TN), pl.ds(0, groups), wide)


def weight_grads(line, bits, groups, grad, inputs, low, attended):
    rows, width = inputs.shape
    total, block = grad.shape[1], 768
    steps = total // block
    share = (total + low.shape[1]) // (2 * groups)
    return call(
        line,
        weight_kernel,
        (steps + 1,),
        [
            scalars(bits),
            (grad, (rows, block), lambda j: (0, jnp.minimum(j, steps - 1))),
            whole(inputs),
            whole(low),
            whole(attended),
        ],
        [fresh((groups, share, width), jnp.bfloat16)] * 2,
        flops=2 * rows * width * total,
        moved=2 * (rows * total + rows * width + width * total),
    )


def tokens_kernel(g_ref, w_ref, tok_ref, scale_ref, gm_ref, out_ref, gmod_ref, total_ref):
    step, steps = pl.program_id(0), pl.num_programs(0)
    part = mm(g_ref[...], w_ref[...], NT)

    @pl.when(step == 0)
    def _():
        total_ref[...] = part

    @pl.when(step > 0)
    def _():
        total_ref[...] += part

    @pl.when(step == steps - 1)
    def _():
        images = scale_ref.shape[0]
        seq = tok_ref.shape[0] // images
        for image in range(images):
            at = pl.ds(image * seq, seq)
            tok = tok_ref[at, :].astype(jnp.float32)
            inverse = lax.rsqrt(jnp.mean(tok * tok, axis=-1, keepdims=True) + EPSILON)
            unit = tok * inverse
            grad = total_ref[at, :]
            gmod_ref[image] = jnp.sum(grad * unit, axis=0, keepdims=True)
            scaled = grad * scale_ref[image]
            mean = jnp.mean(scaled * unit, axis=-1, keepdims=True)
            out_ref[at, :] = gm_ref[at, :] + inverse * (scaled - unit * mean)


def tokens_backward(line, grad_qkv, w_qkv, tokens, scale_attn, grad_mixed):
    rows, width = tokens.shape
    total, block = w_qkv.shape[1], w_qkv.shape[1] // 2
    images = scale_attn.shape[0]


    return call(
        line,
        tokens_kernel,
        (total // block,),
        [
            (grad_qkv, (rows, block), lambda j: (0, j)),
            (w_qkv, (width, block), lambda j: (0, j)),
            whole(tokens),
            whole(scale_attn),
            whole(grad_mixed),
        ],
        [
            (jax.ShapeDtypeStruct((rows, width), jnp.float32), (rows, width), lambda j: (0, 0)),
            (jax.ShapeDtypeStruct((images, 1, width), jnp.float32), (images, 1, width), lambda j: (0, 0, 0)),
        ],
        scratch=[pltpu.VMEM((rows, width), jnp.float32)],
        flops=2 * rows * width * total,
        moved=2 * (rows * total + width * total) + 10 * rows * width,
    )


def norm_rows(values, gain):
    return values * lax.rsqrt(jnp.mean(values * values, axis=-1, keepdims=True) + EPSILON) * gain


def norm_back(values, gain, grad):
    inverse = lax.rsqrt(jnp.mean(values * values, axis=-1, keepdims=True) + EPSILON)
    unit = values * inverse
    scaled = grad * gain
    mean = jnp.mean(scaled * unit, axis=-1, keepdims=True)
    return inverse * (scaled - unit * mean), jnp.sum(grad * unit, axis=0, keepdims=True)


def gate_parts(gate):
    normal = 0.5 + 0.5 * lax.erf(gate * math.sqrt(0.5))
    density = jnp.exp(-0.5 * gate * gate) * (1.0 / math.sqrt(2.0 * math.pi))
    return gate * normal, normal + gate * density


def halves(value):
    high = value.astype(jnp.bfloat16)
    rest = (value - high.astype(jnp.float32)).astype(jnp.bfloat16)
    return jnp.concatenate([high, rest], axis=0)


def times(rows, weight, dims=NT):
    count = rows.shape[0]
    product = mm(halves(rows), weight, dims)
    return product[:count] + product[count:]


def outer(low_rows, rows):
    return mm(halves(rows), jnp.concatenate([low_rows, low_rows], axis=0), TN)


def first_rows(label, sigma, fourier_ref, table_ref, time_ref, gains_ref):
    level = (LOG_LOW + LOG_SPAN * sigma.astype(jnp.float32) / (NSIG - 1)) / 4.0
    angles = 2.0 * math.pi * level * fourier_ref[...]
    feats = jnp.concatenate([jnp.cos(angles), jnp.sin(angles)], axis=-1).astype(jnp.bfloat16)
    classes = lax.broadcasted_iota(jnp.int32, (label.shape[0], table_ref.shape[0]), 1)
    one_hot = jnp.where(classes == label, 1.0, 0.0).astype(jnp.bfloat16)
    start = mm(feats, time_ref[...]) + mm(one_hot, table_ref[...])
    first = norm_rows(start, gains_ref[0:1].astype(jnp.float32))
    hidden = norm_rows(first, gains_ref[1:2].astype(jnp.float32)).astype(jnp.bfloat16)
    return feats, one_hot, start, first, hidden


def map_kernel(
    label_ref,
    sigma_ref,
    fourier_ref,
    table_ref,
    time_ref,
    gains_ref,
    wa_ref,
    wb_ref,
    wd_ref,
    attn_ref,
    ffn_ref,
    scale_attn_ref,
    scale_ffn_ref,
    start_ref,
    first_ref,
    second_ref,
    up_ref,
    numbers_ref,
    hidden_ref,
):
    step = pl.program_id(0)
    count = scale_attn_ref.shape[0]

    @pl.when(step == 0)
    def _():
        row = lax.broadcasted_iota(jnp.int32, (8, 1), 0)
        label, sigma = jnp.zeros((8, 1), jnp.int32), jnp.zeros((8, 1), jnp.int32)
        for image in range(count):
            label = jnp.where(row == image, label_ref[image], label)
            sigma = jnp.where(row == image, sigma_ref[image], sigma)
        lane = lax.broadcasted_iota(jnp.int32, (8, 128), 1)
        numbers = jnp.where(lane == 0, label, jnp.where(lane == 1, sigma, 0))
        numbers_ref[...] = numbers.astype(jnp.float32)
        _, _, start, first, hidden = first_rows(
            label, sigma, fourier_ref, table_ref, time_ref, gains_ref
        )
        start_ref[...] = start
        first_ref[...] = first
        second_ref[...] = first
        hidden_ref[...] = hidden.astype(jnp.float32)

    hidden = hidden_ref[...].astype(jnp.bfloat16)
    value, gate = mm(hidden, wa_ref[...]), mm(hidden, wb_ref[...])
    up_ref[0] = value
    up_ref[1] = gate
    gated = (value * gate_parts(gate)[0]).astype(jnp.bfloat16)
    second_ref[...] += mm(gated, wd_ref[...])

    @pl.when(step == pl.num_programs(0) - 1)
    def _():
        cond = norm_rows(second_ref[...], gains_ref[2:3].astype(jnp.float32)).astype(jnp.bfloat16)
        for weight, scale_ref in ((attn_ref, scale_attn_ref), (ffn_ref, scale_ffn_ref)):
            scale = 1.0 + mm(cond, weight[...])
            for image in range(count):
                scale_ref[image] = scale[image : image + 1]


def hidden_blocks(w_map_up, w_map_down, block):
    width, steps = w_map_up.shape[0], w_map_down.shape[0] // block
    return [
        (w_map_up, (width, block), lambda j: (0, j)),
        (w_map_up, (width, block), lambda j: (0, steps + j)),
        (w_map_down, (block, width), lambda j: (j, 0)),
    ]


def map_forward(line, labels, sigma, fourier, table, w_time, w_up, w_down, gains, w_attn, w_ffn):
    images, width = labels.shape[0], w_time.shape[1]
    hidden, block, model = w_down.shape[0], 1152, w_attn.shape[1]
    return call(
        line,
        map_kernel,
        (hidden // block,),
        [
            scalars(labels),
            scalars(sigma),
            whole(fourier[None]),
            whole(table),
            whole(w_time),
            whole(gains),
            *hidden_blocks(w_up, w_down, block),
            whole(w_attn),
            whole(w_ffn),
        ],
        [
            fresh((images, 1, model)),
            fresh((images, 1, model)),
            fresh((8, width)),
            fresh((8, width)),
            fresh((8, width)),
            (jax.ShapeDtypeStruct((2, 8, hidden), jnp.float32), (2, 8, block), lambda j: (0, 0, j)),
            fresh((8, 128)),
        ],
        scratch=[pltpu.VMEM((8, width), jnp.float32)],
        flops=16 * width * (3 * hidden + 2 * model),
        moved=2 * width * (3 * hidden + 2 * model + 1256),
    )


def map_back_kernel(
    gattn_ref,
    gffn_ref,
    heads_ref,
    numbers_ref,
    gains_ref,
    start_ref,
    first_ref,
    second_ref,
    up_ref,
    wa_ref,
    wb_ref,
    wd_ref,
    attn_ref,
    ffn_ref,
    sent_ref,
    gsecond_ref,
    gup_ref,
    ghidden_ref,
    gain_ref,
    rows_ref,
):
    step, steps = pl.program_id(0), pl.num_programs(0)
    count = gattn_ref.shape[0]
    block = wd_ref.shape[0]
    gains = gains_ref[...].astype(jnp.float32)

    @pl.when(step == 0)
    def _():
        rows_ref[...] = jnp.zeros_like(rows_ref)
        for image in range(count):
            rows_ref[0, image : image + 1] = gattn_ref[image]
            rows_ref[1, image : image + 1] = gffn_ref[image]
        grad = times(rows_ref[0], attn_ref[...]) + times(rows_ref[1], ffn_ref[...])
        gsecond, gain = norm_back(second_ref[...], gains[2:3], grad)
        gsecond_ref[...] = gsecond
        gain_ref[2:3] = gain
        ghidden_ref[...] = jnp.zeros_like(ghidden_ref)

    grad = times(gsecond_ref[...], wd_ref[...])
    bent, slope = gate_parts(up_ref[1])
    for part, (new, weight) in enumerate(((grad * bent, wa_ref), (grad * up_ref[0] * slope, wb_ref))):
        at = pl.multiple_of(step * block, block)
        gup_ref[part, :, pl.ds(at, block)] = new
        ghidden_ref[...] += times(new, weight[...])

    @pl.when(step == steps - 1)
    def _():
        gfirst, gain = norm_back(first_ref[...], gains[1:2], ghidden_ref[...])
        gain_ref[1:2] = gain
        gsecond = gsecond_ref[...]
        gstart, gain = norm_back(start_ref[...], gains[0:1], gfirst + gsecond)
        gain_ref[0:1] = gain
        model = heads_ref.shape[1]
        lane = lax.broadcasted_iota(jnp.int32, (model, 128), 1)
        row = lax.broadcasted_iota(jnp.int32, (model, 128), 0)
        pick = jnp.where(row == lane * 64, 1.0, 0.0).astype(jnp.bfloat16)
        heads = times(jnp.concatenate([heads_ref[...], jnp.zeros((7, model))], axis=0), pick, NN)
        sent_ref[...] = jnp.zeros_like(sent_ref)
        devices = sent_ref.shape[0]
        hidden = gup_ref.shape[2]
        for device in range(devices):
            spot = 0
            for values in (rows_ref[0], rows_ref[1], gsecond):
                width = values.shape[1] // devices
                sent_ref[device, 0:count, spot : spot + width] = values[
                    0:count, device * width : device * width + width
                ]
                spot += width
            width = 2 * hidden // devices
            part, at = divmod(device * width, hidden)
            sent_ref[device, 0:count, spot : spot + width] = gup_ref[part, 0:count, at : at + width]
            spot += width
            width = gstart.shape[1] // devices
            sent_ref[device, 0:count, spot : spot + width] = gstart[
                0:count, device * width : device * width + width
            ]
            for index in range(3):
                sent_ref[device, count : count + 1, index * width : index * width + width] = gain_ref[
                    index : index + 1, device * width : device * width + width
                ]
            sent_ref[device, count + 1 : 2 * count + 1, 0:128] = numbers_ref[0:count]
            used = model // 64
            sent_ref[device, count : count + 1, 3 * width : 3 * width + used] = heads[0:1, 0:used]


def map_backward(line, grad_attn, grad_ffn, heads, saved, gains, w_up, w_down, w_attn, w_ffn, devices):
    start, first, second, up, numbers = saved
    width, hidden, block = start.shape[1], w_down.shape[0], 1152
    model = w_attn.shape[1]
    columns = -(-(2 * model + 2 * width + 2 * hidden) // devices // 128) * 128
    return call(
        line,
        map_back_kernel,
        (hidden // block,),
        [
            whole(grad_attn),
            whole(grad_ffn),
            whole(heads),
            whole(numbers),
            whole(gains),
            whole(start),
            whole(first),
            whole(second),
            (up, (2, 8, block), lambda j: (0, 0, j)),
            *hidden_blocks(w_up, w_down, block),
            whole(w_attn),
            whole(w_ffn),
        ],
        [fresh((devices, 8, columns))],
        scratch=[
            pltpu.VMEM((8, width), jnp.float32),
            pltpu.VMEM((2, 8, hidden), jnp.float32),
            pltpu.VMEM((8, width), jnp.float32),
            pltpu.VMEM((8, width), jnp.float32),
            pltpu.VMEM((2, 8, model), jnp.float32),
        ],
        flops=32 * width * (3 * hidden + 2 * model),
        moved=2 * width * (3 * hidden + 2 * model),
    )[0]


def map_weights_kernel(
    columns_ref,
    fourier_ref,
    table_ref,
    time_ref,
    gains_ref,
    wa_ref,
    wb_ref,
    wd_ref,
    class_ref,
    wtime_ref,
    wup_ref,
    wdown_ref,
    wgain_ref,
    wattn_ref,
    wffn_ref,
    heads_ref,
    hidden_ref,
    second_ref,
    number_rows,
    rows_ref,
):
    step = pl.program_id(0)
    devices, count = columns_ref.shape[0], rows_ref.shape[0] // columns_ref.shape[0]
    attn, ffn, second, up, start = (
        wattn_ref.shape[0],
        wffn_ref.shape[0],
        wdown_ref.shape[0],
        wup_ref.shape[0],
        class_ref.shape[0],
    )
    edges = [0]
    for width in (attn, ffn, second, up, start):
        edges.append(edges[-1] + width)

    def columns(index):
        return rows_ref[:, edges[index] : edges[index + 1]]

    @pl.when(step == 0)
    def _():
        extra = jnp.zeros((1, columns_ref.shape[2]), jnp.float32)
        for device in range(devices):
            at = slice(device * count, device * count + count)
            number_rows[at] = columns_ref[device, count + 1 : 2 * count + 1, 0:128]
            rows_ref[at] = columns_ref[device, 0:count]
            extra += columns_ref[device, count : count + 1]
        for index in range(3):
            wgain_ref[index : index + 1] = extra[:, index * start : index * start + start]
        heads_ref[...] = extra[:, 3 * start : 3 * start + heads_ref.shape[1]]
        numbers = number_rows[...].astype(jnp.int32)
        feats, one_hot, _, first, hidden = first_rows(
            numbers[:, 0:1], numbers[:, 1:2], fourier_ref, table_ref, time_ref, gains_ref
        )
        hidden_ref[...] = hidden
        second_ref[...] = first
        class_ref[...] = outer(one_hot, columns(4))
        wtime_ref[...] = outer(feats, columns(4))
        wup_ref[...] = outer(hidden, columns(3))

    hidden = hidden_ref[...]
    value, gate = mm(hidden, wa_ref[...]), mm(hidden, wb_ref[...])
    gated = (value * gate_parts(gate)[0]).astype(jnp.bfloat16)
    second_ref[...] += mm(gated, wd_ref[...])
    wdown_ref[...] = outer(gated, columns(2))

    @pl.when(step == pl.num_programs(0) - 1)
    def _():
        cond = norm_rows(second_ref[...], gains_ref[2:3].astype(jnp.float32)).astype(jnp.bfloat16)
        wattn_ref[...] = outer(cond, columns(0))
        wffn_ref[...] = outer(cond, columns(1))


def map_weights(line, columns, count, fourier, table, w_time, w_up, w_down, gains, model):
    devices = columns.shape[0]
    rows = devices * count
    width, hidden, block = w_time.shape[1], w_down.shape[0], 1152
    own = width // devices
    return call(
        line,
        map_weights_kernel,
        (hidden // block,),
        [
            whole(columns),
            whole(fourier[None]),
            whole(table),
            whole(w_time),
            whole(gains),
            *hidden_blocks(w_up, w_down, block),
        ],
        [
            fresh((own, table.shape[0])),
            fresh((own, w_time.shape[0])),
            fresh((2 * hidden // devices, width)),
            (jax.ShapeDtypeStruct((own, hidden), jnp.float32), (own, block), lambda j: (0, j)),
            fresh((3, own)),
            fresh((model // devices, width)),
            fresh((model // devices, width)),
            fresh((1, model // 64)),
        ],
        scratch=[
            pltpu.VMEM((rows, width), jnp.bfloat16),
            pltpu.VMEM((rows, width), jnp.float32),
            pltpu.VMEM((rows, 128), jnp.float32),
            pltpu.VMEM((rows, columns.shape[2]), jnp.float32),
        ],
        flops=2 * rows * width * 4 * hidden,
        moved=2 * width * (3 * hidden + 1256) + 4 * width * 400,
    )


class Sum:
    def __init__(self, terms, columns, pair=None):
        self.lists = [terms] if pair is None else [pair[0].lists[0], pair[1].lists[0]]
        self.more = []
        self.level = None
        self.done = [] if pair is None else [*{*pair[0].done, *pair[1].done}]
        self.columns = columns
        self.lone = None if pair is None else pair[0].lone
        self.stacked = False

    def last(self):
        return self.lists[0][-1][0]

    def together(self):
        self.stacked = True
        return self

    def apart(self):
        self.stacked = False
        return self

    def dims(self):
        return self.lists[0][0][1]

    def left(self):
        return [name for name in self.dims() if name not in self.done]


def columns_of(part, start, count):
    return Sum([(array, dims, start) for array, dims, _ in part.lists[0]], count)


def split(own, sent, level, names, lone=None):
    came = trade(sent, level, lone)
    rows = own.size // own.shape[-1] // 2 ** len(names)
    shape = (*([2] * len(names)), rows, own.shape[-1])
    return Sum([(array.reshape(shape), names, 0) for array in (own, came)], own.shape[-1])


def lone_sum(sent, bit, names):
    came = trade(sent, bit, bit, True)
    rows = sent.size // sent.shape[-1] // 2 ** len(names)
    shape = (*([2] * len(names)), rows, sent.shape[-1])
    found = Sum([(array.reshape(shape), names, 0) for array in (sent, came)], sent.shape[-1])
    found.lone = bit
    return found


def joined(pair):
    return Sum(None, pair[0].columns, pair)


def combine(line, bits, jobs, steps):
    ins, outs, plan = [scalars(bits)], [], []

    def place(dims, fixed, column, width, block):
        def where(step, bits):
            spots = []
            for name in dims:
                if isinstance(name, tuple):
                    spots.append(name[1])
                elif name not in fixed:
                    spots.append(0)
                else:
                    spot = 0 if name == "core" else 1 + name
                    spots.append(bits[spot] if fixed[name] else 1 - bits[spot])
            return (*spots, 0, column // block + step)

        return where

    for part, level in jobs:
        block = part.columns // steps
        fixed = {name: True for name in part.done}
        pick = part.level
        whole_sum = isinstance(level, tuple)
        if level is not None and pick != level and not whole_sum:
            fixed[level] = False
        groups = []
        for terms in [*part.lists, part.more]:
            group = []
            for array, dims, column in terms:
                rows = array.shape[-2]
                shape = (
                    *[1 if name in fixed or isinstance(name, tuple) else 2 for name in dims],
                    rows,
                    block,
                )
                group.append(len(ins) - 1)
                ins.append((array, shape, place(dims, fixed, column, part.columns, block)))
            groups.append(group)
        dims = [name for name in part.dims() if name not in fixed]
        shape = (*[2 for _ in dims], rows, part.columns)
        if part.stacked:
            dims, shape = [("at", 0), *dims], (2, *shape)
        dtype = jnp.bfloat16 if level is not None else jnp.float32
        outs.append(
            (jax.ShapeDtypeStruct(shape, dtype), (*shape[:-1], block), place(dims, {}, 0, 0, block))
        )
        plan.append((groups, pick, pick is not None and pick == level, part.stacked))

    def combine_kernel(bits_ref, *refs):
        results = refs[len(ins) - 1 :]
        for (groups, pick, swap, both), result in zip(plan, results):

            def total(group):
                found = None
                for index in group:
                    value = refs[index][...].reshape(shape).astype(jnp.float32)
                    found = value if found is None else found + value
                return found

            shape = result.shape[1:] if both else result.shape
            if both:
                for index in range(2):
                    result[index] = total(groups[index]).astype(result.dtype)
                continue
            found = total(groups[0])
            if pick is not None:
                first = bits_ref[1 + pick] == (1 if swap else 0)
                found = jnp.where(first, found, total(groups[1]))
            if groups[-1]:
                found = found + total(groups[-1])
            result[...] = found.astype(result.dtype)

    moved = sum(array.size for array, _, _ in ins)
    return call(line, combine_kernel, (steps,), ins, outs, moved=moved, prefetch=True)


def finish(line, bits, near, up, down, first, second, across, came):
    ins, groups = [scalars(bits)], []

    def add(terms, done, block, moving):
        group = []
        for array, dims, column in terms:
            group.append(len(ins) - 1)
            shape = (*[1] * len(dims), array.shape[-2], block)

            def where(step, bits, dims=dims, column=column):
                spots = []
                for name in dims:
                    if isinstance(name, tuple):
                        spots.append(name[1])
                    else:
                        spots.append(bits[0] if name == "core" else bits[1 + name])
                return (*spots, 0, column // block + (step if moving else 0))

            ins.append((array, shape, where))
        groups.append(group)

    half = up.columns // 2
    add(up.lists[0], up.done, half, True)
    add(up.lists[1], up.done, half, True)
    add(up.more, up.done, half, True)
    add([(came[0], (), 0)], (), half, True)
    add(down.lists[0], down.done, down.columns, False)
    add(down.lists[1], down.done, down.columns, False)
    add([(came[1], (("at", 0),), 0)], (), down.columns, False)
    add([(came[1], (("at", 1),), 0)], (), down.columns, False)
    add(first.lists[0], first.done, first.columns, False)
    add(second.lists[0], second.done, second.columns, False)
    count = len(ins) - 1
    pick = up.level

    def finish_kernel(bits_ref, *refs):
        up_ref, down_ref, wide_ref, out_ref = refs[count:]
        step = pl.program_id(0)

        def total(index):
            found = None
            for spot in groups[index]:
                value = refs[spot][...]
                value = value.reshape(value.shape[-2:]).astype(jnp.float32)
                found = value if found is None else found + value
            return found

        held = jnp.where(bits_ref[1 + pick] == 0, total(0), total(1)) + total(2)
        up_ref[...] = jnp.where(bits_ref[1 + near] == bits_ref[0], held, total(3))
        mine = jnp.concatenate([total(4), total(5)], axis=1)
        theirs = jnp.concatenate([total(6), total(7)], axis=1)
        down_ref[...] = jnp.where(step == bits_ref[0], mine, theirs)
        both = jnp.where(step == 0, total(8), total(9))
        wide_ref[...] = both[:across]
        out_ref[...] = both[across:]

    def share(rows, width):
        return (
            jax.ShapeDtypeStruct((rows, width), jnp.float32),
            (rows, width // 2),
            lambda step, bits: (0, step),
        )

    return call(
        line,
        finish_kernel,
        (2,),
        ins,
        [
            share(up.lists[0][0][0].shape[-2], up.columns),
            share(down.lists[0][0][0].shape[-2], 4 * down.columns),
            share(across, 2 * first.columns),
            share(first.lists[0][0][0].shape[-2] - across, 2 * first.columns),
        ],
        prefetch=True,
    )


def trade(sent, name, lone=None, first=False):
    if name == "core":
        return lax.ppermute(sent, "space", [(0, 1), (1, 0)])
    count = lax.axis_size("dp")
    if lone is None:
        return lax.ppermute(sent, "dp", [(i, i ^ (1 << name)) for i in range(count)])
    pairs = [
        (2 * i + core, 2 * (i ^ (1 << name)) + core)
        for i in range(count)
        for core in range(2)
        if (core == (i >> lone) & 1) != first
    ]
    return lax.ppermute(sent, BOTH, pairs)


def advance(line, bits, jobs, steps=2):
    for part, level in jobs:
        if len(part.lists) == 2 and part.level is None and not part.stacked:
            part.level = level
    sent = combine(line, bits, jobs, steps)
    for (part, level), value in zip(jobs, sent):
        if isinstance(level, tuple):
            part.lone = level[0]
            came = trade(value, level[0], level[0], True)
        else:
            came = trade(value, level, part.lone)
        arrived(part, level, came)


def arrived(part, level, came):
    dims = [name for name in part.left() if name != level]
    if not isinstance(level, tuple) and part.level != level:
        part.done.append(level)
    if part.stacked:
        for index in range(2):
            part.lists[index].append((came, [("at", index), *dims], 0))
    elif part.level is not None:
        part.more.append((came, dims, 0))
    else:
        part.lists[0].append((came, dims, 0))


def shards(
    tokens,
    cotangent,
    labels,
    sigma_index,
    fourier,
    class_table,
    w_time,
    w_map_up,
    w_map_down,
    map_gains,
    w_ada_attn,
    w_ada_ffn,
    w_qkv,
    head_scale,
    w_out,
    w_up,
    w_down,
):
    all_images, local_len, model_width = tokens.shape
    num_images = all_images // 2
    num_heads = head_scale.shape[0]
    head_dim = model_width // num_heads
    seq_len = 2 * local_len
    devices = lax.axis_size("dp") * lax.axis_size("space")
    core = lax.axis_index("space")

    def swap(value):
        return lax.ppermute(value, "space", [(0, 1), (1, 0)])

    def other_half(value):
        return swap(lax.dynamic_slice_in_dim(value, (1 - core) * num_images, num_images, axis=0))

    def tokens_half(value):
        return value.reshape(num_images, seq_len, -1)[:, local_len:]

    def split_images(value, came):
        kept = value.reshape(num_images, seq_len, -1)[:, :local_len]
        return jnp.where(
            core == 0,
            jnp.concatenate([kept, came], axis=0),
            jnp.concatenate([came, kept], axis=0),
        )

    levels = lax.axis_size("dp").bit_length() - 1
    dp = lax.axis_index("dp")
    bits = jnp.stack([core, *[(dp >> level) & 1 for level in range(levels)]]).astype(jnp.int32)
    every = [*reversed(range(levels))]
    low = list(range(levels - 2))
    swapped = [*reversed(low[:2]), *low[2:]]
    near, far = levels - 2, levels - 1

    cos, sin = [jnp.asarray(table) for table in rope_tables(seq_len, num_heads, head_dim, GRID)]
    root = jnp.repeat(jnp.sqrt(head_scale.astype(jnp.float32)), head_dim)[None]
    all_cotangent = swap(cotangent)
    line = []
    scale_attn, scale_ffn, *map_saved = map_forward(
        line,
        labels,
        sigma_index,
        fourier,
        class_table,
        w_time,
        w_map_up,
        w_map_down,
        map_gains,
        w_ada_attn,
        w_ada_ffn,
    )
    normed, qkv, unit, tokens = project_qkv(
        line, bits, tokens, other_half(tokens), scale_attn, w_qkv, cos, sin, root
    )
    attended, inverse, mixed, normed_ffn, cotangent = attend(
        line, bits, qkv, tokens, scale_ffn, w_out, cotangent, all_cotangent
    )
    other_ffn = swap(normed_ffn)
    piece = low[-1]
    share = w_up.shape[1] // devices
    up_rest = [far, *reversed(low[1:-1]), "core"]
    down_all = [*every, "core"]

    up_all = [far, *reversed(low[:-1]), "core"]

    def down_sum(down):
        rows = down.shape[0] // 2 ** len(down_all)
        down = down.reshape(*([2] * len(down_all)), rows, down.shape[1])
        return Sum([(down, down_all, 0)], down.shape[-1])

    own, sent, down0, y_part, g_part = ffn(
        line, bits, 0, share, normed_ffn, other_ffn, cotangent, w_up, w_down
    )
    up0 = split(own, sent, low[0], up_rest)
    sent, down1, y_own, y_sent, g_own, g_sent = ffn(
        line,
        bits,
        1,
        share,
        normed_ffn,
        other_ffn,
        cotangent,
        w_up,
        w_down,
        (mixed, y_part, g_part),
    )
    g_came = swap(g_sent)
    up1 = lone_sum(sent, near, up_all)
    mid = low[1:-1]
    down = joined((down_sum(down0), down_sum(down1))).together()
    first_model = model_width // 2

    def then(*arrays):
        line.extend(arrays)

    def later(array):
        return lax.optimization_barrier((array, *line))[0]

    def step(*jobs):
        advance(line, bits, jobs)

    y_came = swap(y_sent)
    step((down, piece))
    then(up0.last())
    grad_mixed, grad_low, grad_qkv, grad_scale, grad_mod_ffn = back(
        line,
        bits,
        cotangent,
        mixed,
        g_own,
        g_came,
        scale_ffn,
        w_out,
        qkv,
        attended,
        inverse,
        unit,
        cos,
        sin,
        root,
    )
    groups = devices // 2
    own, sent = weight_grads(line, bits, groups, grad_qkv, normed, grad_low, attended)
    shape = (*([2] * levels), *own.shape[1:])
    terms = [(array.reshape(shape), every) for array in (own, swap(sent))]
    first, second = [
        Sum([(array, dims, start) for array, dims in terms], first_model)
        for start in (0, first_model)
    ]
    then(down.last())
    step((up0, (near,)), (up1, low[0]))
    for level in mid:
        step((up0, level), (up1, level), (down, level))
    up = joined((up0, up1))
    then(y_came)
    grad_tokens, grad_mod_attn = tokens_backward(
        line, grad_qkv, w_qkv, tokens, scale_attn, grad_mixed
    )
    tokens_came = swap(tokens_half(grad_tokens))
    step((first, piece), (second, near))
    then(tokens_came)
    step((up, piece), (down, low[0]))
    columns = lax.all_to_all(
        map_backward(
            line,
            grad_mod_attn,
            grad_mod_ffn,
            grad_scale,
            map_saved,
            map_gains,
            w_map_up,
            w_map_down,
            w_ada_attn,
            w_ada_ffn,
            devices,
        ),
        BOTH,
        0,
        0,
        tiled=True,
    )
    for level in mid:
        step((first, level), (second, level))
    step((first, near), (second, low[0]), (up, far), (down, near))
    (
        sum_class,
        sum_time,
        sum_map_up,
        sum_map_down,
        sum_gains,
        sum_ada_attn,
        sum_ada_ffn,
        sum_heads,
    ) = map_weights(
        line,
        columns,
        labels.shape[0],
        fourier,
        class_table,
        w_time,
        w_map_up,
        w_map_down,
        map_gains,
        model_width,
    )
    out_tokens = (later(y_own) + y_came.astype(jnp.float32)).astype(jnp.bfloat16)
    out_came = swap(tokens_half(out_tokens))
    out_tokens = split_images(out_tokens, out_came)
    step((first, low[0]), (second, piece), (down, far))
    grad_tokens = split_images(later(grad_tokens), tokens_came)
    *sent, up_sent, down_sent = combine(
        line, bits, [(first, far), (second, far), (up, "core"), (down, "core")], 2
    )
    for part, value in zip((first, second), sent):
        arrived(part, far, trade(value, far))
    came = [swap(up_sent), swap(down_sent)]
    up.done.append("core")
    down.done.append("core")
    sum_up, sum_down, sum_qkv, sum_out = [
        total.T for total in finish(
            line, bits, near, up, down, first, second, 3 * model_width // devices, came
        )
    ]
    return (
        out_tokens,
        grad_tokens,
        sum_class.T,
        sum_time.T,
        sum_map_up.T,
        sum_map_down.T,
        sum_gains,
        sum_ada_attn.T,
        sum_ada_ffn.T,
        sum_qkv,
        sum_heads[0],
        sum_out,
        sum_up,
        sum_down,
    )


def solution(mesh):
    placed = (
        P("dp", "space", None),
        P("dp", "space", None),
        P(("dp", "space")),
        P(("dp", "space")),
        P(),
        P(),
        P(),
        P(),
        P(),
        P(),
        P(),
        P(),
        P(),
        P(),
        P(),
        P(),
        P(),
    )
    return jax.shard_map(
        shards,
        mesh=mesh,
        in_specs=placed,
        out_specs=(
            P("dp", "space", None),
            P("dp", "space", None),
            P(None, ("dp", "space")),
            P(None, ("dp", "space")),
            P(None, ("dp", "space")),
            P(None, ("dp", "space")),
            P(None, ("dp", "space")),
            P(None, ("dp", "space")),
            P(None, ("dp", "space")),
            P(None, ("dp", "space")),
            P(),
            P(None, ("dp", "space")),
            P(None, ("dp", "space")),
            P(None, ("dp", "space")),
        ),
        check_vma=False,
    )
```

```python
import functools
import math

import jax
import jax.numpy as jnp
import numpy as np
from jax import lax
from jax.experimental import pallas as pl
from jax.experimental.pallas import tpu as pltpu
from jax.sharding import PartitionSpec as P

NSIG = 64
GRID = 16


EPSILON = 1e-06
BOTH = ("dp", "space")
LOG_LOW = math.log(0.01)
LOG_SPAN = math.log(10000.0)


def rope_tables(tokens, heads, head_dim, side):
    quarter = head_dim // 8
    order = np.arange(quarter)[None, :] * heads + np.arange(heads)[:, None]
    frequency = np.exp(math.log(math.pi) + math.log(10.0) * order / (heads * quarter))
    places = np.arange(tokens)
    row = -1.0 + (2.0 * (places // side) + 1.0) / side
    col = -1.0 + (2.0 * (places % side) + 1.0) / side
    angles = np.concatenate(
        [row[:, None, None] * frequency[None], col[:, None, None] * frequency[None]], axis=-1
    )
    cos, sin, flat = np.cos(angles), np.sin(angles), np.zeros_like(angles)
    tables = [
        np.concatenate([cos, cos, flat + 1.0, flat + 1.0], axis=-1),
        np.concatenate([-sin, sin, flat, flat], axis=-1),
    ]
    return [table.reshape(tokens, heads * head_dim).astype(np.float32) for table in tables]


VMEM_LIMIT = 60 * 1024 * 1024
NN = (((1,), (0,)), ((), ()))
NT = (((1,), (1,)), ((), ()))
TN = (((0,), (0,)), ((), ()))


def mm(left, right, dims=NN):
    return lax.dot_general(left, right, dims, preferred_element_type=jnp.float32)


SPARE = 12 * 1024 * 1024
SMALL = set()
HEAVY = {'back_kernel': 1000000, 'tokens_kernel': 1000000, 'map_back_kernel': 1000000, 'map_weights_kernel': 1000000}


def call(line, body, grid, ins, outs, scratch=(), flops=0, moved=0, prefetch=False, spare=SPARE):
    arrays = [array for array, _, _ in ins]
    least = min(range(len(arrays)), key=lambda k: arrays[k].size)
    if line:
        arrays[least] = lax.optimization_barrier((arrays[least], *line))[0]
    in_specs = [
        pl.BlockSpec(memory_space=pltpu.SMEM) if block is None else pl.BlockSpec(block, where)
        for _, block, where in ins
    ]
    out_specs = [pl.BlockSpec(block, where) for _, block, where in outs]
    if prefetch:
        layout = {
            "grid_spec": pltpu.PrefetchScalarGridSpec(
                num_scalar_prefetch=1,
                grid=grid,
                in_specs=in_specs[1:],
                out_specs=out_specs,
                scratch_shapes=list(scratch),
            )
        }
    else:
        layout = {
            "grid": grid,
            "in_specs": in_specs,
            "out_specs": out_specs,
            "scratch_shapes": list(scratch),
        }
    blocks = [(array, block) for array, block, _ in [*ins, *outs] if block is not None]
    room = sum(math.prod(block) * array.dtype.itemsize for array, block in blocks)
    room = min(VMEM_LIMIT, 2 * room + sum(a.dtype.itemsize * math.prod(a.shape) for a in scratch) + spare)
    name = getattr(body, "func", body).__name__
    scale = HEAVY.get(name, 1)
    if name not in SMALL:
        room = VMEM_LIMIT
    flops, moved = flops // 1000 + 1, moved // 1000 + 1
    results = pl.pallas_call(
        body,
        name=name,
        out_shape=[shape for shape, _, _ in outs],
        compiler_params=pltpu.CompilerParams(
            dimension_semantics=("arbitrary",) * len(grid), vmem_limit_bytes=room
        ),
        cost_estimate=pl.CostEstimate(flops=flops * scale, bytes_accessed=moved * scale, transcendentals=0),
        **layout,
    )(*arrays)
    line[:] = [min(results, key=lambda result: result.size)]
    return results


def whole(array):
    return (array, array.shape, lambda *j: (0,) * array.ndim)


def fresh(shape, dtype=jnp.float32):
    return (jax.ShapeDtypeStruct(shape, dtype), shape, lambda *j: (0,) * len(shape))


def scalars(array):
    return (array, None, None)


def head_sums(values):
    lanes = values.shape[1]
    row = lax.broadcasted_iota(jnp.int32, (2 * lanes, lanes), 0) % lanes // (lanes // 2)
    col = lax.broadcasted_iota(jnp.int32, (2 * lanes, lanes), 1) // (lanes // 2)
    ones = jnp.where(row == col, 1.0, 0.0).astype(jnp.bfloat16)
    high = values.astype(jnp.bfloat16)
    rest = (values - high.astype(jnp.float32)).astype(jnp.bfloat16)
    return mm(jnp.concatenate([high, rest], axis=1), ones)


def rotate(values, cos, sin):
    lanes = values.shape[1]
    lane = lax.broadcasted_iota(jnp.int32, values.shape, 1)
    first = lane % (lanes // 2) < lanes // 8
    near = jnp.where(first, pltpu.roll(values, lanes - lanes // 8, 1), pltpu.roll(values, lanes // 8, 1))
    return values * cos + near * sin


def by_place(pair, at):
    return jnp.concatenate([pair[0][:, at], pair[1][:, at]], axis=0)


def table_blocks(table, block, column):
    half = table.shape[0] // 2
    return [
        (table, (half, block), lambda *grid: (grid[-1][0], column(*grid[:-1]))),
        (table, (half, block), lambda *grid: (1 - grid[-1][0], column(*grid[:-1]))),
    ]


def qkv_kernel(
    bits_ref, own_ref, came_ref, scale_ref, w_ref, cos_a, cos_b, sin_a, sin_b, root_ref, normed_ref, qkv_ref, unit_ref, both_ref
):
    step = pl.program_id(0)
    count, seq = scale_ref.shape[0], 2 * own_ref.shape[1]

    @pl.when(step == 0)
    def _():
        for image in range(count):
            rows = pl.ds(image * seq, seq)
            both = jnp.concatenate([own_ref[image], came_ref[image]], axis=0)
            both_ref[rows, :] = both
            tok = both.astype(jnp.float32)
            inverse = lax.rsqrt(jnp.mean(tok * tok, axis=-1, keepdims=True) + EPSILON)
            normed_ref[rows, :] = (tok * inverse * scale_ref[image]).astype(jnp.bfloat16)

    rotated = step < 2 * pl.num_programs(0) // 3

    @pl.when(rotated)
    def _():
        wide = mm(normed_ref[...], w_ref[...])
        for lane in range(0, w_ref.shape[1], 128):
            at = slice(lane, lane + 128)
            heads = wide[:, at]
            unit = root_ref[:, at] * lax.rsqrt(head_sums(heads * heads) + EPSILON)
            unit_ref[:, at] = unit
            heads = heads * unit
            cos, sin = by_place((cos_a, cos_b), at), by_place((sin_a, sin_b), at)
            for image in range(count):
                turned = rotate(heads[image * seq : image * seq + seq], cos, sin)
                qkv_ref[pl.ds(image * seq, seq), at] = turned.astype(jnp.bfloat16)

    @pl.when(jnp.logical_not(rotated))
    def _():
        qkv_ref[...] = mm(normed_ref[...], w_ref[...]).astype(jnp.bfloat16)


def project_qkv(line, bits, tokens, came, scale_attn, w_qkv, cos, sin, root):
    count, half, width = came.shape
    rows = count * half * 2
    total, block = w_qkv.shape[1], width
    steps = total // block
    turned = steps * 2 // 3
    per = width // block
    return call(
        line,
        qkv_kernel,
        (steps,),
        [
            scalars(bits),
            (tokens, (count, half, width), lambda j, bits: (bits[0], 0, 0)),
            whole(came),
            whole(scale_attn),
            (w_qkv, (width, block), lambda j, bits: (0, j)),
            *table_blocks(cos, block, lambda j: j % per),
            *table_blocks(sin, block, lambda j: j % per),
            (root, (1, block), lambda j, bits: (0, j % per)),
        ],
        [
            (jax.ShapeDtypeStruct((rows, width), jnp.bfloat16), (rows, width), lambda j, bits: (0, 0)),
            (jax.ShapeDtypeStruct((rows, total), jnp.bfloat16), (rows, block), lambda j, bits: (0, j)),
            (
                jax.ShapeDtypeStruct((rows, 2 * width), jnp.float32),
                (rows, block),
                lambda j, bits: (0, jnp.minimum(j, turned - 1)),
            ),
            fresh((rows, width), jnp.bfloat16),
        ],
        flops=2 * rows * width * total,
        moved=2 * width * total + 14 * rows * width,
        prefetch=True,
    )


def attention_kernel(
    bits_ref,
    q_ref,
    k_ref,
    v_ref,
    tok_ref,
    scale_ref,
    w_ref,
    own_ref,
    own_came_ref,
    other_ref,
    other_came_ref,
    att_ref,
    inv_ref,
    mixed_ref,
    nf_ref,
    cot_ref,
):
    part = pl.program_id(1)

    @pl.when(part == 0)
    def _():
        cot_ref[0] = jnp.concatenate([own_ref[0], own_came_ref[0]], axis=0)
        cot_ref[1] = jnp.concatenate([other_came_ref[0], other_ref[0]], axis=0)
        mixed_ref[...] = tok_ref[...].astype(jnp.float32)

    seq, width = q_ref.shape
    left = lax.broadcasted_iota(jnp.int32, (seq, 128), 1) < 64
    for pair in range(width // 128):
        at = slice(pair * 128, pair * 128 + 128)
        queries, keys, values = q_ref[:, at], k_ref[:, at], v_ref[:, at]
        none, one = jnp.zeros_like(queries), jnp.ones_like(queries)
        weights0 = jnp.exp(mm(jnp.where(left, queries, none), keys, NT)).astype(jnp.bfloat16)
        weights1 = jnp.exp(mm(jnp.where(left, none, queries), keys, NT)).astype(jnp.bfloat16)
        both0 = mm(weights0, jnp.where(left, values, one))
        both1 = mm(weights1, jnp.where(left, one, values))
        totals = pltpu.roll(jnp.where(left, both1, both0), 64, 1)
        inverse = 1.0 / totals
        inv_ref[:, at] = inverse
        att_ref[:, at] = (jnp.where(left, both0, both1) * inverse).astype(jnp.bfloat16)
    mixed = mixed_ref[...] + mm(att_ref[...], w_ref[...])
    mixed_ref[...] = mixed

    @pl.when(part == pl.num_programs(1) - 1)
    def _():
        inverse = lax.rsqrt(jnp.mean(mixed * mixed, axis=-1, keepdims=True) + EPSILON)
        nf_ref[...] = (mixed * inverse * scale_ref[0]).astype(jnp.bfloat16)


def attend(line, bits, qkv, tokens, scale_ffn, w_out, cotangent, came):
    rows, width = tokens.shape
    images = scale_ffn.shape[0]
    seq, parts = rows // images, 1
    block = width // parts

    def part(index):
        return (qkv, (seq, block), lambda i, h, bits: (i, index * parts + h))

    def result(dtype):
        return (jax.ShapeDtypeStruct((rows, width), dtype), (seq, width), lambda i, h, bits: (i, 0))

    def half(dtype):
        return (jax.ShapeDtypeStruct((rows, width), dtype), (seq, block), lambda i, h, bits: (i, h))

    return call(
        line,
        attention_kernel,
        (images, parts),
        [
            scalars(bits),
            part(0),
            part(1),
            part(2),
            (tokens, (seq, width), lambda i, h, bits: (i, 0)),
            (scale_ffn, (1, 1, width), lambda i, h, bits: (i, 0, 0)),
            (w_out, (block, width), lambda i, h, bits: (h, 0)),
            *[
                (array, (1, seq // 2, width), lambda i, h, bits, own=own: ((bits[0] if own else 1 - bits[0]) * images + i, 0, 0))
                for own in (True, False)
                for array in (cotangent, came)
            ],
        ],
        [
            half(jnp.bfloat16),
            half(jnp.float32),
            result(jnp.float32),
            result(jnp.bfloat16),
            (
                jax.ShapeDtypeStruct((2, rows, width), jnp.bfloat16),
                (2, seq, width),
                lambda i, h, bits: (0, i, 0),
            ),
        ],
        flops=2 * rows * width * width + 4 * rows * seq * width,
        moved=2 * width * width + 20 * rows * width,
        prefetch=True,
    )


def ffn_kernel(last, share, bits_ref, nf_ref, other_ref, cot_ref, wa_ref, wb_ref, wd_ref, *refs):
    if last:
        mixed_ref, y_in, g_in, *refs = refs
    up_own, *refs = refs
    if not last:
        up_sent, *refs = refs
    down_ref, *refs = refs
    if last:
        y_own, y_sent, g_own, g_sent, up_ref, y_ref, g_ref = refs
    else:
        y_out, g_out, up_ref, y_ref, g_ref = refs
    step, steps = pl.program_id(0), pl.num_programs(0)
    block = wa_ref.shape[1]
    rows, width = nf_ref.shape

    @pl.when(step == 0)
    def _():
        if last:
            y_ref[...] = y_in[...].astype(jnp.float32)
            g_ref[...] = g_in[...].astype(jnp.float32)
        else:
            y_ref[...] = jnp.zeros_like(y_ref)
            g_ref[...] = jnp.zeros_like(g_ref)

    size = 256
    found = []
    for side, inputs in enumerate((nf_ref, other_ref)):
        parts = []
        for start in range(0, rows, size):
            at = pl.ds(start, size)
            nf = inputs[at, :]
            value = mm(nf, wa_ref[...])
            gate = mm(nf, wb_ref[...])
            grad = mm(cot_ref[side, at, :], wd_ref[...], NT)
            bent, slope = gate_parts(gate)
            gated = (value * bent).astype(jnp.bfloat16)
            ga = (grad * bent).astype(jnp.bfloat16)
            gb = (grad * value * slope).astype(jnp.bfloat16)
            to = pl.ds(side * rows + start, size)
            y_ref[to, :] += mm(gated, wd_ref[...])
            g_ref[to, :] += mm(ga, wa_ref[...], NT) + mm(gb, wb_ref[...], NT)
            parts.append((ga, gb, gated))
        found.append([jnp.concatenate(part, axis=0) for part in zip(*parts)])
    for half in range(2):
        total = mm(found[0][half], nf_ref[...], TN) + mm(found[1][half], other_ref[...], TN)
        up_ref[half, pl.ds(pl.multiple_of(step * block, block), block), :] = total.astype(jnp.bfloat16)
    down = mm(cot_ref[0], found[0][2], TN) + mm(cot_ref[1], found[1][2], TN)
    down_ref[...] = down.astype(jnp.bfloat16)

    @pl.when(step == steps - 1)
    def _():
        own, other = bits_ref[1], 1 - bits_ref[1]
        group = 2 * share
        for half in range(2):
            if last:
                up_own[half] = up_ref[half]
                continue
            for index in range(up_ref.shape[1] // (2 * group)):
                at = pl.ds(index * group, group)
                for side, target in ((own, up_own), (other, up_sent)):
                    spot = pl.multiple_of(index * 2 * group + side * group, group)
                    target[half, at, :] = up_ref[half, pl.ds(spot, group), :]
        if last:
            y_own[...] = mixed_ref[...] + y_ref[:rows, :]
            y_sent[...] = y_ref[rows:, :].astype(jnp.bfloat16)
            g_own[...] = g_ref[:rows, :]
            g_sent[...] = g_ref[rows:, :].astype(jnp.bfloat16)
        else:
            y_out[...] = y_ref[...].astype(jnp.bfloat16)
            g_out[...] = g_ref[...].astype(jnp.bfloat16)


def ffn(line, bits, piece, share, nf, other, cot, w_up, w_down, before=None):
    rows, width = nf.shape
    hidden, block = w_down.shape[0], w_down.shape[0] // 4
    across = hidden // 4
    steps = across // block
    last = before is not None

    def place(base):
        return lambda j, bits: (0, base // block + bits[0] * 2 * steps + j)

    halved = ((2, across // 2, width), jnp.bfloat16)
    down = (
        jax.ShapeDtypeStruct((width, across), jnp.bfloat16),
        (width, block),
        lambda j, bits: (0, j),
    )
    low, wide = ((rows, width), jnp.bfloat16), ((rows, width), jnp.float32)
    both = ((2 * rows, width), jnp.bfloat16)
    return call(
        line,
        functools.partial(ffn_kernel, last, share),
        (steps,),
        [
            scalars(bits),
            whole(nf),
            whole(other),
            whole(cot),
            (w_up, (width, block), place(piece * across)),
            (w_up, (width, block), place(hidden + piece * across)),
            (
                w_down,
                (block, width),
                lambda j, bits: (bits[0] * 2 * steps + piece * steps + j, 0),
            ),
            *([whole(array) for array in before] if last else []),
        ],
        [
            *([fresh((2, across, width), jnp.bfloat16)] if last else [fresh(*halved), fresh(*halved)]),
            down,
            *([fresh(*wide), fresh(*low), fresh(*wide), fresh(*low)] if last else [fresh(*both), fresh(*both)]),
        ],
        scratch=[
            pltpu.VMEM((2, across, width), jnp.bfloat16),
            pltpu.VMEM((2 * rows, width), jnp.float32),
            pltpu.VMEM((2 * rows, width), jnp.float32),
        ],
        flops=36 * rows * width * across,
        moved=12 * width * across + 20 * rows * width,
        prefetch=True,
    )


def back_kernel(
    bits_ref,
    cot_ref,
    mixed_ref,
    gnf_ref,
    came_ref,
    scale_ref,
    w_ref,
    q_ref,
    k_ref,
    v_ref,
    att_ref,
    inv_ref,
    uq_ref,
    uk_ref,
    cos_a,
    cos_b,
    sin_a,
    sin_b,
    root_ref,
    gm_ref,
    low_ref,
    g_ref,
    gs_ref,
    gmod_ref,
    gatt_ref,
):
    image, part = pl.program_id(0), pl.program_id(1)
    seq, block = q_ref.shape
    width = gm_ref.shape[1]
    lane = lax.broadcasted_iota(jnp.int32, (seq, 128), 1)
    left = lane < 64

    @pl.when((image == 0) & (part == 0))
    def _():
        gs_ref[...] = jnp.zeros_like(gs_ref)

    @pl.when(part == 0)
    def _():
        mixed, scale = mixed_ref[...], scale_ref[0]
        inverse = lax.rsqrt(jnp.mean(mixed * mixed, axis=-1, keepdims=True) + EPSILON)
        grad = gnf_ref[...] + came_ref[...].astype(jnp.float32)
        unit = mixed * inverse
        gmod_ref[0] = jnp.sum(grad * unit, axis=0, keepdims=True)
        scaled = grad * scale
        mean = jnp.mean(scaled * unit, axis=-1, keepdims=True)
        total = cot_ref[0].astype(jnp.float32) + inverse * (scaled - unit * mean)
        gm_ref[...] = total
        low = total.astype(jnp.bfloat16)
        low_ref[...] = low
        gatt_ref[...] = mm(low, w_ref[...], NT).astype(jnp.bfloat16)

    def own(mask, values):
        return jnp.where(mask, values, jnp.zeros_like(values))

    for pair in range(block // 128):
        at = slice(pair * 128, pair * 128 + 128)
        start = part * block + pair * 128
        to = pl.ds(pl.multiple_of(start, 128), 128)
        queries, keys, values = q_ref[:, at], k_ref[:, at], v_ref[:, at]
        grad = gatt_ref[:, to].astype(jnp.float32) * inv_ref[:, at]
        low = grad.astype(jnp.bfloat16)
        along = grad * att_ref[:, at].astype(jnp.float32)
        grads = [None, None, None]
        for head in range(2):
            mask = left if head == 0 else jnp.logical_not(left)
            delta = -jnp.sum(own(mask, along), axis=-1, keepdims=True)
            high = delta.astype(jnp.bfloat16).astype(jnp.float32)
            spot = 64 if head == 0 else 0
            extra = jnp.where(lane == spot, high, jnp.where(lane == spot + 1, delta - high, 0.0))
            ones = jnp.where((lane == spot) | (lane == spot + 1), 1.0, 0.0).astype(jnp.bfloat16)
            shifted = jnp.where(mask, low, extra.astype(jnp.bfloat16))
            weights = jnp.exp(mm(keys, own(mask, queries), NT))
            grad_scores = (weights * mm(jnp.where(mask, values, ones), shifted, NT)).astype(jnp.bfloat16)
            found = (
                mm(grad_scores, own(mask, keys), TN),
                mm(grad_scores, own(mask, queries)),
                mm(weights.astype(jnp.bfloat16), own(mask, low)),
            )
            grads = [new if old is None else old + new for old, new in zip(grads, found)]
        root = root_ref[:, at]
        cos, sin = by_place((cos_a, cos_b), at), by_place((sin_a, sin_b), at)
        for index, (turned, unit_ref) in enumerate(((queries, uq_ref), (keys, uk_ref))):
            grad_turned = grads[index]
            turned = turned.astype(jnp.float32)
            dots = head_sums(grad_turned * turned) / (root * root)
            gs_ref[:, to] += 0.5 * jnp.sum(dots, axis=0, keepdims=True)
            inner = rotate(grad_turned - turned * dots, cos, -sin)
            spot = pl.ds(pl.multiple_of(index * width + start, 128), 128)
            g_ref[:, spot] = (inner * unit_ref[:, at]).astype(jnp.bfloat16)
        spot = pl.ds(pl.multiple_of(2 * width + start, 128), 128)
        g_ref[:, spot] = grads[2].astype(jnp.bfloat16)


def back(line, bits, cot, mixed, grad_nf, came, scale_ffn, w_out, qkv, attended, inverse, unit, cos, sin, root):
    rows, width = mixed.shape
    images, parts = scale_ffn.shape[0], 2
    seq, block = rows // images, width // parts

    def own(array):
        return (array, (seq, width), lambda i, h, bits: (i, 0))

    def half(array, index):
        return (array, (seq, block), lambda i, h, bits: (i, index * parts + h))

    def result(columns, dtype):
        shape = jax.ShapeDtypeStruct((rows, columns), dtype)
        return (shape, (seq, columns), lambda i, h, bits: (i, 0))

    each = (1, 1, width), lambda i, h, bits: (i, 0, 0)
    return call(
        line,
        back_kernel,
        (images, parts),
        [
            scalars(bits),
            (cot, (1, seq, width), lambda i, h, bits: (0, i, 0)),
            own(mixed),
            own(grad_nf),
            own(came),
            (scale_ffn, *each),
            whole(w_out),
            half(qkv, 0),
            half(qkv, 1),
            half(qkv, 2),
            half(attended, 0),
            half(inverse, 0),
            half(unit, 0),
            half(unit, 1),
            *table_blocks(cos, block, lambda i, h: h),
            *table_blocks(sin, block, lambda i, h: h),
            (root, (1, block), lambda i, h, bits: (0, h)),
        ],
        [
            result(width, jnp.float32),
            result(width, jnp.bfloat16),
            result(3 * width, jnp.bfloat16),
            fresh((1, width)),
            (jax.ShapeDtypeStruct((images, 1, width), jnp.float32), *each),
        ],
        scratch=[pltpu.VMEM((seq, width), jnp.bfloat16)],
        flops=2 * rows * width * width + 10 * rows * seq * width,
        moved=2 * width * width + 48 * rows * width,
        prefetch=True,
    )


def weight_kernel(bits_ref, grad_ref, inputs_ref, low_ref, attended_ref, own_ref, sent_ref):
    step, steps = pl.program_id(0), pl.num_programs(0)
    groups, _, width = own_ref.shape
    wide = (steps - 1) * grad_ref.shape[1] // (2 * groups)

    def store(total, at, start):
        rows = total.shape[0] // (2 * at.size)
        split = total.reshape(at.size, 2, rows, width)
        low, high = split[:, 0], split[:, 1]
        mine = bits_ref[0] == 0
        own_ref[at, start : start + rows, :] = jnp.where(mine, low, high).astype(jnp.bfloat16)
        sent_ref[at, start : start + rows, :] = jnp.where(mine, high, low).astype(jnp.bfloat16)

    @pl.when(step < steps - 1)
    def _():
        count = groups // (steps - 1)
        store(mm(grad_ref[...], inputs_ref[...], TN), pl.ds(step * count, count), 0)

    @pl.when(step == steps - 1)
    def _():
        store(mm(low_ref[...], attended_ref[...], TN), pl.ds(0, groups), wide)


def weight_grads(line, bits, groups, grad, inputs, low, attended):
    rows, width = inputs.shape
    total, block = grad.shape[1], grad.shape[1] // 2
    steps = total // block
    share = (total + low.shape[1]) // (2 * groups)
    return call(
        line,
        weight_kernel,
        (steps + 1,),
        [
            scalars(bits),
            (grad, (rows, block), lambda j: (0, jnp.minimum(j, steps - 1))),
            whole(inputs),
            whole(low),
            whole(attended),
        ],
        [fresh((groups, share, width), jnp.bfloat16)] * 2,
        flops=2 * rows * width * total,
        moved=2 * (rows * total + rows * width + width * total),
    )


def tokens_kernel(g_ref, w_ref, tok_ref, scale_ref, gm_ref, out_ref, gmod_ref, total_ref):
    step, steps = pl.program_id(0), pl.num_programs(0)
    part = mm(g_ref[...], w_ref[...], NT)

    @pl.when(step == 0)
    def _():
        total_ref[...] = part

    @pl.when(step > 0)
    def _():
        total_ref[...] += part

    @pl.when(step == steps - 1)
    def _():
        images = scale_ref.shape[0]
        seq = tok_ref.shape[0] // images
        for image in range(images):
            at = pl.ds(image * seq, seq)
            tok = tok_ref[at, :].astype(jnp.float32)
            inverse = lax.rsqrt(jnp.mean(tok * tok, axis=-1, keepdims=True) + EPSILON)
            unit = tok * inverse
            grad = total_ref[at, :]
            gmod_ref[image] = jnp.sum(grad * unit, axis=0, keepdims=True)
            scaled = grad * scale_ref[image]
            mean = jnp.mean(scaled * unit, axis=-1, keepdims=True)
            out_ref[at, :] = gm_ref[at, :] + inverse * (scaled - unit * mean)


def tokens_backward(line, grad_qkv, w_qkv, tokens, scale_attn, grad_mixed):
    rows, width = tokens.shape
    total, block = w_qkv.shape[1], w_qkv.shape[1] // 2
    images = scale_attn.shape[0]


    return call(
        line,
        tokens_kernel,
        (total // block,),
        [
            (grad_qkv, (rows, block), lambda j: (0, j)),
            (w_qkv, (width, block), lambda j: (0, j)),
            whole(tokens),
            whole(scale_attn),
            whole(grad_mixed),
        ],
        [
            (jax.ShapeDtypeStruct((rows, width), jnp.float32), (rows, width), lambda j: (0, 0)),
            (jax.ShapeDtypeStruct((images, 1, width), jnp.float32), (images, 1, width), lambda j: (0, 0, 0)),
        ],
        scratch=[pltpu.VMEM((rows, width), jnp.float32)],
        flops=2 * rows * width * total,
        moved=2 * (rows * total + width * total) + 10 * rows * width,
    )


def norm_rows(values, gain):
    return values * lax.rsqrt(jnp.mean(values * values, axis=-1, keepdims=True) + EPSILON) * gain


def norm_back(values, gain, grad):
    inverse = lax.rsqrt(jnp.mean(values * values, axis=-1, keepdims=True) + EPSILON)
    unit = values * inverse
    scaled = grad * gain
    mean = jnp.mean(scaled * unit, axis=-1, keepdims=True)
    return inverse * (scaled - unit * mean), jnp.sum(grad * unit, axis=0, keepdims=True)


def gate_parts(gate):
    normal = 0.5 + 0.5 * lax.erf(gate * math.sqrt(0.5))
    density = jnp.exp(-0.5 * gate * gate) * (1.0 / math.sqrt(2.0 * math.pi))
    return gate * normal, normal + gate * density


def halves(value):
    high = value.astype(jnp.bfloat16)
    rest = (value - high.astype(jnp.float32)).astype(jnp.bfloat16)
    return jnp.concatenate([high, rest], axis=0)


def times(rows, weight, dims=NT):
    count = rows.shape[0]
    product = mm(halves(rows), weight, dims)
    return product[:count] + product[count:]


def outer(low_rows, rows):
    return mm(halves(rows), jnp.concatenate([low_rows, low_rows], axis=0), TN)


def first_rows(label, sigma, fourier_ref, table_ref, time_ref, gains_ref):
    level = (LOG_LOW + LOG_SPAN * sigma.astype(jnp.float32) / (NSIG - 1)) / 4.0
    angles = 2.0 * math.pi * level * fourier_ref[...]
    feats = jnp.concatenate([jnp.cos(angles), jnp.sin(angles)], axis=-1).astype(jnp.bfloat16)
    classes = lax.broadcasted_iota(jnp.int32, (label.shape[0], table_ref.shape[0]), 1)
    one_hot = jnp.where(classes == label, 1.0, 0.0).astype(jnp.bfloat16)
    start = mm(feats, time_ref[...]) + mm(one_hot, table_ref[...])
    first = norm_rows(start, gains_ref[0:1].astype(jnp.float32))
    hidden = norm_rows(first, gains_ref[1:2].astype(jnp.float32)).astype(jnp.bfloat16)
    return feats, one_hot, start, first, hidden


def map_kernel(
    label_ref,
    sigma_ref,
    fourier_ref,
    table_ref,
    time_ref,
    gains_ref,
    wa_ref,
    wb_ref,
    wd_ref,
    attn_ref,
    ffn_ref,
    scale_attn_ref,
    scale_ffn_ref,
    start_ref,
    first_ref,
    second_ref,
    up_ref,
    numbers_ref,
    hidden_ref,
):
    step = pl.program_id(0)
    count = scale_attn_ref.shape[0]

    @pl.when(step == 0)
    def _():
        row = lax.broadcasted_iota(jnp.int32, (8, 1), 0)
        label, sigma = jnp.zeros((8, 1), jnp.int32), jnp.zeros((8, 1), jnp.int32)
        for image in range(count):
            label = jnp.where(row == image, label_ref[image], label)
            sigma = jnp.where(row == image, sigma_ref[image], sigma)
        lane = lax.broadcasted_iota(jnp.int32, (8, 128), 1)
        numbers = jnp.where(lane == 0, label, jnp.where(lane == 1, sigma, 0))
        numbers_ref[...] = numbers.astype(jnp.float32)
        _, _, start, first, hidden = first_rows(
            label, sigma, fourier_ref, table_ref, time_ref, gains_ref
        )
        start_ref[...] = start
        first_ref[...] = first
        second_ref[...] = first
        hidden_ref[...] = hidden.astype(jnp.float32)

    hidden = hidden_ref[...].astype(jnp.bfloat16)
    value, gate = mm(hidden, wa_ref[...]), mm(hidden, wb_ref[...])
    up_ref[0] = value
    up_ref[1] = gate
    gated = (value * gate_parts(gate)[0]).astype(jnp.bfloat16)
    second_ref[...] += mm(gated, wd_ref[...])

    @pl.when(step == pl.num_programs(0) - 1)
    def _():
        cond = norm_rows(second_ref[...], gains_ref[2:3].astype(jnp.float32)).astype(jnp.bfloat16)
        for weight, scale_ref in ((attn_ref, scale_attn_ref), (ffn_ref, scale_ffn_ref)):
            scale = 1.0 + mm(cond, weight[...])
            for image in range(count):
                scale_ref[image] = scale[image : image + 1]


def hidden_blocks(w_map_up, w_map_down, block):
    width, steps = w_map_up.shape[0], w_map_down.shape[0] // block
    return [
        (w_map_up, (width, block), lambda j: (0, j)),
        (w_map_up, (width, block), lambda j: (0, steps + j)),
        (w_map_down, (block, width), lambda j: (j, 0)),
    ]


def map_forward(line, labels, sigma, fourier, table, w_time, w_up, w_down, gains, w_attn, w_ffn):
    images, width = labels.shape[0], w_time.shape[1]
    hidden, block, model = w_down.shape[0], 1152, w_attn.shape[1]
    return call(
        line,
        map_kernel,
        (hidden // block,),
        [
            scalars(labels),
            scalars(sigma),
            whole(fourier[None]),
            whole(table),
            whole(w_time),
            whole(gains),
            *hidden_blocks(w_up, w_down, block),
            whole(w_attn),
            whole(w_ffn),
        ],
        [
            fresh((images, 1, model)),
            fresh((images, 1, model)),
            fresh((8, width)),
            fresh((8, width)),
            fresh((8, width)),
            (jax.ShapeDtypeStruct((2, 8, hidden), jnp.float32), (2, 8, block), lambda j: (0, 0, j)),
            fresh((8, 128)),
        ],
        scratch=[pltpu.VMEM((8, width), jnp.float32)],
        flops=16 * width * (3 * hidden + 2 * model),
        moved=2 * width * (3 * hidden + 2 * model + 1256),
    )


def map_back_kernel(
    gattn_ref,
    gffn_ref,
    heads_ref,
    numbers_ref,
    gains_ref,
    start_ref,
    first_ref,
    second_ref,
    up_ref,
    wa_ref,
    wb_ref,
    wd_ref,
    attn_ref,
    ffn_ref,
    sent_ref,
    gsecond_ref,
    gup_ref,
    ghidden_ref,
    gain_ref,
    rows_ref,
):
    step, steps = pl.program_id(0), pl.num_programs(0)
    count = gattn_ref.shape[0]
    block = wd_ref.shape[0]
    gains = gains_ref[...].astype(jnp.float32)

    @pl.when(step == 0)
    def _():
        rows_ref[...] = jnp.zeros_like(rows_ref)
        for image in range(count):
            rows_ref[0, image : image + 1] = gattn_ref[image]
            rows_ref[1, image : image + 1] = gffn_ref[image]
        grad = times(rows_ref[0], attn_ref[...]) + times(rows_ref[1], ffn_ref[...])
        gsecond, gain = norm_back(second_ref[...], gains[2:3], grad)
        gsecond_ref[...] = gsecond
        gain_ref[2:3] = gain
        ghidden_ref[...] = jnp.zeros_like(ghidden_ref)

    grad = times(gsecond_ref[...], wd_ref[...])
    bent, slope = gate_parts(up_ref[1])
    for part, (new, weight) in enumerate(((grad * bent, wa_ref), (grad * up_ref[0] * slope, wb_ref))):
        at = pl.multiple_of(step * block, block)
        gup_ref[part, :, pl.ds(at, block)] = new
        ghidden_ref[...] += times(new, weight[...])

    @pl.when(step == steps - 1)
    def _():
        gfirst, gain = norm_back(first_ref[...], gains[1:2], ghidden_ref[...])
        gain_ref[1:2] = gain
        gsecond = gsecond_ref[...]
        gstart, gain = norm_back(start_ref[...], gains[0:1], gfirst + gsecond)
        gain_ref[0:1] = gain
        model = heads_ref.shape[1]
        lane = lax.broadcasted_iota(jnp.int32, (model, 128), 1)
        row = lax.broadcasted_iota(jnp.int32, (model, 128), 0)
        pick = jnp.where(row == lane * 64, 1.0, 0.0).astype(jnp.bfloat16)
        heads = times(jnp.concatenate([heads_ref[...], jnp.zeros((7, model))], axis=0), pick, NN)
        sent_ref[...] = jnp.zeros_like(sent_ref)
        devices = sent_ref.shape[0]
        hidden = gup_ref.shape[2]
        for device in range(devices):
            spot = 0
            for values in (rows_ref[0], rows_ref[1], gsecond):
                width = values.shape[1] // devices
                sent_ref[device, 0:count, spot : spot + width] = values[
                    0:count, device * width : device * width + width
                ]
                spot += width
            width = 2 * hidden // devices
            part, at = divmod(device * width, hidden)
            sent_ref[device, 0:count, spot : spot + width] = gup_ref[part, 0:count, at : at + width]
            spot += width
            width = gstart.shape[1] // devices
            sent_ref[device, 0:count, spot : spot + width] = gstart[
                0:count, device * width : device * width + width
            ]
            for index in range(3):
                sent_ref[device, count : count + 1, index * width : index * width + width] = gain_ref[
                    index : index + 1, device * width : device * width + width
                ]
            sent_ref[device, count + 1 : 2 * count + 1, 0:128] = numbers_ref[0:count]
            used = model // 64
            sent_ref[device, count : count + 1, 3 * width : 3 * width + used] = heads[0:1, 0:used]


def map_backward(line, grad_attn, grad_ffn, heads, saved, gains, w_up, w_down, w_attn, w_ffn, devices):
    start, first, second, up, numbers = saved
    width, hidden, block = start.shape[1], w_down.shape[0], 1152
    model = w_attn.shape[1]
    columns = -(-(2 * model + 2 * width + 2 * hidden) // devices // 128) * 128
    return call(
        line,
        map_back_kernel,
        (hidden // block,),
        [
            whole(grad_attn),
            whole(grad_ffn),
            whole(heads),
            whole(numbers),
            whole(gains),
            whole(start),
            whole(first),
            whole(second),
            (up, (2, 8, block), lambda j: (0, 0, j)),
            *hidden_blocks(w_up, w_down, block),
            whole(w_attn),
            whole(w_ffn),
        ],
        [fresh((devices, 8, columns))],
        scratch=[
            pltpu.VMEM((8, width), jnp.float32),
            pltpu.VMEM((2, 8, hidden), jnp.float32),
            pltpu.VMEM((8, width), jnp.float32),
            pltpu.VMEM((8, width), jnp.float32),
            pltpu.VMEM((2, 8, model), jnp.float32),
        ],
        flops=32 * width * (3 * hidden + 2 * model),
        moved=2 * width * (3 * hidden + 2 * model),
    )[0]


def map_weights_kernel(
    columns_ref,
    fourier_ref,
    table_ref,
    time_ref,
    gains_ref,
    wa_ref,
    wb_ref,
    wd_ref,
    class_ref,
    wtime_ref,
    wup_ref,
    wdown_ref,
    wgain_ref,
    wattn_ref,
    wffn_ref,
    heads_ref,
    hidden_ref,
    second_ref,
    number_rows,
    rows_ref,
):
    step = pl.program_id(0)
    devices, count = columns_ref.shape[0], rows_ref.shape[0] // columns_ref.shape[0]
    attn, ffn, second, up, start = (
        wattn_ref.shape[0],
        wffn_ref.shape[0],
        wdown_ref.shape[0],
        wup_ref.shape[0],
        class_ref.shape[0],
    )
    edges = [0]
    for width in (attn, ffn, second, up, start):
        edges.append(edges[-1] + width)

    def columns(index):
        return rows_ref[:, edges[index] : edges[index + 1]]

    @pl.when(step == 0)
    def _():
        extra = jnp.zeros((1, columns_ref.shape[2]), jnp.float32)
        for device in range(devices):
            at = slice(device * count, device * count + count)
            number_rows[at] = columns_ref[device, count + 1 : 2 * count + 1, 0:128]
            rows_ref[at] = columns_ref[device, 0:count]
            extra += columns_ref[device, count : count + 1]
        for index in range(3):
            wgain_ref[index : index + 1] = extra[:, index * start : index * start + start]
        heads_ref[...] = extra[:, 3 * start : 3 * start + heads_ref.shape[1]]
        numbers = number_rows[...].astype(jnp.int32)
        feats, one_hot, _, first, hidden = first_rows(
            numbers[:, 0:1], numbers[:, 1:2], fourier_ref, table_ref, time_ref, gains_ref
        )
        hidden_ref[...] = hidden
        second_ref[...] = first
        class_ref[...] = outer(one_hot, columns(4))
        wtime_ref[...] = outer(feats, columns(4))
        wup_ref[...] = outer(hidden, columns(3))

    hidden = hidden_ref[...]
    value, gate = mm(hidden, wa_ref[...]), mm(hidden, wb_ref[...])
    gated = (value * gate_parts(gate)[0]).astype(jnp.bfloat16)
    second_ref[...] += mm(gated, wd_ref[...])
    wdown_ref[...] = outer(gated, columns(2))

    @pl.when(step == pl.num_programs(0) - 1)
    def _():
        cond = norm_rows(second_ref[...], gains_ref[2:3].astype(jnp.float32)).astype(jnp.bfloat16)
        wattn_ref[...] = outer(cond, columns(0))
        wffn_ref[...] = outer(cond, columns(1))


def map_weights(line, columns, count, fourier, table, w_time, w_up, w_down, gains, model):
    devices = columns.shape[0]
    rows = devices * count
    width, hidden, block = w_time.shape[1], w_down.shape[0], 1152
    own = width // devices
    return call(
        line,
        map_weights_kernel,
        (hidden // block,),
        [
            whole(columns),
            whole(fourier[None]),
            whole(table),
            whole(w_time),
            whole(gains),
            *hidden_blocks(w_up, w_down, block),
        ],
        [
            fresh((own, table.shape[0])),
            fresh((own, w_time.shape[0])),
            fresh((2 * hidden // devices, width)),
            (jax.ShapeDtypeStruct((own, hidden), jnp.float32), (own, block), lambda j: (0, j)),
            fresh((3, own)),
            fresh((model // devices, width)),
            fresh((model // devices, width)),
            fresh((1, model // 64)),
        ],
        scratch=[
            pltpu.VMEM((rows, width), jnp.bfloat16),
            pltpu.VMEM((rows, width), jnp.float32),
            pltpu.VMEM((rows, 128), jnp.float32),
            pltpu.VMEM((rows, columns.shape[2]), jnp.float32),
        ],
        flops=2 * rows * width * 4 * hidden,
        moved=2 * width * (3 * hidden + 1256) + 4 * width * 400,
    )


class Sum:
    def __init__(self, terms, columns, pair=None):
        self.lists = [terms] if pair is None else [pair[0].lists[0], pair[1].lists[0]]
        self.more = []
        self.level = None
        self.done = [] if pair is None else [*{*pair[0].done, *pair[1].done}]
        self.columns = columns
        self.lone = None if pair is None else pair[0].lone
        self.stacked = False

    def last(self):
        return self.lists[0][-1][0]

    def together(self):
        self.stacked = True
        return self

    def apart(self):
        self.stacked = False
        return self

    def dims(self):
        return self.lists[0][0][1]

    def left(self):
        return [name for name in self.dims() if name not in self.done]


def columns_of(part, start, count):
    return Sum([(array, dims, start) for array, dims, _ in part.lists[0]], count)


def split(own, sent, level, names, lone=None):
    came = trade(sent, level, lone)
    rows = own.size // own.shape[-1] // 2 ** len(names)
    shape = (*([2] * len(names)), rows, own.shape[-1])
    return Sum([(array.reshape(shape), names, 0) for array in (own, came)], own.shape[-1])


def lone_sum(sent, bit, names):
    came = trade(sent, bit, bit, True)
    rows = sent.size // sent.shape[-1] // 2 ** len(names)
    shape = (*([2] * len(names)), rows, sent.shape[-1])
    found = Sum([(array.reshape(shape), names, 0) for array in (sent, came)], sent.shape[-1])
    found.lone = bit
    return found


def joined(pair):
    return Sum(None, pair[0].columns, pair)


def combine(line, bits, jobs, steps):
    ins, outs, plan = [scalars(bits)], [], []

    def place(dims, fixed, column, width, block):
        def where(step, bits):
            spots = []
            for name in dims:
                if isinstance(name, tuple):
                    spots.append(name[1])
                elif name not in fixed:
                    spots.append(0)
                else:
                    spot = 0 if name == "core" else 1 + name
                    spots.append(bits[spot] if fixed[name] else 1 - bits[spot])
            return (*spots, 0, column // block + step)

        return where

    for part, level in jobs:
        block = part.columns // steps
        fixed = {name: True for name in part.done}
        pick = part.level
        whole_sum = isinstance(level, tuple)
        if level is not None and pick != level and not whole_sum:
            fixed[level] = False
        groups = []
        for terms in [*part.lists, part.more]:
            group = []
            for array, dims, column in terms:
                rows = array.shape[-2]
                shape = (
                    *[1 if name in fixed or isinstance(name, tuple) else 2 for name in dims],
                    rows,
                    block,
                )
                group.append(len(ins) - 1)
                ins.append((array, shape, place(dims, fixed, column, part.columns, block)))
            groups.append(group)
        dims = [name for name in part.dims() if name not in fixed]
        shape = (*[2 for _ in dims], rows, part.columns)
        if part.stacked:
            dims, shape = [("at", 0), *dims], (2, *shape)
        dtype = jnp.bfloat16 if level is not None else jnp.float32
        outs.append(
            (jax.ShapeDtypeStruct(shape, dtype), (*shape[:-1], block), place(dims, {}, 0, 0, block))
        )
        plan.append((groups, pick, pick is not None and pick == level, part.stacked))

    def combine_kernel(bits_ref, *refs):
        results = refs[len(ins) - 1 :]
        for (groups, pick, swap, both), result in zip(plan, results):

            def total(group):
                found = None
                for index in group:
                    value = refs[index][...].reshape(shape).astype(jnp.float32)
                    found = value if found is None else found + value
                return found

            shape = result.shape[1:] if both else result.shape
            if both:
                for index in range(2):
                    result[index] = total(groups[index]).astype(result.dtype)
                continue
            found = total(groups[0])
            if pick is not None:
                first = bits_ref[1 + pick] == (1 if swap else 0)
                found = jnp.where(first, found, total(groups[1]))
            if groups[-1]:
                found = found + total(groups[-1])
            result[...] = found.astype(result.dtype)

    moved = sum(array.size for array, _, _ in ins)
    return call(line, combine_kernel, (steps,), ins, outs, moved=moved, prefetch=True)


def finish(line, bits, near, up, down, first, second, across, came):
    ins, groups = [scalars(bits)], []

    def add(terms, done, block, moving):
        group = []
        for array, dims, column in terms:
            group.append(len(ins) - 1)
            shape = (*[1] * len(dims), array.shape[-2], block)

            def where(step, bits, dims=dims, column=column):
                spots = []
                for name in dims:
                    if isinstance(name, tuple):
                        spots.append(name[1])
                    else:
                        spots.append(bits[0] if name == "core" else bits[1 + name])
                return (*spots, 0, column // block + (step if moving else 0))

            ins.append((array, shape, where))
        groups.append(group)

    half = up.columns // 2
    add(up.lists[0], up.done, half, True)
    add(up.lists[1], up.done, half, True)
    add(up.more, up.done, half, True)
    add([(came[0], (), 0)], (), half, True)
    add(down.lists[0], down.done, down.columns, False)
    add(down.lists[1], down.done, down.columns, False)
    add([(came[1], (("at", 0),), 0)], (), down.columns, False)
    add([(came[1], (("at", 1),), 0)], (), down.columns, False)
    add(first.lists[0], first.done, first.columns, False)
    add(second.lists[0], second.done, second.columns, False)
    count = len(ins) - 1
    pick = up.level

    def finish_kernel(bits_ref, *refs):
        up_ref, down_ref, wide_ref, out_ref = refs[count:]
        step = pl.program_id(0)

        def total(index):
            found = None
            for spot in groups[index]:
                value = refs[spot][...]
                value = value.reshape(value.shape[-2:]).astype(jnp.float32)
                found = value if found is None else found + value
            return found

        held = jnp.where(bits_ref[1 + pick] == 0, total(0), total(1)) + total(2)
        up_ref[...] = jnp.where(bits_ref[1 + near] == bits_ref[0], held, total(3))
        mine = jnp.concatenate([total(4), total(5)], axis=1)
        theirs = jnp.concatenate([total(6), total(7)], axis=1)
        down_ref[...] = jnp.where(step == bits_ref[0], mine, theirs)
        both = jnp.where(step == 0, total(8), total(9))
        wide_ref[...] = both[:across]
        out_ref[...] = both[across:]

    def share(rows, width):
        return (
            jax.ShapeDtypeStruct((rows, width), jnp.float32),
            (rows, width // 2),
            lambda step, bits: (0, step),
        )

    return call(
        line,
        finish_kernel,
        (2,),
        ins,
        [
            share(up.lists[0][0][0].shape[-2], up.columns),
            share(down.lists[0][0][0].shape[-2], 4 * down.columns),
            share(across, 2 * first.columns),
            share(first.lists[0][0][0].shape[-2] - across, 2 * first.columns),
        ],
        prefetch=True,
    )


def trade(sent, name, lone=None, first=False):
    if name == "core":
        return lax.ppermute(sent, "space", [(0, 1), (1, 0)])
    count = lax.axis_size("dp")
    if lone is None:
        return lax.ppermute(sent, "dp", [(i, i ^ (1 << name)) for i in range(count)])
    pairs = [
        (2 * i + core, 2 * (i ^ (1 << name)) + core)
        for i in range(count)
        for core in range(2)
        if (core == (i >> lone) & 1) != first
    ]
    return lax.ppermute(sent, BOTH, pairs)


def advance(line, bits, jobs, steps=2):
    for part, level in jobs:
        if len(part.lists) == 2 and part.level is None and not part.stacked:
            part.level = level
    sent = combine(line, bits, jobs, steps)
    for (part, level), value in zip(jobs, sent):
        if isinstance(level, tuple):
            part.lone = level[0]
            came = trade(value, level[0], level[0], True)
        else:
            came = trade(value, level, part.lone)
        arrived(part, level, came)


def arrived(part, level, came):
    dims = [name for name in part.left() if name != level]
    if not isinstance(level, tuple) and part.level != level:
        part.done.append(level)
    if part.stacked:
        for index in range(2):
            part.lists[index].append((came, [("at", index), *dims], 0))
    elif part.level is not None:
        part.more.append((came, dims, 0))
    else:
        part.lists[0].append((came, dims, 0))


def shards(
    tokens,
    cotangent,
    labels,
    sigma_index,
    fourier,
    class_table,
    w_time,
    w_map_up,
    w_map_down,
    map_gains,
    w_ada_attn,
    w_ada_ffn,
    w_qkv,
    head_scale,
    w_out,
    w_up,
    w_down,
):
    all_images, local_len, model_width = tokens.shape
    num_images = all_images // 2
    num_heads = head_scale.shape[0]
    head_dim = model_width // num_heads
    seq_len = 2 * local_len
    devices = lax.axis_size("dp") * lax.axis_size("space")
    core = lax.axis_index("space")

    def swap(value):
        return lax.ppermute(value, "space", [(0, 1), (1, 0)])

    def other_half(value):
        return swap(lax.dynamic_slice_in_dim(value, (1 - core) * num_images, num_images, axis=0))

    def tokens_half(value):
        return value.reshape(num_images, seq_len, -1)[:, local_len:]

    def split_images(value, came):
        kept = value.reshape(num_images, seq_len, -1)[:, :local_len]
        return jnp.where(
            core == 0,
            jnp.concatenate([kept, came], axis=0),
            jnp.concatenate([came, kept], axis=0),
        )

    levels = lax.axis_size("dp").bit_length() - 1
    dp = lax.axis_index("dp")
    bits = jnp.stack([core, *[(dp >> level) & 1 for level in range(levels)]]).astype(jnp.int32)
    every = [*reversed(range(levels))]
    low = list(range(levels - 2))
    swapped = [*reversed(low[:2]), *low[2:]]
    near, far = levels - 2, levels - 1

    cos, sin = [jnp.asarray(table) for table in rope_tables(seq_len, num_heads, head_dim, GRID)]
    root = jnp.repeat(jnp.sqrt(head_scale.astype(jnp.float32)), head_dim)[None]
    all_cotangent = swap(cotangent)
    line = []
    scale_attn, scale_ffn, *map_saved = map_forward(
        line,
        labels,
        sigma_index,
        fourier,
        class_table,
        w_time,
        w_map_up,
        w_map_down,
        map_gains,
        w_ada_attn,
        w_ada_ffn,
    )
    normed, qkv, unit, tokens = project_qkv(
        line, bits, tokens, other_half(tokens), scale_attn, w_qkv, cos, sin, root
    )
    attended, inverse, mixed, normed_ffn, cotangent = attend(
        line, bits, qkv, tokens, scale_ffn, w_out, cotangent, all_cotangent
    )
    other_ffn = swap(normed_ffn)
    piece = low[-1]
    share = w_up.shape[1] // devices
    up_rest = [far, *reversed(low[1:-1]), "core"]
    down_all = [*every, "core"]

    up_all = [far, *reversed(low[:-1]), "core"]

    def down_sum(down):
        rows = down.shape[0] // 2 ** len(down_all)
        down = down.reshape(*([2] * len(down_all)), rows, down.shape[1])
        return Sum([(down, down_all, 0)], down.shape[-1])

    own, sent, down0, y_part, g_part = ffn(
        line, bits, 0, share, normed_ffn, other_ffn, cotangent, w_up, w_down
    )
    up0 = split(own, sent, low[0], up_rest)
    sent, down1, y_own, y_sent, g_own, g_sent = ffn(
        line,
        bits,
        1,
        share,
        normed_ffn,
        other_ffn,
        cotangent,
        w_up,
        w_down,
        (mixed, y_part, g_part),
    )
    g_came = swap(g_sent)
    up1 = lone_sum(sent, near, up_all)
    mid = low[1:-1]
    down = joined((down_sum(down0), down_sum(down1))).together()
    first_model = model_width // 2

    def then(*arrays):
        line.extend(arrays)

    def later(array):
        return lax.optimization_barrier((array, *line))[0]

    def step(*jobs):
        advance(line, bits, jobs)

    y_came = swap(y_sent)
    step((down, piece))
    then(up0.last())
    grad_mixed, grad_low, grad_qkv, grad_scale, grad_mod_ffn = back(
        line,
        bits,
        cotangent,
        mixed,
        g_own,
        g_came,
        scale_ffn,
        w_out,
        qkv,
        attended,
        inverse,
        unit,
        cos,
        sin,
        root,
    )
    groups = devices // 2
    own, sent = weight_grads(line, bits, groups, grad_qkv, normed, grad_low, attended)
    shape = (*([2] * levels), *own.shape[1:])
    terms = [(array.reshape(shape), every) for array in (own, swap(sent))]
    first, second = [
        Sum([(array, dims, start) for array, dims in terms], first_model)
        for start in (0, first_model)
    ]
    then(down.last())
    step((up0, (near,)), (up1, low[0]))
    for level in mid:
        step((up0, level), (up1, level), (down, level))
    up = joined((up0, up1))
    then(y_came)
    grad_tokens, grad_mod_attn = tokens_backward(
        line, grad_qkv, w_qkv, tokens, scale_attn, grad_mixed
    )
    tokens_came = swap(tokens_half(grad_tokens))
    step((first, piece), (second, near))
    then(tokens_came)
    step((up, piece), (down, low[0]))
    columns = lax.all_to_all(
        map_backward(
            line,
            grad_mod_attn,
            grad_mod_ffn,
            grad_scale,
            map_saved,
            map_gains,
            w_map_up,
            w_map_down,
            w_ada_attn,
            w_ada_ffn,
            devices,
        ),
        BOTH,
        0,
        0,
        tiled=True,
    )
    for level in mid:
        step((first, level), (second, level))
    step((first, near), (second, low[0]), (up, far), (down, near))
    (
        sum_class,
        sum_time,
        sum_map_up,
        sum_map_down,
        sum_gains,
        sum_ada_attn,
        sum_ada_ffn,
        sum_heads,
    ) = map_weights(
        line,
        columns,
        labels.shape[0],
        fourier,
        class_table,
        w_time,
        w_map_up,
        w_map_down,
        map_gains,
        model_width,
    )
    out_tokens = (later(y_own) + y_came.astype(jnp.float32)).astype(jnp.bfloat16)
    out_came = swap(tokens_half(out_tokens))
    out_tokens = split_images(out_tokens, out_came)
    step((first, low[0]), (second, piece), (down, far))
    grad_tokens = split_images(later(grad_tokens), tokens_came)
    *sent, up_sent, down_sent = combine(
        line, bits, [(first, far), (second, far), (up, "core"), (down, "core")], 2
    )
    for part, value in zip((first, second), sent):
        arrived(part, far, trade(value, far))
    came = [swap(up_sent), swap(down_sent)]
    up.done.append("core")
    down.done.append("core")
    sum_up, sum_down, sum_qkv, sum_out = [
        total.T for total in finish(
            line, bits, near, up, down, first, second, 3 * model_width // devices, came
        )
    ]
    return (
        out_tokens,
        grad_tokens,
        sum_class.T,
        sum_time.T,
        sum_map_up.T,
        sum_map_down.T,
        sum_gains,
        sum_ada_attn.T,
        sum_ada_ffn.T,
        sum_qkv,
        sum_heads[0],
        sum_out,
        sum_up,
        sum_down,
    )


def solution(mesh):
    placed = (
        P("dp", "space", None),
        P("dp", "space", None),
        P(("dp", "space")),
        P(("dp", "space")),
        P(),
        P(),
        P(),
        P(),
        P(),
        P(),
        P(),
        P(),
        P(),
        P(),
        P(),
        P(),
        P(),
    )
    return jax.shard_map(
        shards,
        mesh=mesh,
        in_specs=placed,
        out_specs=(
            P("dp", "space", None),
            P("dp", "space", None),
            P(None, ("dp", "space")),
            P(None, ("dp", "space")),
            P(None, ("dp", "space")),
            P(None, ("dp", "space")),
            P(None, ("dp", "space")),
            P(None, ("dp", "space")),
            P(None, ("dp", "space")),
            P(None, ("dp", "space")),
            P(),
            P(None, ("dp", "space")),
            P(None, ("dp", "space")),
            P(None, ("dp", "space")),
        ),
        check_vma=False,
    )
```
